256 devices in a mesh: dsp: 8 (over z_lo, x), dp: 32 (over z_hi, y, core).
Axes of the slice: x: 4, y: 4, z: 8 (z_hi: 4, z_lo: 2; z = z_hi * 2 + z_lo), core: 2. Of those that a mesh axis runs over, the one named last changes fastest.
Arguments:
- latents: bfloat16 [32, 8, 128, 1152], P('dp', 'dsp'), may hold values from -16 to 16
- out_grad: bfloat16 [32, 8, 128, 1152], P('dp', 'dsp'), may hold values from -6 to 6
- w_qkv_space: bfloat16 [1152, 1728], replicated, may hold values from -4 to 4
- w_out_space: bfloat16 [1152, 576], replicated, may hold values from -0.25 to 0.25
- w_qkv_time: bfloat16 [1152, 1728], replicated, may hold values from -4 to 4
- w_out_time: bfloat16 [1152, 576], replicated, may hold values from -0.25 to 0.25
Outputs:
- in_grad: bfloat16 [32, 8, 128, 1152], P('dp', 'dsp')
- g_qkv_space: float32 [1152, 1728], P('dp')
- g_out_space: float32 [1152, 576], P('dp')
- g_qkv_time: float32 [1152, 1728], P('dp')
- g_out_time: float32 [1152, 576], P('dp')
The draws below stay inside these ranges and needn't reach their ends.
All inputs are finite; a program needn't handle non-finite values.
Results may differ from the reference program's by a relative error of at most 0.035.
The reference program's roundings to bfloat16 on the way count: a program that leaves them out, or rounds other values in their place, can miss the bound.
Values may be sent and summed in bfloat16 or wider, within the bound.
No kernel may reach another device: no remote copies, remote signals or barrier semaphores. Data moves between devices by JAX's collectives and lax.ppermute only.
A program may use at most 128 MiB of HBM per device.

```python
import jax
import jax.numpy as jnp
from jax import lax

D = 1152
HEADS = 8
HDIM = 72
S = 128
HD = 576
F = 8
CLIPS = 32
N_DSP = 8


def qkv_weights(key):
    keys = jax.random.split(key, 2)
    inner = HEADS * HDIM
    whole = jnp.clip(jax.random.normal(keys[1], (D, 3 * inner), jnp.float32), -4.0, 4.0)
    return whole * D ** (-0.5)


def draw_w_qkv_space(key, part):
    key = jax.random.fold_in(key, 3)
    return qkv_weights(key).astype(jnp.bfloat16)


def draw_w_qkv_time(key, part):
    key = jax.random.fold_in(key, 7)
    return qkv_weights(key).astype(jnp.bfloat16)


def draw_latents(key, part):
    key = jax.random.fold_in(key, 11)
    keys = jax.random.split(key, 2)
    order = jax.random.permutation(keys[0], CLIPS)
    column = jnp.arange(D) // (D // CLIPS)
    boost = jnp.where(order[:, None] == column[None, :], 4.0, 1.0)
    values = jnp.clip(jax.random.normal(keys[1], (CLIPS, F, S, D), jnp.float32), -4.0, 4.0)
    return (values * boost[:, None, None, :]).astype(jnp.bfloat16)


def raised(values, key, source, target, parts, factor):
    owner, partner = [(jnp.arange(values.shape[position]) // (values.shape[position] // parts)).reshape([-1 if axis == position else 1 for axis in range(values.ndim)]) for position in (source, target)]
    chosen = jax.random.permutation(key, parts)[partner]
    strong = (owner == chosen) | (owner == (partner + parts // 2) % parts)
    return jnp.where(strong, factor * values, values)


def shard_levels(own_key, shape, cuts, least, top_value):
    factor_of, own = 1.0, jax.random.fold_in(own_key, 6)
    for axis_at, parts in cuts:
        steps = jnp.exp(jax.random.uniform(jax.random.fold_in(own, axis_at), (parts,), jnp.float32, least / len(cuts), top_value / len(cuts)))
        factor_of = factor_of * jnp.repeat(steps, shape[axis_at] // parts).reshape([-1 if axis == axis_at else 1 for axis in range(len(shape))])
    return factor_of


def normal_values(key, dims, scale, most, shards=(), dtype=jnp.bfloat16):
    gain = shard_levels(key, dims, shards, -0.22, 0.18) if shards else 1.0
    drawn = jax.random.normal(key, dims, jnp.float32) * scale * gain
    return jnp.minimum(jnp.maximum(drawn, -most), most).astype(dtype)


def gaussian_with(own_key, extent, scale, reach, cuts, heavy, dtype=jnp.bfloat16):
    result = scale * jax.random.normal(own_key, extent, jnp.float32)
    if cuts:
        result = result * shard_levels(own_key, extent, cuts, -0.22, 0.18)
    return jnp.clip(raised(result, jax.random.fold_in(own_key, 3), *heavy), -reach, reach).astype(dtype)


def setup_inputs(seed: int = 0) -> dict:
    seeds = jax.random.split(jax.random.key(seed), 7)
    return {
        "latents": draw_latents(jax.random.fold_in(seeds[6], 71), 0),
        "out_grad": gaussian_with(seeds[1], (CLIPS, F, S, D), 1.0, 6.0, ((0, 32), (1, 8)), (0, 3, 32, 2.75)),
        "w_qkv_space": draw_w_qkv_space(jax.random.fold_in(seeds[6], 71), 0),
        "w_out_space": normal_values(seeds[3], (D, HD), HD ** -0.5, 0.25),
        "w_qkv_time": draw_w_qkv_time(jax.random.fold_in(seeds[6], 71), 0),
        "w_out_time": normal_values(seeds[5], (D, HD), HD ** -0.5, 0.25),
    }


epsilon = 1e-06

def einsum_form(text, length_first):
    if length_first:
        return text.replace('gl', 'lg').replace('gm', 'mg')
    return text

def norm_rows(stream):
    values = stream.astype(jnp.float32)
    centred = values - lax.optimization_barrier(jnp.mean(values, axis=-1, keepdims=True))
    inverse = lax.rsqrt(lax.optimization_barrier(jnp.mean(centred * centred, axis=-1, keepdims=True)) + epsilon)
    return (centred * inverse, inverse)

def split_heads(packed, outer, middle, inner, head_count):
    head_size = inner // head_count
    query_part = packed[:, :inner].reshape(outer, middle, head_count, head_size)
    key_part = packed[:, inner:2 * inner].reshape(outer, middle, head_count, head_size)
    value_part = packed[:, 2 * inner:].reshape(outer, middle, head_count, head_size)
    return (query_part, key_part, value_part)

def block_forward(stream, w_qkv, w_out, head_count, length_first):
    outer, middle, width = stream.shape
    inner = w_out.shape[1]
    scale_factor = (inner // head_count) ** (-0.5)
    normed, inverse = norm_rows(stream)
    hidden = normed.astype(jnp.bfloat16)
    packed = jnp.dot(hidden.reshape(outer * middle, width), w_qkv, preferred_element_type=jnp.float32).astype(jnp.bfloat16)
    query_part, key_part, value_part = split_heads(packed, outer, middle, inner, head_count)
    scores = jnp.einsum(einsum_form('glhe,gmhe->ghlm', length_first), query_part.astype(jnp.float32), key_part.astype(jnp.float32)) * scale_factor
    row_max = lax.optimization_barrier(jnp.max(scores, axis=-1, keepdims=True))
    weights = jnp.exp(scores - row_max)
    probs = weights / lax.optimization_barrier(jnp.sum(weights, axis=-1, keepdims=True))
    probs_low = probs.astype(jnp.bfloat16)
    attended = jnp.einsum(einsum_form('ghlm,gmhe->glhe', length_first), probs_low.astype(jnp.float32), value_part.astype(jnp.float32))
    attended = attended.astype(jnp.bfloat16).reshape(outer * middle, inner)
    return (attended, (normed, inverse, hidden, packed, probs, probs_low))

def residual_out(stream, attended, w_out):
    added = jnp.dot(attended, w_out.T, preferred_element_type=jnp.float32)
    return stream.astype(jnp.float32) + added.reshape(stream.shape)

def block_backward(upstream, saved, w_qkv, w_out, head_count, length_first):
    outer, middle, width = upstream.shape
    normed, inverse, hidden, packed, probs, probs_low = saved
    inner = w_out.shape[1]
    head_size = inner // head_count
    scale_factor = head_size ** (-0.5)
    flat_up = upstream.reshape(outer * middle, width)
    grad_att = jnp.dot(flat_up, w_out, preferred_element_type=jnp.float32).astype(jnp.bfloat16)
    grad_att = grad_att.reshape(outer, middle, head_count, head_size).astype(jnp.float32)
    query_part, key_part, value_part = split_heads(packed, outer, middle, inner, head_count)
    grad_probs = jnp.einsum(einsum_form('glhe,gmhe->ghlm', length_first), grad_att, value_part.astype(jnp.float32))
    grad_value = jnp.einsum(einsum_form('ghlm,glhe->gmhe', length_first), probs_low.astype(jnp.float32), grad_att).astype(jnp.bfloat16)
    grad_scores = (probs * (grad_probs - lax.optimization_barrier(jnp.sum(probs * grad_probs, axis=-1, keepdims=True))) * scale_factor).astype(jnp.bfloat16)
    grad_query = jnp.einsum(einsum_form('ghlm,gmhe->glhe', length_first), grad_scores.astype(jnp.float32), key_part.astype(jnp.float32)).astype(jnp.bfloat16)
    grad_key = jnp.einsum(einsum_form('ghlm,glhe->gmhe', length_first), grad_scores.astype(jnp.float32), query_part.astype(jnp.float32)).astype(jnp.bfloat16)
    packed_grad = jnp.concatenate([grad_query.reshape(outer * middle, inner), grad_key.reshape(outer * middle, inner), grad_value.reshape(outer * middle, inner)], axis=1)
    grad_hidden = jnp.dot(packed_grad, w_qkv.T, preferred_element_type=jnp.float32).reshape(outer, middle, width)
    mean_grad = lax.optimization_barrier(jnp.mean(grad_hidden, axis=-1, keepdims=True))
    mean_cross = lax.optimization_barrier(jnp.mean(grad_hidden * normed, axis=-1, keepdims=True))
    grad_in = upstream.astype(jnp.float32) + inverse * (grad_hidden - mean_grad - normed * mean_cross)
    return (grad_in, packed_grad)

def group_sum(left, right, groups, axis):
    outer, middle = (left.shape[0], left.shape[1])
    right = right.reshape(outer, middle, right.shape[-1])
    if axis == 0:
        left_group = left.reshape(groups, outer // groups * middle, left.shape[2])
        right_group = right.reshape(groups, outer // groups * middle, right.shape[2])
    else:
        left_group = jnp.swapaxes(left.reshape(outer, groups, middle // groups, left.shape[2]), 0, 1).reshape(groups, -1, left.shape[2])
        right_group = jnp.swapaxes(right.reshape(outer, groups, middle // groups, right.shape[2]), 0, 1).reshape(groups, -1, right.shape[2])
    pieces = jnp.einsum('rnx,rny->rxy', left_group.astype(jnp.float32), right_group.astype(jnp.float32)).astype(jnp.bfloat16)
    return lax.optimization_barrier(jnp.sum(pieces.astype(jnp.float32), axis=0))

def reference(latents, out_grad, w_qkv_space, w_out_space, w_qkv_time, w_out_time):

    def clip_step(totals, clip_pair):
        clip_input, clip_grad = clip_pair
        attended_s, saved_s = block_forward(clip_input, w_qkv_space, w_out_space, HEADS, False)
        spatial_out = residual_out(clip_input, attended_s, w_out_space).astype(jnp.bfloat16)
        attended_t, saved_t = block_forward(spatial_out, w_qkv_time, w_out_time, HEADS, True)
        grad_mid, packed_t = block_backward(clip_grad, saved_t, w_qkv_time, w_out_time, HEADS, True)
        grad_mid = grad_mid.astype(jnp.bfloat16)
        grad_in, packed_s = block_backward(grad_mid, saved_s, w_qkv_space, w_out_space, HEADS, False)
        pieces = (group_sum(saved_s[2], packed_s, N_DSP, 0), group_sum(grad_mid, attended_s, N_DSP, 0), group_sum(saved_t[2], packed_t, N_DSP, 1), group_sum(clip_grad, attended_t, N_DSP, 1))
        totals = tuple((total + piece for total, piece in zip(totals, pieces)))
        return (totals, grad_in.astype(jnp.bfloat16))
    inner = HEADS * HDIM
    start = (jnp.zeros((D, 3 * inner), jnp.float32), jnp.zeros((D, inner), jnp.float32), jnp.zeros((D, 3 * inner), jnp.float32), jnp.zeros((D, inner), jnp.float32))
    totals, grads_in = lax.scan(clip_step, start, (latents, out_grad))
    return (grads_in, totals[0], totals[1], totals[2], totals[3])
```

```python
import jax
import jax.numpy as jnp
from jax import lax
from jax.experimental import pallas as pl
from jax.experimental.pallas import tpu as pltpu
from jax.sharding import Mesh, PartitionSpec as P

D = 1152
HEADS = 8
HDIM = 72
HD = 576
S = 128
POS = 16
ROWS = 36
HALF = 18
PIECE = 384
SCALE = HDIM ** (-0.5)
EPS = 1e-06
BF = jnp.bfloat16
F32 = jnp.float32
MIB = 1024 * 1024

NN = (((1,), (0,)), ((), ()))
NT = (((1,), (1,)), ((), ()))
TN = (((0,), (0,)), ((), ()))


def dot(a, b, dims=NN):
    return lax.dot_general(a, b, dims, preferred_element_type=F32)


def norm_rows(u):
    centred = u - jnp.mean(u, axis=-1, keepdims=True)
    inverse = lax.rsqrt(jnp.mean(centred * centred, axis=-1, keepdims=True) + EPS)
    return centred * inverse, inverse


def norm_grad(c, g, normed, inverse):
    mean_g = jnp.mean(g, axis=-1, keepdims=True)
    mean_x = jnp.mean(g * normed, axis=-1, keepdims=True)
    return c + inverse * (g - mean_g - normed * mean_x)


def rounded(x):
    return x.astype(BF).astype(F32)


def call(kernel, outs, args, scratch=(), flops=0, limit=24, hbm=()):
    vmem = pl.BlockSpec(memory_space=pltpu.VMEM)
    away = pl.BlockSpec(memory_space=pltpu.HBM)
    moved = 2 * sum(x.size * x.dtype.itemsize for x in args)
    return pl.pallas_call(
        kernel,
        out_shape=[jax.ShapeDtypeStruct(s, t) for s, t in outs],
        in_specs=[away if i in hbm else vmem for i in range(len(args))],
        out_specs=[vmem] * len(outs),
        scratch_shapes=[pltpu.VMEM(s, t) for s, t in scratch]
        + ([pltpu.SemaphoreType.DMA((6,))] if hbm else []),
        compiler_params=pltpu.CompilerParams(vmem_limit_bytes=limit * MIB),
        cost_estimate=pl.CostEstimate(flops=flops, bytes_accessed=moved, transcendentals=0),
    )(*args)


def head(ref, part, h):
    r = part * HD + h * HDIM
    return ref[r : r + HDIM].astype(BF)


def probabilities(pt, h, mask):
    s = dot(head(pt, 1, h), head(pt, 0, h), TN) * SCALE
    if mask is not None:
        s = jnp.where(mask, s, -1e30)
    e = jnp.exp(s - jnp.max(s, axis=0, keepdims=True))
    return e / jnp.sum(e, axis=0, keepdims=True)


def attend(pt, at, probs, mask):
    for h in range(HEADS):
        p = probabilities(pt, h, mask)
        probs[h] = p
        at[h * HDIM : (h + 1) * HDIM] = dot(head(pt, 2, h), p.astype(BF))


def attend_grad(pt, ga, probs, pg):
    for h in range(HEADS):
        q, k, v, g = head(pt, 0, h), head(pt, 1, h), head(pt, 2, h), head(ga, 0, h)
        p = probs[h]
        gp = dot(v, g, TN)
        gs = (p * (gp - jnp.sum(p * gp, axis=0, keepdims=True)) * SCALE).astype(BF)
        r = h * HDIM
        pg[r : r + HDIM] = dot(k, gs)
        pg[HD + r : HD + r + HDIM] = dot(q, gs, NT)
        pg[2 * HD + r : 2 * HD + r + HDIM] = dot(g, p.astype(BF), NT)


def space_forward_kernel(
    u_hbm, c_hbm, wq_hbm, wo_hbm,
    out, probs, pts, mine, theirs,
    pt, at, u_ref, c_ref, wq, wo, t, perm, sems,
):
    pairs = [(u_hbm, u_ref)]
    for i in range(3):
        rows = pl.ds(i * HD, HD)
        pairs.append((wq_hbm.at[rows], wq.at[rows]))
    pairs += [(wo_hbm, wo), (c_hbm, c_ref)]
    copies = [pltpu.make_async_copy(x, y, sems.at[i]) for i, (x, y) in enumerate(pairs)]
    copies[0].start()
    copies[1].start()
    copies[0].wait()
    copies[2].start()
    copies[3].start()
    u = u_ref[...].astype(F32)
    normed, _ = norm_rows(u)
    hidden = normed.astype(BF)
    lay_rows(mine, theirs, 0, hidden.astype(F32), t, perm)
    for i in range(3):
        copies[1 + i].wait()
        if i == 0:
            copies[4].start()
            copies[5].start()
        pt[i * HD : (i + 1) * HD] = rounded(dot(wq[i * HD : (i + 1) * HD], hidden, NT))
    pts[...] = pt[...].astype(BF)
    attend(pt, at, probs, None)
    a = at[...].astype(BF)
    mine[576:1152] = a
    theirs[576:1152] = a
    copies[4].wait()
    so = (u + dot(a, wo[...], TN)).astype(BF)
    copies[5].wait()
    for i in range(8):
        out[i, 0:POS] = so[i * POS : (i + 1) * POS]
        out[i, POS : 2 * POS] = c_ref[i * POS : (i + 1) * POS]


def time_kernel(x_ref, wq, wo, me, te, mid, mine, theirs, pt, at, ga, pg, probs, u_ref, c_ref, t, perm):
    for i in range(8):
        u_ref[i * POS : (i + 1) * POS] = x_ref[i, 0:POS]
        c_ref[i * POS : (i + 1) * POS] = x_ref[i, POS : 2 * POS]
    c = c_ref[...]
    normed, inverse = norm_rows(u_ref[...].astype(F32))
    pt[...] = rounded(dot(wq[...], normed.astype(BF), NT))
    ga[...] = rounded(dot(wo[...], c, NT))
    row = lax.broadcasted_iota(jnp.int32, (S, S), 0)
    col = lax.broadcasted_iota(jnp.int32, (S, S), 1)
    attend(pt, at, probs, (row % POS) == (col % POS))
    attend_grad(pt, ga, probs, pg)
    g = pg[...].astype(BF)
    grad = dot(g, wq[...], TN)
    mid[...] = norm_grad(c.astype(F32), grad, normed, inverse).astype(BF)
    lay_rows(mine, theirs, 0, rounded(normed), t, perm)
    lay_rows(mine, theirs, 576, c.astype(F32), t, perm)
    a = at[...].astype(BF)
    for out in (mine, theirs):
        out[1152:2880] = g
        out[2880:3456] = a
    mine[3456:4608] = me[...]
    theirs[3456:4608] = te[...]


def space_attention_grad_kernel(c_ref, probs, pts, wo, mine, theirs, pt, ga, pg, t, perm):
    c = c_ref[...]
    ga[...] = rounded(dot(wo[...], c, NT))
    pt[...] = pts[...].astype(F32)
    attend_grad(pt, ga, probs, pg)
    g = pg[...].astype(BF)
    lay_rows(mine, theirs, 0, c.astype(F32), t, perm)
    for out in (mine, theirs):
        out[576:2304] = g


def in_grad_kernel(c_ref, u_ref, g_ref, wq, in_grad):
    grad = dot(g_ref[576:2304], wq[...], TN)
    normed, inverse = norm_rows(u_ref[...].astype(F32))
    in_grad[...] = norm_grad(c_ref[...].astype(F32), grad, normed, inverse).astype(BF)


def spread(x, t, perm):
    t[...] = x.T
    for core in range(2):
        for y in range(4):
            for half in range(2):
                for z in range(4):
                    src = ROWS * (z * 8 + y * 2 + core) + HALF * half
                    dst = 576 * core + 144 * y + 72 * half + HALF * z
                    perm[dst : dst + HALF] = t[src : src + HALF]


def lay_rows(mine, theirs, base, x, t, perm):
    spread(x, t, perm)
    core = lax.axis_index("core")
    for out, half in ((mine, core), (theirs, 1 - core)):
        rows = perm[pl.ds(pl.multiple_of(half * 576, 576), 576)]
        out[base : base + 576] = rows.astype(BF)


def quarter(h, p):
    core = lax.axis_index("core")
    a = h * core + p * (1 - core)
    b = h * (1 - core) + p * core
    return 2 * a + (a + b) % 2


def bits(i):
    core = lax.axis_index("core")
    a, b = i // 2, ((i + 1) // 2) % 2
    return a * core + b * (1 - core), a * (1 - core) + b * core


PAIRS = ([[0, 1], [3, 2]], [[0, 3], [1, 2]])
BITS = [(h, p) for h in range(2) for p in range(2)]


def product_kernel(me, oe, ml, ol, out, left):
    early, late = (me, oe), (ml, ol)
    streams = (((early, 0), (early, 576)), ((early, 3456), (late, 0)))
    grads = (((early, 1152, 432), (early, 2880, 144)), ((late, 576, 432), (early, 4032, 144)))
    for i, (hy, py) in enumerate(BITS):
        for k in range(2):
            for f, (pair, first) in enumerate(streams[k]):
                rows = pl.ds(pl.multiple_of(quarter(hy, py) * 144 + first, 144), 144)
                for j, ref in enumerate(pair):
                    left[k, f, i * 144 : (i + 1) * 144, j * S : (j + 1) * S] = ref[rows]
    for hx, px in BITS:
        q = quarter(hx, px)
        parts = []
        for k in range(2):
            for f, (pair, first, n) in enumerate(grads[k]):
                rows = pl.ds(pl.multiple_of(first + q * n, 144), n)
                right = jnp.concatenate([ref[rows] for ref in pair], axis=1)
                parts.append(dot(left[k, f], right, NT))
        both = jnp.concatenate(parts, axis=1)
        for i, (hy, py) in enumerate(BITS):
            for hz in range(2):
                r = 144 * i + 72 * hz
                out[(hx * 2 + hy) * 2 + hz, px * 2 + py] = both[r : r + 72].astype(BF)


def first_sum_kernel(x_ref, out):
    for place in range(4):
        acc = x_ref[0, place].astype(F32)
        for j in range(1, 8):
            acc = acc + x_ref[j, place].astype(F32)
        for z in range(4):
            m = acc[HALF * z : HALF * (z + 1)]
            h, p = bits(z)
            tiles = [m[:, S * i : S * (i + 1)] for i in range(9)] + [jnp.zeros((14, S), F32)]
            rows = pl.ds(pl.multiple_of(p * 176, 176), 176)
            out[place * 2 + h, rows] = jnp.concatenate(tiles, axis=0).astype(BF)


def second_sum_kernel(x_ref, keep, send):
    own = bits(lax.axis_index("zh"))[1]
    for i, out in enumerate((keep, send)):
        rows = pl.ds(pl.multiple_of((own + i) % 2 * 176, 176), 176)
        acc = x_ref[0, rows].astype(F32)
        for j in range(1, 8):
            acc = acc + x_ref[j, rows].astype(F32)
        out[...] = acc[0:162].astype(BF)


def copies_kernel(k_ref, g_ref, out):
    acc = (k_ref[...].astype(F32) + g_ref[...].astype(F32)).astype(BF)
    for i in range(8):
        out[i] = acc


def last_kernel(x_ref, qt, ot, qs, os):
    for half in range(2):
        parts = []
        for x in range(4):
            p = x_ref[half * 4 + x].astype(F32)
            parts.append(jnp.concatenate([p[HALF * i : HALF * (i + 1)] for i in range(9)], axis=1))
        rows = pl.ds(HALF * half, HALF)
        for base, qkv, proj in ((0, qt, ot), (HD, qs, os)):
            qkv[rows] = jnp.concatenate([p[:, base : base + 432] for p in parts], axis=1)
            proj[rows] = jnp.concatenate([p[:, base + 432 : base + HD] for p in parts], axis=1)


def swap(x, axes, groups=None):
    return lax.all_to_all(
        x, axes, split_axis=0, concat_axis=0, axis_index_groups=groups, tiled=True
    )


DSP = ("zl", "x")


def cubes():
    groups = []
    for core in range(2):
        for gx in PAIRS[core]:
            for gy in PAIRS[core]:
                for even in (0, 2, 4, 6):
                    gz = (even, (even + (1, 7)[core]) % 8)
                    groups.append(
                        [
                            (((z % 2) * 4 + x) * 4 + z // 2) * 8 + y * 2 + core
                            for x in gx
                            for y in gy
                            for z in gz
                        ]
                    )
    return groups


def wide_cubes():
    return [
        [((x * 4 + z) * 4 + y) * 2 + core for x in gx for y in gy for z in gz]
        for core in range(2)
        for gx in PAIRS[1 - core]
        for gy in PAIRS[1 - core]
        for gz in PAIRS[core]
    ]


def last_pair(x):
    pairs = []
    for core in range(2):
        for i, j in PAIRS[1 - core]:
            pairs += [(i * 2 + core, j * 2 + core), (j * 2 + core, i * 2 + core)]
    return lax.ppermute(x, ("zh", "core"), pairs)


def to_other_core(x):
    return lax.ppermute(x, "core", [(0, 1), (1, 0)])


def local(latents, out_grad, wqs, wos, wqt, wot):
    u = latents[0, 0]
    wqs, wos, wqt, wot = wqs.T, wos.T, wqt.T, wot.T
    wide, thin, square = ((3 * HD, S), F32), ((HD, S), F32), ((HEADS, S, S), F32)
    full, flipped, factors = ((S, D), BF), ((D, S), F32), [((4608, S), BF)] * 2
    dense = 2 * S * D * 4 * HD
    early = [((1152, S), BF)] * 2
    late = [((2304, S), BF)] * 2
    sent, probs, pts, mine_e, theirs_e = call(
        space_forward_kernel,
        [((8, 2 * POS, D), BF), square, ((3 * HD, S), BF)] + early,
        (u, out_grad[0, 0], wqs, wos),
        [wide, thin, full, full, ((3 * HD, D), BF), ((HD, D), BF), flipped, flipped],
        flops=dense,
        limit=56,
        hbm=(0, 1, 2, 3),
    )
    mid, mine_e, theirs_e = call(
        time_kernel,
        [full] + factors,
        (swap(sent, DSP), wqt, wot, mine_e, theirs_e),
        [wide, thin, thin, wide, square, full, full, flipped, flipped],
        flops=2 * dense,
    )
    mid = swap(mid.reshape(8, POS, D), DSP).reshape(S, D)
    mid, theirs_e = lax.optimization_barrier((mid, theirs_e))
    theirs_e = to_other_core(theirs_e)
    mine_l, theirs_l = call(
        space_attention_grad_kernel,
        late,
        (mid, probs, pts, wos),
        [wide, thin, wide, flipped, flipped],
        flops=dense // 4,
    )
    theirs_l = to_other_core(theirs_l)
    (in_grad,) = call(in_grad_kernel, [full], (mid, u, mine_l, wqs), flops=dense)
    in_grad, theirs_l = lax.optimization_barrier((in_grad, theirs_l))
    (terms,) = call(
        product_kernel,
        [((8, 4, 72, D), BF)],
        (mine_e, theirs_e, mine_l, theirs_l),
        [((2, 2, 576, 2 * S), BF)],
        flops=4 * HD * 256 * 4 * HD,
        limit=32,
    )
    terms = swap(terms, ("zl", "x", "zh", "y", "core"), cubes())
    (terms,) = call(first_sum_kernel, [((8, 352, S), BF)], (terms,), limit=32)
    terms = swap(terms, ("x", "zh", "y", "core"), wide_cubes())
    keep, send = call(second_sum_kernel, [((162, S), BF)] * 2, (terms,))
    (copies,) = call(copies_kernel, [((8, 162, S), BF)], (keep, last_pair(send)))
    copies = swap(copies, DSP)
    gqt, got, gqs, gos = call(
        last_kernel, [((ROWS, 3 * HD), F32), ((ROWS, HD), F32)] * 2, (copies,)
    )
    return in_grad[None, None], gqs, gos, gqt, got


def solution(mesh):
    fine = Mesh(mesh.devices.reshape(2, 4, 4, 4, 2), ("zl", "x", "zh", "y", "core"))
    dp = ("zh", "y", "core")
    act = P(dp, ("zl", "x"), None, None)
    in_specs = (act, act, P(), P(), P(), P())
    out_specs = (act, P(dp, None), P(dp, None), P(dp, None), P(dp, None))
    return jax.shard_map(local, mesh=fine, in_specs=in_specs, out_specs=out_specs, check_vma=False)
```

```python
import functools

import jax
import jax.numpy as jnp
from jax import lax
from jax.experimental import pallas as pl
from jax.experimental.pallas import tpu as pltpu
from jax.sharding import Mesh, PartitionSpec as P

D = 1152
HEADS = 8
HDIM = 72
HD = 576
S = 128
POS = 16
ROWS = 36
HALF = 18
PIECE = 384
PIECE = 384
SCALE = HDIM ** (-0.5)
EPS = 1e-06
BF = jnp.bfloat16
F32 = jnp.float32
MIB = 1024 * 1024

NN = (((1,), (0,)), ((), ()))
NT = (((1,), (1,)), ((), ()))
TN = (((0,), (0,)), ((), ()))


def dot(a, b, dims=NN):
    return lax.dot_general(a, b, dims, preferred_element_type=F32)


def norm_rows(u):
    centred = u - jnp.mean(u, axis=-1, keepdims=True)
    inverse = lax.rsqrt(jnp.mean(centred * centred, axis=-1, keepdims=True) + EPS)
    return centred * inverse, inverse


def norm_grad(c, g, normed, inverse):
    mean_g = jnp.mean(g, axis=-1, keepdims=True)
    mean_x = jnp.mean(g * normed, axis=-1, keepdims=True)
    return c + inverse * (g - mean_g - normed * mean_x)


def rounded(x):
    return x.astype(BF).astype(F32)


def call(kernel, outs, args, scratch=(), flops=0, limit=24, hbm=()):
    vmem = pl.BlockSpec(memory_space=pltpu.VMEM)
    away = pl.BlockSpec(memory_space=pltpu.HBM)
    moved = 2 * sum(x.size * x.dtype.itemsize for x in args)
    return pl.pallas_call(
        kernel,
        out_shape=[jax.ShapeDtypeStruct(s, t) for s, t in outs],
        in_specs=[away if i in hbm else vmem for i in range(len(args))],
        out_specs=[vmem] * len(outs),
        scratch_shapes=[pltpu.VMEM(s, t) for s, t in scratch]
        + ([pltpu.SemaphoreType.DMA((6,))] if hbm else []),
        compiler_params=pltpu.CompilerParams(vmem_limit_bytes=limit * MIB),
        cost_estimate=pl.CostEstimate(flops=flops, bytes_accessed=moved, transcendentals=0),
    )(*args)


def head(ref, part, h):
    r = part * HD + h * HDIM
    return ref[r : r + HDIM].astype(BF)


def probabilities(pt, h, mask):
    s = dot(head(pt, 1, h), head(pt, 0, h), TN) * SCALE
    if mask is not None:
        s = jnp.where(mask, s, -1e30)
    e = jnp.exp(s - jnp.max(s, axis=0, keepdims=True))
    return e / jnp.sum(e, axis=0, keepdims=True)


def attend(pt, at, probs, mask):
    for h in range(HEADS):
        p = probabilities(pt, h, mask)
        probs[h] = p
        at[h * HDIM : (h + 1) * HDIM] = dot(head(pt, 2, h), p.astype(BF))


def attend_grad(pt, ga, probs, pg):
    for h in range(HEADS):
        q, k, v, g = head(pt, 0, h), head(pt, 1, h), head(pt, 2, h), head(ga, 0, h)
        p = probs[h]
        gp = dot(v, g, TN)
        gs = (p * (gp - jnp.sum(p * gp, axis=0, keepdims=True)) * SCALE).astype(BF)
        r = h * HDIM
        pg[r : r + HDIM] = dot(k, gs)
        pg[HD + r : HD + r + HDIM] = dot(q, gs, NT)
        pg[2 * HD + r : 2 * HD + r + HDIM] = dot(g, p.astype(BF), NT)


def space_forward_kernel(
    u_hbm, c_hbm, wq_hbm, wo_hbm,
    out, probs, pts, mine, theirs,
    pt, at, u_ref, c_ref, wq, wo, t, perm, sems,
):
    pairs = [(u_hbm, u_ref)]
    for i in range(3):
        rows = pl.ds(i * HD, HD)
        pairs.append((wq_hbm.at[rows], wq.at[rows]))
    pairs += [(wo_hbm, wo), (c_hbm, c_ref)]
    copies = [pltpu.make_async_copy(x, y, sems.at[i]) for i, (x, y) in enumerate(pairs)]
    for copy in copies:
        copy.start()
    copies[0].wait()
    u = u_ref[...].astype(F32)
    normed, _ = norm_rows(u)
    hidden = normed.astype(BF)
    lay_rows(mine, theirs, 0, hidden.astype(F32), t, perm)
    for i in range(3):
        copies[1 + i].wait()
        pt[i * HD : (i + 1) * HD] = rounded(dot(wq[i * HD : (i + 1) * HD], hidden, NT))
    pts[...] = pt[...].astype(BF)
    attend(pt, at, probs, None)
    a = at[...].astype(BF)
    mine[576:1152] = a
    theirs[576:1152] = a
    copies[4].wait()
    so = (u + dot(a, wo[...], TN)).astype(BF)
    copies[5].wait()
    for i in range(8):
        out[i, 0:POS] = so[i * POS : (i + 1) * POS]
        out[i, POS : 2 * POS] = c_ref[i * POS : (i + 1) * POS]


def time_kernel(x_ref, wq, wo, me, te, mid, mine, theirs, pt, at, ga, pg, probs, u_ref, c_ref, t, perm):
    for i in range(8):
        u_ref[i * POS : (i + 1) * POS] = x_ref[i, 0:POS]
        c_ref[i * POS : (i + 1) * POS] = x_ref[i, POS : 2 * POS]
    c = c_ref[...]
    normed, inverse = norm_rows(u_ref[...].astype(F32))
    pt[...] = rounded(dot(wq[...], normed.astype(BF), NT))
    ga[...] = rounded(dot(wo[...], c, NT))
    row = lax.broadcasted_iota(jnp.int32, (S, S), 0)
    col = lax.broadcasted_iota(jnp.int32, (S, S), 1)
    attend(pt, at, probs, (row % POS) == (col % POS))
    attend_grad(pt, ga, probs, pg)
    g = pg[...].astype(BF)
    grad = dot(g, wq[...], TN)
    mid[...] = norm_grad(c.astype(F32), grad, normed, inverse).astype(BF)
    lay_rows(mine, theirs, 0, rounded(normed), t, perm)
    lay_rows(mine, theirs, 576, c.astype(F32), t, perm)
    a = at[...].astype(BF)
    for out in (mine, theirs):
        out[1152:2880] = g
        out[2880:3456] = a
    mine[3456:4608] = me[...]
    theirs[3456:4608] = te[...]


def space_attention_grad_kernel(c_ref, probs, pts, wo, mine, theirs, pt, ga, pg, t, perm):
    c = c_ref[...]
    ga[...] = rounded(dot(wo[...], c, NT))
    pt[...] = pts[...].astype(F32)
    attend_grad(pt, ga, probs, pg)
    g = pg[...].astype(BF)
    lay_rows(mine, theirs, 0, c.astype(F32), t, perm)
    for out in (mine, theirs):
        out[576:2304] = g


def in_grad_kernel(c_ref, u_ref, g_ref, wq, in_grad):
    grad = dot(g_ref[576:2304], wq[...], TN)
    normed, inverse = norm_rows(u_ref[...].astype(F32))
    in_grad[...] = norm_grad(c_ref[...].astype(F32), grad, normed, inverse).astype(BF)


def spread(x, t, perm):
    t[...] = x.T
    for own in range(2):

        @pl.when(lax.axis_index("zl") == own)
        def _():
            for core in range(2):
                for y in range(4):
                    for half in range(2):
                        for z in range(4):
                            src = ROWS * (z * 8 + y * 2 + core) + HALF * (half ^ own)
                            dst = 576 * core + 144 * y + 72 * half + HALF * z
                            perm[dst : dst + HALF] = t[src : src + HALF]


def lay_rows(mine, theirs, base, x, t, perm):
    spread(x, t, perm)
    core = lax.axis_index("core")
    for out, half in ((mine, core), (theirs, 1 - core)):
        rows = perm[pl.ds(pl.multiple_of(half * 576, 576), 576)]
        out[base : base + 576] = rows.astype(BF)


def quarter(axis, h, p):
    me, core = lax.axis_index(axis), lax.axis_index("core")
    a = (me // 2 + (h * core + p * (1 - core))) % 2
    b = ((me + 1) // 2 + (h * (1 - core) + p * core)) % 2
    return 2 * a + (a + b) % 2


def bits(i):
    core = lax.axis_index("core")
    a, b = i // 2, ((i + 1) // 2) % 2
    return a * core + b * (1 - core), a * (1 - core) + b * core


PAIRS = ([[0, 1], [3, 2]], [[0, 3], [1, 2]])
BITS = [(h, p) for h in range(2) for p in range(2)]


STREAMS = {"xt": (0, 0), "ct": (0, 576), "xs": (0, 3456), "cs": (1, 0)}
SEGMENTS = (
    (("xt", 0, 1152, 432, 0, 384),),
    (("xt", 0, 1152, 432, 384, 48), ("ct", 0, 2880, 144, 0, 144), ("xs", 1, 576, 432, 0, 192)),
    (("xs", 1, 576, 432, 192, 240), ("cs", 0, 4032, 144, 0, 144)),
)


def product_kernel(piece, *refs):
    *factors, keep, send, left = refs
    pairs = [factors[i : i + 2] for i in range(0, len(factors), 2)]
    for k, (stream, *_) in enumerate(SEGMENTS[piece]):
        which, first = STREAMS[stream]
        for i, (hy, py) in enumerate(BITS):
            rows = pl.ds(pl.multiple_of(quarter("y", hy, py) * 144 + first, 144), 144)
            for j, ref in enumerate(pairs[which]):
                left[k, i * 144 : (i + 1) * 144, j * S : (j + 1) * S] = ref[rows]
    for hx, px in BITS:
        q = quarter("x", hx, px)
        parts = []
        for k, (_, which, first, n, start, count) in enumerate(SEGMENTS[piece]):
            rows = pl.ds(pl.multiple_of(first + start + q * n, 16), count)
            right = jnp.concatenate([ref[rows] for ref in pairs[which]], axis=1)
            parts.append(dot(left[k], right, NT))
        both = jnp.concatenate(parts, axis=1)
        for i, (hy, py) in enumerate(BITS):
            for hz in range(2):
                r = 144 * i + 72 * hz
                one, two, three = ((hx, hy, hz), (hy, hz, hx), (hz, hx, hy))[piece]
                out = send if one else keep
                out[two, three, px * 2 + py] = both[r : r + 72].astype(BF)


def halve_kernel(k_ref, g_ref, keep, send):
    for i, out in enumerate((keep, send)):
        out[...] = (k_ref[i].astype(F32) + g_ref[i].astype(F32)).astype(BF)


def join_kernel(*refs):
    keep, got, out = refs[:3], refs[3:6], refs[6]
    own_x, own_y = bits(lax.axis_index("x"))[1], bits(lax.axis_index("y"))[1]
    for px in range(2):
        for py in range(2):
            place = ((own_x + px) % 2) * 2 + (own_y + py) % 2
            i = px * 2 + py
            accs = [k[i].astype(F32) + g[i].astype(F32) for k, g in zip(keep, got)]
            for z in range(4):
                h, p = bits(z)
                rows = slice(HALF * z, HALF * (z + 1))
                tiles = [acc[rows, S * j : S * (j + 1)] for acc in accs for j in range(3)]
                tiles.append(jnp.zeros((14, S), F32))
                to = pl.ds(pl.multiple_of(p * 176, 176), 176)
                out[place * 2 + h, to] = jnp.concatenate(tiles, axis=0).astype(BF)


def second_sum_kernel(x_ref, keep, send):
    own = bits(lax.axis_index("zh"))[1]
    for i, out in enumerate((keep, send)):
        rows = pl.ds(pl.multiple_of((own + i) % 2 * 176, 176), 176)
        acc = x_ref[0, rows].astype(F32)
        for j in range(1, 8):
            acc = acc + x_ref[j, rows].astype(F32)
        out[...] = acc[0:162].astype(BF)


def copies_kernel(k_ref, g_ref, out):
    acc = (k_ref[...].astype(F32) + g_ref[...].astype(F32)).astype(BF)
    for i in range(8):
        out[i] = acc


def last_kernel(x_ref, qt, ot, qs, os):
    for half in range(2):
        parts = []
        for x in range(4):
            p = x_ref[half * 4 + x].astype(F32)
            parts.append(jnp.concatenate([p[HALF * i : HALF * (i + 1)] for i in range(9)], axis=1))
        rows = pl.ds(HALF * half, HALF)
        for base, qkv, proj in ((0, qt, ot), (HD, qs, os)):
            qkv[rows] = jnp.concatenate([p[:, base : base + 432] for p in parts], axis=1)
            proj[rows] = jnp.concatenate([p[:, base + 432 : base + HD] for p in parts], axis=1)


def swap(x, axes, groups=None):
    return lax.all_to_all(
        x, axes, split_axis=0, concat_axis=0, axis_index_groups=groups, tiled=True
    )


DSP = ("zl", "x")


def ring(x, axis):
    pairs = [(i * 2 + c, j * 2 + c) for c in range(2) for p in PAIRS[c] for i, j in (p, p[::-1])]
    return lax.ppermute(x, (axis, "core"), pairs)


def pair_z(x):
    pairs = []
    for z in range(8):
        for c in range(2):
            up = (z % 2 == 0) == (c == 0)
            to = (z + (1 if up else 7)) % 8
            pairs.append((((z % 2) * 4 + z // 2) * 2 + c, ((to % 2) * 4 + to // 2) * 2 + c))
    return lax.ppermute(x, ("zl", "zh", "core"), pairs)


STEPS = (lambda x: ring(x, "x"), lambda x: ring(x, "y"), pair_z)


def wide_cubes():
    return [
        [((x * 4 + z) * 4 + y) * 2 + core for x in gx for y in gy for z in gz]
        for core in range(2)
        for gx in PAIRS[1 - core]
        for gy in PAIRS[1 - core]
        for gz in PAIRS[core]
    ]


def last_pair(x):
    pairs = []
    for core in range(2):
        for i, j in PAIRS[1 - core]:
            pairs += [(i * 2 + core, j * 2 + core), (j * 2 + core, i * 2 + core)]
    return lax.ppermute(x, ("zh", "core"), pairs)


def to_other_core(x):
    return lax.ppermute(x, "core", [(0, 1), (1, 0)])


def local(latents, out_grad, wqs, wos, wqt, wot):
    u = latents[0, 0]
    wqs, wos, wqt, wot = wqs.T, wos.T, wqt.T, wot.T
    wide, thin, square = ((3 * HD, S), F32), ((HD, S), F32), ((HEADS, S, S), F32)
    full, flipped, factors = ((S, D), BF), ((D, S), F32), [((4608, S), BF)] * 2
    dense = 2 * S * D * 4 * HD
    early = [((1152, S), BF)] * 2
    late = [((2304, S), BF)] * 2
    sent, probs, pts, mine_e, theirs_e = call(
        space_forward_kernel,
        [((8, 2 * POS, D), BF), square, ((3 * HD, S), BF)] + early,
        (u, out_grad[0, 0], wqs, wos),
        [wide, thin, full, full, ((3 * HD, D), BF), ((HD, D), BF), flipped, flipped],
        flops=dense,
        limit=56,
        hbm=(0, 1, 2, 3),
    )
    mid, mine_e, theirs_e = call(
        time_kernel,
        [full] + factors,
        (swap(sent, DSP), wqt, wot, mine_e, theirs_e),
        [wide, thin, thin, wide, square, full, full, flipped, flipped],
        flops=2 * dense,
    )
    mid = swap(mid.reshape(8, POS, D), DSP).reshape(S, D)
    mid, theirs_e = lax.optimization_barrier((mid, theirs_e))
    theirs_e = to_other_core(theirs_e)
    mine_l, theirs_l = call(
        space_attention_grad_kernel,
        late,
        (mid, probs, pts, wos),
        [wide, thin, wide, flipped, flipped],
        flops=dense // 4,
    )
    theirs_l = to_other_core(theirs_l)
    (in_grad,) = call(in_grad_kernel, [full], (mid, u, mine_l, wqs), flops=dense)

    def product(piece, *pairs):
        return call(
            functools.partial(product_kernel, piece),
            [((2, 2, 4, 72, PIECE), BF)] * 2,
            pairs,
            [((len(SEGMENTS[piece]), 576, 2 * S), BF)],
            flops=2 * HD * 256 * 4 * PIECE,
        )

    early = (mine_e, theirs_e)
    keep, send = product(0, *early)
    send, theirs_l = lax.optimization_barrier((send, theirs_l))
    pairs = (*early, mine_l, theirs_l)
    halves = [(keep, send), product(1, *pairs), product(2, *pairs)]
    got = [STEPS[i](send) for i, (_, send) in enumerate(halves)]
    in_grad, got[2] = lax.optimization_barrier((in_grad, got[2]))
    for step in (1, 2):
        shape = ((2, 4, 72, PIECE), (4, 72, PIECE))[step - 1]
        halves = [call(halve_kernel, [(shape, BF)] * 2, (h[0], g)) for h, g in zip(halves, got)]
        got = [STEPS[(i + step) % 3](send) for i, (_, send) in enumerate(halves)]
    (terms,) = call(join_kernel, [((8, 352, S), BF)], ([h[0] for h in halves] + got))
    terms = swap(terms, ("x", "zh", "y", "core"), wide_cubes())
    keep, send = call(second_sum_kernel, [((162, S), BF)] * 2, (terms,))
    (copies,) = call(copies_kernel, [((8, 162, S), BF)], (keep, last_pair(send)))
    copies = swap(copies, DSP)
    gqt, got, gqs, gos = call(
        last_kernel, [((ROWS, 3 * HD), F32), ((ROWS, HD), F32)] * 2, (copies,)
    )
    return in_grad[None, None], gqs, gos, gqt, got


def solution(mesh):
    fine = Mesh(mesh.devices.reshape(2, 4, 4, 4, 2), ("zl", "x", "zh", "y", "core"))
    dp = ("zh", "y", "core")
    act = P(dp, ("zl", "x"), None, None)
    in_specs = (act, act, P(), P(), P(), P())
    out_specs = (act, P(dp, None), P(dp, None), P(dp, None), P(dp, None))
    return jax.shard_map(local, mesh=fine, in_specs=in_specs, out_specs=out_specs, check_vma=False)
```

```python
import functools

import jax
import jax.numpy as jnp
from jax import lax
from jax.experimental import pallas as pl
from jax.experimental.pallas import tpu as pltpu
from jax.sharding import Mesh, PartitionSpec as P

D = 1152
HEADS = 8
HDIM = 72
HD = 576
S = 128
POS = 16
ROWS = 36
HALF = 18
PIECE = 384
PIECE = 384
SCALE = HDIM ** (-0.5)
EPS = 1e-06
BF = jnp.bfloat16
F32 = jnp.float32
MIB = 1024 * 1024

NN = (((1,), (0,)), ((), ()))
NT = (((1,), (1,)), ((), ()))
TN = (((0,), (0,)), ((), ()))


def dot(a, b, dims=NN):
    return lax.dot_general(a, b, dims, preferred_element_type=F32)


def norm_rows(u):
    centred = u - jnp.mean(u, axis=-1, keepdims=True)
    inverse = lax.rsqrt(jnp.mean(centred * centred, axis=-1, keepdims=True) + EPS)
    return centred * inverse, inverse


def norm_grad(c, g, normed, inverse):
    mean_g = jnp.mean(g, axis=-1, keepdims=True)
    mean_x = jnp.mean(g * normed, axis=-1, keepdims=True)
    return c + inverse * (g - mean_g - normed * mean_x)


def rounded(x):
    return x.astype(BF).astype(F32)


def call(kernel, outs, args, scratch=(), flops=0, limit=24, hbm=()):
    vmem = pl.BlockSpec(memory_space=pltpu.VMEM)
    away = pl.BlockSpec(memory_space=pltpu.HBM)
    moved = 2 * sum(x.size * x.dtype.itemsize for x in args)
    return pl.pallas_call(
        kernel,
        out_shape=[jax.ShapeDtypeStruct(s, t) for s, t in outs],
        in_specs=[away if i in hbm else vmem for i in range(len(args))],
        out_specs=[vmem] * len(outs),
        scratch_shapes=[pltpu.VMEM(s, t) for s, t in scratch]
        + ([pltpu.SemaphoreType.DMA((6,))] if hbm else []),
        compiler_params=pltpu.CompilerParams(vmem_limit_bytes=limit * MIB),
        cost_estimate=pl.CostEstimate(flops=flops, bytes_accessed=moved, transcendentals=0),
    )(*args)


def head(ref, part, h):
    r = part * HD + h * HDIM
    return ref[r : r + HDIM].astype(BF)


def probabilities(pt, h, mask):
    s = dot(head(pt, 1, h), head(pt, 0, h), TN) * SCALE
    if mask is not None:
        s = jnp.where(mask, s, -1e30)
    e = jnp.exp(s - jnp.max(s, axis=0, keepdims=True))
    return e / jnp.sum(e, axis=0, keepdims=True)


def attend(pt, at, probs):
    for h in range(HEADS):
        p = probabilities(pt, h, None)
        probs[h] = p
        at[h * HDIM : (h + 1) * HDIM] = dot(head(pt, 2, h), p.astype(BF))


def attend_grad(pt, ga, p, h, pg):
    q, k, v, g = head(pt, 0, h), head(pt, 1, h), head(pt, 2, h), head(ga, 0, h)
    gp = dot(v, g, TN)
    gs = (p * (gp - jnp.sum(p * gp, axis=0, keepdims=True)) * SCALE).astype(BF)
    r = h * HDIM
    pg[r : r + HDIM] = dot(k, gs)
    pg[HD + r : HD + r + HDIM] = dot(q, gs, NT)
    pg[2 * HD + r : 2 * HD + r + HDIM] = dot(g, p.astype(BF), NT)


def space_forward_kernel(
    u_hbm, c_hbm, wq_hbm, wo_hbm,
    out, probs, pts, mine, theirs,
    pt, at, u_ref, c_ref, wq, wo, t, perm, sems,
):
    pairs = [(u_hbm, u_ref)]
    for i in range(3):
        rows = pl.ds(i * HD, HD)
        pairs.append((wq_hbm.at[rows], wq.at[rows]))
    pairs += [(wo_hbm, wo), (c_hbm, c_ref)]
    copies = [pltpu.make_async_copy(x, y, sems.at[i]) for i, (x, y) in enumerate(pairs)]
    for copy in copies:
        copy.start()
    copies[0].wait()
    u = u_ref[...].astype(F32)
    normed, _ = norm_rows(u)
    hidden = normed.astype(BF)
    lay_rows(mine, theirs, 0, hidden.astype(F32), t, perm)
    for i in range(3):
        copies[1 + i].wait()
        pt[i * HD : (i + 1) * HD] = rounded(dot(wq[i * HD : (i + 1) * HD], hidden, NT))
    pts[...] = pt[...].astype(BF)
    attend(pt, at, probs)
    a = at[...].astype(BF)
    mine[576:1152] = a
    theirs[576:1152] = a
    copies[4].wait()
    so = (u + dot(a, wo[...], TN)).astype(BF)
    copies[5].wait()
    for i in range(8):
        out[i, 0:POS] = so[i * POS : (i + 1) * POS]
        out[i, POS : 2 * POS] = c_ref[i * POS : (i + 1) * POS]


def time_kernel(x_ref, wq, wo, me, te, mid, mine, theirs, pt, at, ga, pg, u_ref, c_ref, t, perm):
    for i in range(8):
        u_ref[i * POS : (i + 1) * POS] = x_ref[i, 0:POS]
        c_ref[i * POS : (i + 1) * POS] = x_ref[i, POS : 2 * POS]
    c = c_ref[...]
    normed, inverse = norm_rows(u_ref[...].astype(F32))
    pt[...] = rounded(dot(wq[...], normed.astype(BF), NT))
    ga[...] = rounded(dot(wo[...], c, NT))
    row = lax.broadcasted_iota(jnp.int32, (S, S), 0)
    col = lax.broadcasted_iota(jnp.int32, (S, S), 1)
    mask = (row % POS) == (col % POS)
    for h in range(HEADS):
        p = probabilities(pt, h, mask)
        at[h * HDIM : (h + 1) * HDIM] = dot(head(pt, 2, h), p.astype(BF))
        attend_grad(pt, ga, p, h, pg)
    g = pg[...].astype(BF)
    grad = dot(g, wq[...], TN)
    mid[...] = norm_grad(c.astype(F32), grad, normed, inverse).astype(BF)
    lay_rows(mine, theirs, 0, rounded(normed), t, perm)
    lay_rows(mine, theirs, 576, c.astype(F32), t, perm)
    a = at[...].astype(BF)
    for out in (mine, theirs):
        out[1152:2880] = g
        out[2880:3456] = a
    mine[3456:4608] = me[...]
    theirs[3456:4608] = te[...]


def space_attention_grad_kernel(c_ref, probs, pts, wo, mine, theirs, pt, ga, pg, t, perm):
    c = c_ref[...]
    ga[...] = rounded(dot(wo[...], c, NT))
    pt[...] = pts[...].astype(F32)
    for h in range(HEADS):
        attend_grad(pt, ga, probs[h], h, pg)
    g = pg[...].astype(BF)
    lay_rows(mine, theirs, 0, c.astype(F32), t, perm)
    for out in (mine, theirs):
        out[576:2304] = g


def in_grad_kernel(c_ref, u_ref, g_ref, wq, in_grad):
    grad = dot(g_ref[576:2304], wq[...], TN)
    normed, inverse = norm_rows(u_ref[...].astype(F32))
    in_grad[...] = norm_grad(c_ref[...].astype(F32), grad, normed, inverse).astype(BF)


def spread(x, t, perm):
    t[...] = x.T
    for own in range(2):

        @pl.when(lax.axis_index("zl") == own)
        def _():
            for core in range(2):
                for y in range(4):
                    for half in range(2):
                        for z in range(4):
                            src = ROWS * (z * 8 + y * 2 + core) + HALF * (half ^ own)
                            dst = 576 * core + 144 * y + 72 * half + HALF * z
                            perm[dst : dst + HALF] = t[src : src + HALF]


def lay_rows(mine, theirs, base, x, t, perm):
    spread(x, t, perm)
    core = lax.axis_index("core")
    for out, half in ((mine, core), (theirs, 1 - core)):
        rows = perm[pl.ds(pl.multiple_of(half * 576, 576), 576)]
        out[base : base + 576] = rows.astype(BF)


def quarter(axis, h, p):
    me, core = lax.axis_index(axis), lax.axis_index("core")
    a = (me // 2 + (h * core + p * (1 - core))) % 2
    b = ((me + 1) // 2 + (h * (1 - core) + p * core)) % 2
    return 2 * a + (a + b) % 2


def bits(i):
    core = lax.axis_index("core")
    a, b = i // 2, ((i + 1) // 2) % 2
    return a * core + b * (1 - core), a * (1 - core) + b * core


PAIRS = ([[0, 1], [3, 2]], [[0, 3], [1, 2]])
BITS = [(h, p) for h in range(2) for p in range(2)]


STREAMS = {"xt": (0, 0), "ct": (0, 576), "xs": (0, 3456), "cs": (1, 0)}
SEGMENTS = (
    (("xt", 0, 1152, 432, 0, 384),),
    (("xt", 0, 1152, 432, 384, 48), ("ct", 0, 2880, 144, 0, 144), ("xs", 1, 576, 432, 0, 192)),
    (("xs", 1, 576, 432, 192, 240), ("cs", 0, 4032, 144, 0, 144)),
)


def product_kernel(piece, *refs):
    *factors, keep, send, left = refs
    pairs = [factors[i : i + 2] for i in range(0, len(factors), 2)]
    for k, (stream, *_) in enumerate(SEGMENTS[piece]):
        which, first = STREAMS[stream]
        for i, (hy, py) in enumerate(BITS):
            rows = pl.ds(pl.multiple_of(quarter("y", hy, py) * 144 + first, 144), 144)
            for j, ref in enumerate(pairs[which]):
                left[k, i * 144 : (i + 1) * 144, j * S : (j + 1) * S] = ref[rows]
    for hx, px in BITS:
        q = quarter("x", hx, px)
        parts = []
        for k, (_, which, first, n, start, count) in enumerate(SEGMENTS[piece]):
            rows = pl.ds(pl.multiple_of(first + start + q * n, 16), count)
            right = jnp.concatenate([ref[rows] for ref in pairs[which]], axis=1)
            parts.append(dot(left[k], right, NT))
        both = jnp.concatenate(parts, axis=1)
        for i, (hy, py) in enumerate(BITS):
            for hz in range(2):
                r = 144 * i + 72 * hz
                one, two, three = ((hx, hy, hz), (hy, hz, hx), (hz, hx, hy))[piece]
                out = send if one else keep
                out[two, three, px * 2 + py] = both[r : r + 72].astype(out.dtype)


def halve_kernel(k_ref, g_ref, keep, send):
    for i, out in enumerate((keep, send)):
        out[...] = (k_ref[i] + g_ref[i].astype(F32)).astype(out.dtype)


def join_kernel(*refs):
    keep, got, out = refs[:3], refs[3:6], refs[6]
    own_x, own_y = bits(lax.axis_index("x"))[1], bits(lax.axis_index("y"))[1]
    for px in range(2):
        for py in range(2):
            place = ((own_x + px) % 2) * 2 + (own_y + py) % 2
            i = px * 2 + py
            accs = [k[i] + g[i].astype(F32) for k, g in zip(keep, got)]
            for z in range(4):
                h, p = bits(z)
                rows = slice(HALF * z, HALF * (z + 1))
                tiles = [acc[rows, S * j : S * (j + 1)] for acc in accs for j in range(3)]
                tiles.append(jnp.zeros((14, S), F32))
                to = pl.ds(pl.multiple_of(p * 176, 176), 176)
                out[place * 2 + h, to] = jnp.concatenate(tiles, axis=0).astype(BF)


def second_sum_kernel(x_ref, keep, send):
    own = bits(lax.axis_index("zh"))[1]
    for i, out in enumerate((keep, send)):
        rows = pl.ds(pl.multiple_of((own + i) % 2 * 176, 176), 176)
        acc = x_ref[0, rows].astype(F32)
        for j in range(1, 8):
            acc = acc + x_ref[j, rows].astype(F32)
        out[...] = acc[0:162].astype(out.dtype)


def copies_kernel(k_ref, g_ref, out):
    acc = (k_ref[...] + g_ref[...].astype(F32)).astype(BF)
    for i in range(8):
        out[i] = acc


def last_kernel(x_ref, qt, ot, qs, os):
    for half in range(2):
        parts = []
        for x in range(4):
            p = x_ref[half * 4 + x].astype(F32)
            parts.append(jnp.concatenate([p[HALF * i : HALF * (i + 1)] for i in range(9)], axis=1))
        rows = pl.ds(HALF * half, HALF)
        for base, qkv, proj in ((0, qt, ot), (HD, qs, os)):
            qkv[rows] = jnp.concatenate([p[:, base : base + 432] for p in parts], axis=1)
            proj[rows] = jnp.concatenate([p[:, base + 432 : base + HD] for p in parts], axis=1)


def swap(x, axes, groups=None):
    return lax.all_to_all(
        x, axes, split_axis=0, concat_axis=0, axis_index_groups=groups, tiled=True
    )


DSP = ("zl", "x")


def ring(x, axis):
    pairs = [(i * 2 + c, j * 2 + c) for c in range(2) for p in PAIRS[c] for i, j in (p, p[::-1])]
    return lax.ppermute(x, (axis, "core"), pairs)


def pair_z(x):
    pairs = []
    for z in range(8):
        for c in range(2):
            up = (z % 2 == 0) == (c == 0)
            to = (z + (1 if up else 7)) % 8
            pairs.append((((z % 2) * 4 + z // 2) * 2 + c, ((to % 2) * 4 + to // 2) * 2 + c))
    return lax.ppermute(x, ("zl", "zh", "core"), pairs)


STEPS = (lambda x: ring(x, "x"), lambda x: ring(x, "y"), pair_z)


def wide_cubes():
    return [
        [((x * 4 + z) * 4 + y) * 2 + core for x in gx for y in gy for z in gz]
        for core in range(2)
        for gx in PAIRS[1 - core]
        for gy in PAIRS[1 - core]
        for gz in PAIRS[core]
    ]


def last_pair(x):
    pairs = []
    for core in range(2):
        for i, j in PAIRS[1 - core]:
            pairs += [(i * 2 + core, j * 2 + core), (j * 2 + core, i * 2 + core)]
    return lax.ppermute(x, ("zh", "core"), pairs)


def to_other_core(x):
    return lax.ppermute(x, "core", [(0, 1), (1, 0)])


def local(latents, out_grad, wqs, wos, wqt, wot):
    u = latents[0, 0]
    wqs, wos, wqt, wot = wqs.T, wos.T, wqt.T, wot.T
    wide, thin, square = ((3 * HD, S), F32), ((HD, S), F32), ((HEADS, S, S), F32)
    full, flipped, factors = ((S, D), BF), ((D, S), F32), [((4608, S), BF)] * 2
    dense = 2 * S * D * 4 * HD
    early = [((1152, S), BF)] * 2
    late = [((2304, S), BF)] * 2
    sent, probs, pts, mine_e, theirs_e = call(
        space_forward_kernel,
        [((8, 2 * POS, D), BF), square, ((3 * HD, S), BF)] + early,
        (u, out_grad[0, 0], wqs, wos),
        [wide, thin, full, full, ((3 * HD, D), BF), ((HD, D), BF), flipped, flipped],
        flops=dense,
        limit=56,
        hbm=(0, 1, 2, 3),
    )
    mid, mine_e, theirs_e = call(
        time_kernel,
        [full] + factors,
        (swap(sent, DSP), wqt, wot, mine_e, theirs_e),
        [wide, thin, thin, wide, full, full, flipped, flipped],
        flops=2 * dense,
    )
    mid = swap(mid.reshape(8, POS, D), DSP).reshape(S, D)
    mid, theirs_e = lax.optimization_barrier((mid, theirs_e))
    theirs_e = to_other_core(theirs_e)
    mine_l, theirs_l = call(
        space_attention_grad_kernel,
        late,
        (mid, probs, pts, wos),
        [wide, thin, wide, flipped, flipped],
        flops=dense // 4,
    )
    theirs_l = to_other_core(theirs_l)
    (in_grad,) = call(in_grad_kernel, [full], (mid, u, mine_l, wqs), flops=dense)

    def product(piece, *pairs):
        return call(
            functools.partial(product_kernel, piece),
            [((2, 2, 4, 72, PIECE), F32), ((2, 2, 4, 72, PIECE), BF)],
            pairs,
            [((len(SEGMENTS[piece]), 576, 2 * S), BF)],
            flops=2 * HD * 256 * 4 * PIECE,
        )

    early = (mine_e, theirs_e)
    keep, send = product(0, *early)
    keep, theirs_l = lax.optimization_barrier((keep, theirs_l))
    pairs = (*early, mine_l, theirs_l)
    halves = [(keep, send), product(1, *pairs), product(2, *pairs)]
    got = [STEPS[i](send) for i, (_, send) in enumerate(halves)]
    in_grad, got[2] = lax.optimization_barrier((in_grad, got[2]))
    for step in (1, 2):
        shape = ((2, 4, 72, PIECE), (4, 72, PIECE))[step - 1]
        halves = [
            call(halve_kernel, [(shape, F32), (shape, BF)], (h[0], g)) for h, g in zip(halves, got)
        ]
        got = [STEPS[(i + step) % 3](send) for i, (_, send) in enumerate(halves)]
    (terms,) = call(join_kernel, [((8, 352, S), BF)], ([h[0] for h in halves] + got))
    terms = swap(terms, ("x", "zh", "y", "core"), wide_cubes())
    keep, send = call(second_sum_kernel, [((162, S), F32), ((162, S), BF)], (terms,))
    (copies,) = call(copies_kernel, [((8, 162, S), BF)], (keep, last_pair(send)))
    copies = swap(copies, DSP)
    gqt, got, gqs, gos = call(
        last_kernel, [((ROWS, 3 * HD), F32), ((ROWS, HD), F32)] * 2, (copies,)
    )
    return in_grad[None, None], gqs, gos, gqt, got


def solution(mesh):
    fine = Mesh(mesh.devices.reshape(2, 4, 4, 4, 2), ("zl", "x", "zh", "y", "core"))
    dp = ("zh", "y", "core")
    act = P(dp, ("zl", "x"), None, None)
    in_specs = (act, act, P(), P(), P(), P())
    out_specs = (act, P(dp, None), P(dp, None), P(dp, None), P(dp, None))
    return jax.shard_map(local, mesh=fine, in_specs=in_specs, out_specs=out_specs, check_vma=False)
```

```python
import functools

import jax
import jax.numpy as jnp
from jax import lax
from jax.experimental import pallas as pl
from jax.experimental.pallas import tpu as pltpu
from jax.sharding import Mesh, PartitionSpec as P

D = 1152
HEADS = 8
HDIM = 72
HD = 576
S = 128
POS = 16
ROWS = 36
HALF = 18
PIECE = 384
PIECE = 384
SCALE = HDIM ** (-0.5)
EPS = 1e-06
BF = jnp.bfloat16
F32 = jnp.float32
MIB = 1024 * 1024

NN = (((1,), (0,)), ((), ()))
NT = (((1,), (1,)), ((), ()))
TN = (((0,), (0,)), ((), ()))


def dot(a, b, dims=NN):
    return lax.dot_general(a, b, dims, preferred_element_type=F32)


def norm_rows(u):
    centred = u - jnp.mean(u, axis=-1, keepdims=True)
    inverse = lax.rsqrt(jnp.mean(centred * centred, axis=-1, keepdims=True) + EPS)
    return centred * inverse, inverse


def norm_grad(c, g, normed, inverse):
    mean_g = jnp.mean(g, axis=-1, keepdims=True)
    mean_x = jnp.mean(g * normed, axis=-1, keepdims=True)
    return c + inverse * (g - mean_g - normed * mean_x)


def rounded(x):
    return x.astype(BF).astype(F32)


def call(kernel, outs, args, scratch=(), flops=0, limit=24, hbm=()):
    vmem = pl.BlockSpec(memory_space=pltpu.VMEM)
    away = pl.BlockSpec(memory_space=pltpu.HBM)
    moved = 2 * sum(x.size * x.dtype.itemsize for x in args)
    return pl.pallas_call(
        kernel,
        out_shape=[jax.ShapeDtypeStruct(s, t) for s, t in outs],
        in_specs=[away if i in hbm else vmem for i in range(len(args))],
        out_specs=[vmem] * len(outs),
        scratch_shapes=[pltpu.VMEM(s, t) for s, t in scratch]
        + ([pltpu.SemaphoreType.DMA((6,))] if hbm else []),
        compiler_params=pltpu.CompilerParams(vmem_limit_bytes=limit * MIB),
        cost_estimate=pl.CostEstimate(flops=flops, bytes_accessed=moved, transcendentals=0),
    )(*args)


def head(ref, part, h):
    r = part * HD + h * HDIM
    return ref[r : r + HDIM].astype(BF)


def probabilities(pt, h, mask):
    s = dot(head(pt, 1, h), head(pt, 0, h), TN) * SCALE
    if mask is not None:
        s = jnp.where(mask, s, -1e30)
    e = jnp.exp(s - jnp.max(s, axis=0, keepdims=True))
    return e / jnp.sum(e, axis=0, keepdims=True)


def attend(pt, at, probs, mask):
    for h in range(HEADS):
        p = probabilities(pt, h, mask)
        probs[h] = p
        at[h * HDIM : (h + 1) * HDIM] = dot(head(pt, 2, h), p.astype(BF))


def attend_grad(pt, ga, p, h, pg):
    q, k, v, g = head(pt, 0, h), head(pt, 1, h), head(pt, 2, h), head(ga, 0, h)
    gp = dot(v, g, TN)
    gs = (p * (gp - jnp.sum(p * gp, axis=0, keepdims=True)) * SCALE).astype(BF)
    r = h * HDIM
    pg[r : r + HDIM] = dot(k, gs)
    pg[HD + r : HD + r + HDIM] = dot(q, gs, NT)
    pg[2 * HD + r : 2 * HD + r + HDIM] = dot(g, p.astype(BF), NT)


def space_forward_kernel(
    u_hbm, c_hbm, wq_hbm, wo_hbm,
    out, probs, pts, mine, theirs,
    pt, at, u_ref, c_ref, wq, wo, t, perm, sems,
):
    pairs = [(u_hbm, u_ref)]
    for i in range(3):
        rows = pl.ds(i * HD, HD)
        pairs.append((wq_hbm.at[rows], wq.at[rows]))
    pairs += [(wo_hbm, wo), (c_hbm, c_ref)]
    copies = [pltpu.make_async_copy(x, y, sems.at[i]) for i, (x, y) in enumerate(pairs)]
    for copy in copies:
        copy.start()
    copies[0].wait()
    u = u_ref[...].astype(F32)
    normed, _ = norm_rows(u)
    hidden = normed.astype(BF)
    lay_rows(mine, theirs, 0, hidden.astype(F32), t, perm)
    for i in range(3):
        copies[1 + i].wait()
        pt[i * HD : (i + 1) * HD] = rounded(dot(wq[i * HD : (i + 1) * HD], hidden, NT))
    pts[...] = pt[...].astype(BF)
    attend(pt, at, probs, None)
    a = at[...].astype(BF)
    mine[576:1152] = a
    theirs[576:1152] = a
    copies[4].wait()
    so = (u + dot(a, wo[...], TN)).astype(BF)
    copies[5].wait()
    for i in range(8):
        out[i, 0:POS] = so[i * POS : (i + 1) * POS]
        out[i, POS : 2 * POS] = c_ref[i * POS : (i + 1) * POS]


def time_kernel(x_ref, wq, wo, me, te, mid, mine, theirs, pt, at, ga, pg, probs, u_ref, c_ref, t, perm):
    for i in range(8):
        u_ref[i * POS : (i + 1) * POS] = x_ref[i, 0:POS]
        c_ref[i * POS : (i + 1) * POS] = x_ref[i, POS : 2 * POS]
    c = c_ref[...]
    normed, inverse = norm_rows(u_ref[...].astype(F32))
    pt[...] = rounded(dot(wq[...], normed.astype(BF), NT))
    ga[...] = rounded(dot(wo[...], c, NT))
    row = lax.broadcasted_iota(jnp.int32, (S, S), 0)
    col = lax.broadcasted_iota(jnp.int32, (S, S), 1)
    attend(pt, at, probs, (row % POS) == (col % POS))
    for h in range(HEADS):
        attend_grad(pt, ga, probs[h], h, pg)
    g = pg[...].astype(BF)
    grad = dot(g, wq[...], TN)
    mid[...] = norm_grad(c.astype(F32), grad, normed, inverse).astype(BF)
    lay_rows(mine, theirs, 0, rounded(normed), t, perm)
    lay_rows(mine, theirs, 576, c.astype(F32), t, perm)
    a = at[...].astype(BF)
    for out in (mine, theirs):
        out[1152:2880] = g
        out[2880:3456] = a
    mine[3456:4608] = me[...]
    theirs[3456:4608] = te[...]


def space_attention_grad_kernel(c_ref, probs, pts, wo, mine, theirs, pt, ga, pg, t, perm):
    c = c_ref[...]
    ga[...] = rounded(dot(wo[...], c, NT))
    pt[...] = pts[...].astype(F32)
    for h in range(HEADS):
        attend_grad(pt, ga, probs[h], h, pg)
    g = pg[...].astype(BF)
    lay_rows(mine, theirs, 0, c.astype(F32), t, perm)
    for out in (mine, theirs):
        out[576:2304] = g


def in_grad_kernel(c_ref, u_ref, g_ref, wq, in_grad):
    grad = dot(g_ref[576:2304], wq[...], TN)
    normed, inverse = norm_rows(u_ref[...].astype(F32))
    in_grad[...] = norm_grad(c_ref[...].astype(F32), grad, normed, inverse).astype(BF)


def spread(x, t, perm):
    t[...] = x.T
    for own in range(2):

        @pl.when(lax.axis_index("zl") == own)
        def _():
            for core in range(2):
                for y in range(4):
                    for half in range(2):
                        for z in range(4):
                            src = ROWS * (z * 8 + y * 2 + core) + HALF * (half ^ own)
                            dst = 576 * core + 144 * y + 72 * half + HALF * z
                            perm[dst : dst + HALF] = t[src : src + HALF]


def lay_rows(mine, theirs, base, x, t, perm):
    spread(x, t, perm)
    core = lax.axis_index("core")
    for out, half in ((mine, core), (theirs, 1 - core)):
        rows = perm[pl.ds(pl.multiple_of(half * 576, 576), 576)]
        out[base : base + 576] = rows.astype(BF)


def quarter(axis, h, p):
    me, core = lax.axis_index(axis), lax.axis_index("core")
    a = (me // 2 + (h * core + p * (1 - core))) % 2
    b = ((me + 1) // 2 + (h * (1 - core) + p * core)) % 2
    return 2 * a + (a + b) % 2


def bits(i):
    core = lax.axis_index("core")
    a, b = i // 2, ((i + 1) // 2) % 2
    return a * core + b * (1 - core), a * (1 - core) + b * core


PAIRS = ([[0, 1], [3, 2]], [[0, 3], [1, 2]])
BITS = [(h, p) for h in range(2) for p in range(2)]


STREAMS = {"xt": (0, 0), "ct": (0, 576), "xs": (0, 3456), "cs": (1, 0)}
SEGMENTS = (
    (("xt", 0, 1152, 432, 0, 384),),
    (("xt", 0, 1152, 432, 384, 48), ("ct", 0, 2880, 144, 0, 144), ("xs", 1, 576, 432, 0, 192)),
    (("xs", 1, 576, 432, 192, 240), ("cs", 0, 4032, 144, 0, 144)),
)


def product_kernel(piece, *refs):
    *factors, keep, send, left = refs
    pairs = [factors[i : i + 2] for i in range(0, len(factors), 2)]
    for k, (stream, *_) in enumerate(SEGMENTS[piece]):
        which, first = STREAMS[stream]
        for i, (hy, py) in enumerate(BITS):
            rows = pl.ds(pl.multiple_of(quarter("y", hy, py) * 144 + first, 144), 144)
            for j, ref in enumerate(pairs[which]):
                left[k, i * 144 : (i + 1) * 144, j * S : (j + 1) * S] = ref[rows]
    for hx, px in BITS:
        q = quarter("x", hx, px)
        parts = []
        for k, (_, which, first, n, start, count) in enumerate(SEGMENTS[piece]):
            rows = pl.ds(pl.multiple_of(first + start + q * n, 16), count)
            right = jnp.concatenate([ref[rows] for ref in pairs[which]], axis=1)
            parts.append(dot(left[k], right, NT))
        both = jnp.concatenate(parts, axis=1)
        for i, (hy, py) in enumerate(BITS):
            for hz in range(2):
                r = 144 * i + 72 * hz
                one, two, three = ((hx, hy, hz), (hy, hz, hx), (hz, hx, hy))[piece]
                out = send if one else keep
                out[two, three, px * 2 + py] = both[r : r + 72].astype(out.dtype)


def halve_kernel(k_ref, g_ref, keep, send):
    for i, out in enumerate((keep, send)):
        out[...] = (k_ref[i].astype(F32) + g_ref[i].astype(F32)).astype(out.dtype)


def join_kernel(*refs):
    keep, got, out = refs[:3], refs[3:6], refs[6]
    own_x, own_y = bits(lax.axis_index("x"))[1], bits(lax.axis_index("y"))[1]
    for px in range(2):
        for py in range(2):
            place = ((own_x + px) % 2) * 2 + (own_y + py) % 2
            i = px * 2 + py
            accs = [k[i] + g[i].astype(F32) for k, g in zip(keep, got)]
            for z in range(4):
                h, p = bits(z)
                rows = slice(HALF * z, HALF * (z + 1))
                tiles = [acc[rows, S * j : S * (j + 1)] for acc in accs for j in range(3)]
                tiles.append(jnp.zeros((14, S), F32))
                to = pl.ds(pl.multiple_of(p * 176, 176), 176)
                out[place * 2 + h, to] = jnp.concatenate(tiles, axis=0).astype(BF)


def second_sum_kernel(x_ref, keep, send):
    own = bits(lax.axis_index("zh"))[1]
    for i, out in enumerate((keep, send)):
        rows = pl.ds(pl.multiple_of((own + i) % 2 * 176, 176), 176)
        acc = x_ref[0, rows].astype(F32)
        for j in range(1, 8):
            acc = acc + x_ref[j, rows].astype(F32)
        out[...] = acc[0:162].astype(out.dtype)


def copies_kernel(k_ref, g_ref, out):
    acc = (k_ref[...] + g_ref[...].astype(F32)).astype(BF)
    for i in range(8):
        out[i] = acc


def last_kernel(x_ref, qt, ot, qs, os):
    for half in range(2):
        parts = []
        for x in range(4):
            p = x_ref[half * 4 + x].astype(F32)
            parts.append(jnp.concatenate([p[HALF * i : HALF * (i + 1)] for i in range(9)], axis=1))
        rows = pl.ds(HALF * half, HALF)
        for base, qkv, proj in ((0, qt, ot), (HD, qs, os)):
            qkv[rows] = jnp.concatenate([p[:, base : base + 432] for p in parts], axis=1)
            proj[rows] = jnp.concatenate([p[:, base + 432 : base + HD] for p in parts], axis=1)


def swap(x, axes, groups=None):
    return lax.all_to_all(
        x, axes, split_axis=0, concat_axis=0, axis_index_groups=groups, tiled=True
    )


DSP = ("zl", "x")


def ring(x, axis):
    pairs = [(i * 2 + c, j * 2 + c) for c in range(2) for p in PAIRS[c] for i, j in (p, p[::-1])]
    return lax.ppermute(x, (axis, "core"), pairs)


def pair_z(x):
    pairs = []
    for z in range(8):
        for c in range(2):
            up = (z % 2 == 0) == (c == 0)
            to = (z + (1 if up else 7)) % 8
            pairs.append((((z % 2) * 4 + z // 2) * 2 + c, ((to % 2) * 4 + to // 2) * 2 + c))
    return lax.ppermute(x, ("zl", "zh", "core"), pairs)


STEPS = (lambda x: ring(x, "x"), lambda x: ring(x, "y"), pair_z)


def wide_cubes():
    return [
        [((x * 4 + z) * 4 + y) * 2 + core for x in gx for y in gy for z in gz]
        for core in range(2)
        for gx in PAIRS[1 - core]
        for gy in PAIRS[1 - core]
        for gz in PAIRS[core]
    ]


def last_pair(x):
    pairs = []
    for core in range(2):
        for i, j in PAIRS[1 - core]:
            pairs += [(i * 2 + core, j * 2 + core), (j * 2 + core, i * 2 + core)]
    return lax.ppermute(x, ("zh", "core"), pairs)


def to_other_core(x):
    return lax.ppermute(x, "core", [(0, 1), (1, 0)])


def local(latents, out_grad, wqs, wos, wqt, wot):
    u = latents[0, 0]
    wqs, wos, wqt, wot = wqs.T, wos.T, wqt.T, wot.T
    wide, thin, square = ((3 * HD, S), F32), ((HD, S), F32), ((HEADS, S, S), F32)
    full, flipped, factors = ((S, D), BF), ((D, S), F32), [((4608, S), BF)] * 2
    dense = 2 * S * D * 4 * HD
    early = [((1152, S), BF)] * 2
    late = [((2304, S), BF)] * 2
    sent, probs, pts, mine_e, theirs_e = call(
        space_forward_kernel,
        [((8, 2 * POS, D), BF), square, ((3 * HD, S), BF)] + early,
        (u, out_grad[0, 0], wqs, wos),
        [wide, thin, full, full, ((3 * HD, D), BF), ((HD, D), BF), flipped, flipped],
        flops=dense,
        limit=56,
        hbm=(0, 1, 2, 3),
    )
    mid, mine_e, theirs_e = call(
        time_kernel,
        [full] + factors,
        (swap(sent, DSP), wqt, wot, mine_e, theirs_e),
        [wide, thin, thin, wide, square, full, full, flipped, flipped],
        flops=2 * dense,
    )
    mid = swap(mid.reshape(8, POS, D), DSP).reshape(S, D)
    mid, theirs_e = lax.optimization_barrier((mid, theirs_e))
    theirs_e = to_other_core(theirs_e)
    mine_l, theirs_l = call(
        space_attention_grad_kernel,
        late,
        (mid, probs, pts, wos),
        [wide, thin, wide, flipped, flipped],
        flops=dense // 4,
    )
    theirs_l = to_other_core(theirs_l)
    (in_grad,) = call(in_grad_kernel, [full], (mid, u, mine_l, wqs), flops=dense)

    def product(piece, *pairs):
        return call(
            functools.partial(product_kernel, piece),
            [((2, 2, 4, 72, PIECE), BF)] * 2,
            pairs,
            [((len(SEGMENTS[piece]), 576, 2 * S), BF)],
            flops=2 * HD * 256 * 4 * PIECE,
        )

    early = (mine_e, theirs_e)
    keep, send = product(0, *early)
    keep, theirs_l = lax.optimization_barrier((keep, theirs_l))
    pairs = (*early, mine_l, theirs_l)
    halves = [(keep, send), product(1, *pairs), product(2, *pairs)]
    got = [STEPS[i](send) for i, (_, send) in enumerate(halves)]
    in_grad, got[2] = lax.optimization_barrier((in_grad, got[2]))
    for step in (1, 2):
        shape = ((2, 4, 72, PIECE), (4, 72, PIECE))[step - 1]
        halves = [
            call(halve_kernel, [(shape, F32), (shape, BF)], (h[0], g)) for h, g in zip(halves, got)
        ]
        got = [STEPS[(i + step) % 3](send) for i, (_, send) in enumerate(halves)]
    (terms,) = call(join_kernel, [((8, 352, S), BF)], ([h[0] for h in halves] + got))
    terms = swap(terms, ("x", "zh", "y", "core"), wide_cubes())
    keep, send = call(second_sum_kernel, [((162, S), F32), ((162, S), BF)], (terms,))
    (copies,) = call(copies_kernel, [((8, 162, S), BF)], (keep, last_pair(send)))
    copies = swap(copies, DSP)
    gqt, got, gqs, gos = call(
        last_kernel, [((ROWS, 3 * HD), F32), ((ROWS, HD), F32)] * 2, (copies,)
    )
    return in_grad[None, None], gqs, gos, gqt, got


def solution(mesh):
    fine = Mesh(mesh.devices.reshape(2, 4, 4, 4, 2), ("zl", "x", "zh", "y", "core"))
    dp = ("zh", "y", "core")
    act = P(dp, ("zl", "x"), None, None)
    in_specs = (act, act, P(), P(), P(), P())
    out_specs = (act, P(dp, None), P(dp, None), P(dp, None), P(dp, None))
    return jax.shard_map(local, mesh=fine, in_specs=in_specs, out_specs=out_specs, check_vma=False)
```

```python
import functools

import jax
import jax.numpy as jnp
from jax import lax
from jax.experimental import pallas as pl
from jax.experimental.pallas import tpu as pltpu
from jax.sharding import Mesh, PartitionSpec as P

D = 1152
HEADS = 8
HDIM = 72
HD = 576
S = 128
POS = 16
ROWS = 36
HALF = 18
PIECE = 384
PIECE = 384
SCALE = HDIM ** (-0.5)
EPS = 1e-06
BF = jnp.bfloat16
F32 = jnp.float32
MIB = 1024 * 1024

NN = (((1,), (0,)), ((), ()))
NT = (((1,), (1,)), ((), ()))
TN = (((0,), (0,)), ((), ()))


def dot(a, b, dims=NN):
    return lax.dot_general(a, b, dims, preferred_element_type=F32)


def norm_rows(u):
    centred = u - jnp.mean(u, axis=-1, keepdims=True)
    inverse = lax.rsqrt(jnp.mean(centred * centred, axis=-1, keepdims=True) + EPS)
    return centred * inverse, inverse


def norm_grad(c, g, normed, inverse):
    mean_g = jnp.mean(g, axis=-1, keepdims=True)
    mean_x = jnp.mean(g * normed, axis=-1, keepdims=True)
    return c + inverse * (g - mean_g - normed * mean_x)


def rounded(x):
    return x.astype(BF).astype(F32)


def call(kernel, outs, args, scratch=(), flops=0, limit=24, hbm=(), far=False):
    vmem = pl.BlockSpec(memory_space=pltpu.VMEM)
    away = pl.BlockSpec(memory_space=pltpu.HBM)
    moved = 2 * sum(x.size * x.dtype.itemsize for x in args)
    return pl.pallas_call(
        kernel,
        out_shape=[jax.ShapeDtypeStruct(s, t) for s, t in outs],
        in_specs=[away if i in hbm else vmem for i in range(len(args))],
        out_specs=[away if far else vmem] * len(outs),
        scratch_shapes=[pltpu.VMEM(s, t) for s, t in scratch]
        + ([pltpu.SemaphoreType.DMA((11,))] if hbm else []),
        compiler_params=pltpu.CompilerParams(vmem_limit_bytes=limit * MIB),
        cost_estimate=pl.CostEstimate(flops=flops, bytes_accessed=moved, transcendentals=0),
    )(*args)


def head(ref, part, h):
    r = part * HD + h * HDIM
    return ref[r : r + HDIM].astype(BF)


def probabilities(pt, h, mask):
    s = dot(head(pt, 1, h), head(pt, 0, h), TN) * SCALE
    if mask is not None:
        s = jnp.where(mask, s, -1e30)
    e = jnp.exp(s - jnp.max(s, axis=0, keepdims=True))
    return e / jnp.sum(e, axis=0, keepdims=True)


def attend(pt, at, probs, mask):
    for h in range(HEADS):
        p = probabilities(pt, h, mask)
        probs[h] = p
        at[h * HDIM : (h + 1) * HDIM] = dot(head(pt, 2, h), p.astype(BF))


def attend_grad(pt, ga, p, h, pg):
    q, k, v, g = head(pt, 0, h), head(pt, 1, h), head(pt, 2, h), head(ga, 0, h)
    gp = dot(v, g, TN)
    gs = (p * (gp - jnp.sum(p * gp, axis=0, keepdims=True)) * SCALE).astype(BF)
    r = h * HDIM
    pg[r : r + HDIM] = dot(k, gs)
    pg[HD + r : HD + r + HDIM] = dot(q, gs, NT)
    pg[2 * HD + r : 2 * HD + r + HDIM] = dot(g, p.astype(BF), NT)


def space_forward_kernel(
    u_hbm, c_hbm, wq_hbm, wo_hbm,
    out_hbm, probs_hbm, pts_hbm, mine_hbm, theirs_hbm,
    pt, at, u_ref, wq, wo, t, perm, so, probs, pts, mine, theirs, sems,
):
    pairs = [(u_hbm, u_ref)]
    for i in range(3):
        rows = pl.ds(i * HD, HD)
        pairs.append((wq_hbm.at[rows], wq.at[rows]))
    pairs += [(wo_hbm, wo), (c_hbm, out_hbm.at[:, pl.ds(POS, POS)])]
    pairs += [(so, out_hbm.at[:, pl.ds(0, POS)]), (probs, probs_hbm), (pts, pts_hbm)]
    pairs += [(mine, mine_hbm), (theirs, theirs_hbm)]
    copies = [pltpu.make_async_copy(x, y, sems.at[i]) for i, (x, y) in enumerate(pairs)]
    for i in range(4):
        copies[i].start()
    copies[0].wait()
    u = u_ref[...].astype(F32)
    normed, _ = norm_rows(u)
    hidden = normed.astype(BF)
    lay_rows(mine, theirs, 0, hidden.astype(F32), t, perm)
    for i in range(3):
        copies[1 + i].wait()
        if i == 0:
            copies[4].start()
            copies[5].start()
        pt[i * HD : (i + 1) * HD] = rounded(dot(wq[i * HD : (i + 1) * HD], hidden, NT))
    pts[...] = pt[...].astype(BF)
    copies[8].start()
    attend(pt, at, probs, None)
    copies[7].start()
    a = at[...].astype(BF)
    mine[576:1152] = a
    theirs[576:1152] = a
    copies[9].start()
    copies[10].start()
    copies[4].wait()
    sums = (u + dot(a, wo[...], TN)).astype(BF)
    for i in range(8):
        so[i] = sums[i * POS : (i + 1) * POS]
    copies[6].start()
    for i in (5, 7, 8, 9, 10, 6):
        copies[i].wait()


def time_kernel(x_ref, wq, wo, me, te, mid, mine, theirs, pt, at, ga, pg, probs, u_ref, c_ref, t, perm):
    for i in range(8):
        u_ref[i * POS : (i + 1) * POS] = x_ref[i, 0:POS]
        c_ref[i * POS : (i + 1) * POS] = x_ref[i, POS : 2 * POS]
    c = c_ref[...]
    normed, inverse = norm_rows(u_ref[...].astype(F32))
    pt[...] = rounded(dot(wq[...], normed.astype(BF), NT))
    ga[...] = rounded(dot(wo[...], c, NT))
    row = lax.broadcasted_iota(jnp.int32, (S, S), 0)
    col = lax.broadcasted_iota(jnp.int32, (S, S), 1)
    attend(pt, at, probs, (row % POS) == (col % POS))
    for h in range(HEADS):
        attend_grad(pt, ga, probs[h], h, pg)
    g = pg[...].astype(BF)
    grad = dot(g, wq[...], TN)
    mid[...] = norm_grad(c.astype(F32), grad, normed, inverse).astype(BF)
    lay_rows(mine, theirs, 0, rounded(normed), t, perm)
    lay_rows(mine, theirs, 576, c.astype(F32), t, perm)
    a = at[...].astype(BF)
    for out in (mine, theirs):
        out[1152:2880] = g
        out[2880:3456] = a
    mine[3456:4608] = me[...]
    theirs[3456:4608] = te[...]


def space_attention_grad_kernel(c_ref, probs, pts, wo, mine, theirs, pt, ga, pg, t, perm):
    c = c_ref[...]
    ga[...] = rounded(dot(wo[...], c, NT))
    pt[...] = pts[...].astype(F32)
    for h in range(HEADS):
        attend_grad(pt, ga, probs[h], h, pg)
    g = pg[...].astype(BF)
    lay_rows(mine, theirs, 0, c.astype(F32), t, perm)
    for out in (mine, theirs):
        out[576:2304] = g


def in_grad_kernel(c_ref, u_ref, g_ref, wq, in_grad):
    grad = dot(g_ref[576:2304], wq[...], TN)
    normed, inverse = norm_rows(u_ref[...].astype(F32))
    in_grad[...] = norm_grad(c_ref[...].astype(F32), grad, normed, inverse).astype(BF)


def spread(x, t, perm):
    t[...] = x.T
    for own in range(2):

        @pl.when(lax.axis_index("zl") == own)
        def _():
            for core in range(2):
                for y in range(4):
                    for half in range(2):
                        for z in range(4):
                            src = ROWS * (z * 8 + y * 2 + core) + HALF * (half ^ own)
                            dst = 576 * core + 144 * y + 72 * half + HALF * z
                            perm[dst : dst + HALF] = t[src : src + HALF]


def lay_rows(mine, theirs, base, x, t, perm):
    spread(x, t, perm)
    core = lax.axis_index("core")
    for out, half in ((mine, core), (theirs, 1 - core)):
        rows = perm[pl.ds(pl.multiple_of(half * 576, 576), 576)]
        out[base : base + 576] = rows.astype(BF)


def quarter(axis, h, p):
    me, core = lax.axis_index(axis), lax.axis_index("core")
    a = (me // 2 + (h * core + p * (1 - core))) % 2
    b = ((me + 1) // 2 + (h * (1 - core) + p * core)) % 2
    return 2 * a + (a + b) % 2


def bits(i):
    core = lax.axis_index("core")
    a, b = i // 2, ((i + 1) // 2) % 2
    return a * core + b * (1 - core), a * (1 - core) + b * core


PAIRS = ([[0, 1], [3, 2]], [[0, 3], [1, 2]])
BITS = [(h, p) for h in range(2) for p in range(2)]


STREAMS = {"xt": (0, 0), "ct": (0, 576), "xs": (0, 3456), "cs": (1, 0)}
SEGMENTS = (
    (("xt", 0, 1152, 432, 0, 384),),
    (("xt", 0, 1152, 432, 384, 48), ("ct", 0, 2880, 144, 0, 144), ("xs", 1, 576, 432, 0, 192)),
    (("xs", 1, 576, 432, 192, 240), ("cs", 0, 4032, 144, 0, 144)),
)


def product_kernel(piece, *refs):
    *factors, keep, send, left = refs
    pairs = [factors[i : i + 2] for i in range(0, len(factors), 2)]
    for k, (stream, *_) in enumerate(SEGMENTS[piece]):
        which, first = STREAMS[stream]
        for i, (hy, py) in enumerate(BITS):
            rows = pl.ds(pl.multiple_of(quarter("y", hy, py) * 144 + first, 144), 144)
            for j, ref in enumerate(pairs[which]):
                left[k, i * 144 : (i + 1) * 144, j * S : (j + 1) * S] = ref[rows]
    for hx, px in BITS:
        q = quarter("x", hx, px)
        parts = []
        for k, (_, which, first, n, start, count) in enumerate(SEGMENTS[piece]):
            rows = pl.ds(pl.multiple_of(first + start + q * n, 16), count)
            right = jnp.concatenate([ref[rows] for ref in pairs[which]], axis=1)
            parts.append(dot(left[k], right, NT))
        both = jnp.concatenate(parts, axis=1)
        for i, (hy, py) in enumerate(BITS):
            for hz in range(2):
                r = 144 * i + 72 * hz
                one, two, three = ((hx, hy, hz), (hy, hz, hx), (hz, hx, hy))[piece]
                out = send if one else keep
                out[two, three, px * 2 + py] = both[r : r + 72].astype(out.dtype)


def halve_kernel(k_ref, g_ref, keep, send):
    for i, out in enumerate((keep, send)):
        out[...] = (k_ref[i].astype(F32) + g_ref[i].astype(F32)).astype(out.dtype)


def join_kernel(*refs):
    keep, got, out = refs[:3], refs[3:6], refs[6]
    own_x, own_y = bits(lax.axis_index("x"))[1], bits(lax.axis_index("y"))[1]
    for px in range(2):
        for py in range(2):
            place = ((own_x + px) % 2) * 2 + (own_y + py) % 2
            i = px * 2 + py
            accs = [k[i] + g[i].astype(F32) for k, g in zip(keep, got)]
            for z in range(4):
                h, p = bits(z)
                rows = slice(HALF * z, HALF * (z + 1))
                tiles = [acc[rows, S * j : S * (j + 1)] for acc in accs for j in range(3)]
                tiles.append(jnp.zeros((14, S), F32))
                to = pl.ds(pl.multiple_of(p * 176, 176), 176)
                out[place * 2 + h, to] = jnp.concatenate(tiles, axis=0).astype(BF)


def second_sum_kernel(x_ref, keep, send):
    own = bits(lax.axis_index("zh"))[1]
    for i, out in enumerate((keep, send)):
        rows = pl.ds(pl.multiple_of((own + i) % 2 * 176, 176), 176)
        acc = x_ref[0, rows].astype(F32)
        for j in range(1, 8):
            acc = acc + x_ref[j, rows].astype(F32)
        out[...] = acc[0:162].astype(out.dtype)


def copies_kernel(k_ref, g_ref, out):
    acc = (k_ref[...] + g_ref[...].astype(F32)).astype(BF)
    for i in range(8):
        out[i] = acc


def last_kernel(x_ref, qt, ot, qs, os):
    for half in range(2):
        parts = []
        for x in range(4):
            p = x_ref[half * 4 + x].astype(F32)
            parts.append(jnp.concatenate([p[HALF * i : HALF * (i + 1)] for i in range(9)], axis=1))
        rows = pl.ds(HALF * half, HALF)
        for base, qkv, proj in ((0, qt, ot), (HD, qs, os)):
            qkv[rows] = jnp.concatenate([p[:, base : base + 432] for p in parts], axis=1)
            proj[rows] = jnp.concatenate([p[:, base + 432 : base + HD] for p in parts], axis=1)


def swap(x, axes, groups=None):
    return lax.all_to_all(
        x, axes, split_axis=0, concat_axis=0, axis_index_groups=groups, tiled=True
    )


DSP = ("zl", "x")


def ring(x, axis):
    pairs = [(i * 2 + c, j * 2 + c) for c in range(2) for p in PAIRS[c] for i, j in (p, p[::-1])]
    return lax.ppermute(x, (axis, "core"), pairs)


def pair_z(x):
    pairs = []
    for z in range(8):
        for c in range(2):
            up = (z % 2 == 0) == (c == 0)
            to = (z + (1 if up else 7)) % 8
            pairs.append((((z % 2) * 4 + z // 2) * 2 + c, ((to % 2) * 4 + to // 2) * 2 + c))
    return lax.ppermute(x, ("zl", "zh", "core"), pairs)


STEPS = (lambda x: ring(x, "x"), lambda x: ring(x, "y"), pair_z)


def wide_cubes():
    return [
        [((x * 4 + z) * 4 + y) * 2 + core for x in gx for y in gy for z in gz]
        for core in range(2)
        for gx in PAIRS[1 - core]
        for gy in PAIRS[1 - core]
        for gz in PAIRS[core]
    ]


def last_pair(x):
    pairs = []
    for core in range(2):
        for i, j in PAIRS[1 - core]:
            pairs += [(i * 2 + core, j * 2 + core), (j * 2 + core, i * 2 + core)]
    return lax.ppermute(x, ("zh", "core"), pairs)


def to_other_core(x):
    return lax.ppermute(x, "core", [(0, 1), (1, 0)])


def local(latents, out_grad, wqs, wos, wqt, wot):
    u = latents[0, 0]
    wqs, wos, wqt, wot = wqs.T, wos.T, wqt.T, wot.T
    wide, thin, square = ((3 * HD, S), F32), ((HD, S), F32), ((HEADS, S, S), F32)
    full, flipped, factors = ((S, D), BF), ((D, S), F32), [((4608, S), BF)] * 2
    dense = 2 * S * D * 4 * HD
    early = [((1152, S), BF)] * 2
    late = [((2304, S), BF)] * 2
    sent, probs, pts, mine_e, theirs_e = call(
        space_forward_kernel,
        [((8, 2 * POS, D), BF), square, ((3 * HD, S), BF)] + early,
        (u, out_grad.reshape(8, POS, D), wqs, wos),
        [wide, thin, full, ((3 * HD, D), BF), ((HD, D), BF), flipped, flipped]
        + [((8, POS, D), BF), square, ((3 * HD, S), BF)]
        + early,
        flops=dense,
        limit=56,
        hbm=(0, 1, 2, 3),
        far=True,
    )
    mid, mine_e, theirs_e = call(
        time_kernel,
        [full] + factors,
        (swap(sent, DSP), wqt, wot, mine_e, theirs_e),
        [wide, thin, thin, wide, square, full, full, flipped, flipped],
        flops=2 * dense,
    )
    mid = swap(mid.reshape(8, POS, D), DSP).reshape(S, D)
    mid, theirs_e = lax.optimization_barrier((mid, theirs_e))
    theirs_e = to_other_core(theirs_e)
    mine_l, theirs_l = call(
        space_attention_grad_kernel,
        late,
        (mid, probs, pts, wos),
        [wide, thin, wide, flipped, flipped],
        flops=dense // 4,
    )
    theirs_l = to_other_core(theirs_l)
    (in_grad,) = call(in_grad_kernel, [full], (mid, u, mine_l, wqs), flops=dense)

    def product(piece, *pairs):
        return call(
            functools.partial(product_kernel, piece),
            [((2, 2, 4, 72, PIECE), BF)] * 2,
            pairs,
            [((len(SEGMENTS[piece]), 576, 2 * S), BF)],
            flops=2 * HD * 256 * 4 * PIECE,
        )

    early = (mine_e, theirs_e)
    keep, send = product(0, *early)
    keep, theirs_l = lax.optimization_barrier((keep, theirs_l))
    pairs = (*early, mine_l, theirs_l)
    halves = [(keep, send), product(1, *pairs), product(2, *pairs)]
    got = [STEPS[i](send) for i, (_, send) in enumerate(halves)]
    in_grad, got[2] = lax.optimization_barrier((in_grad, got[2]))
    for step in (1, 2):
        shape = ((2, 4, 72, PIECE), (4, 72, PIECE))[step - 1]
        halves = [
            call(halve_kernel, [(shape, F32), (shape, BF)], (h[0], g)) for h, g in zip(halves, got)
        ]
        got = [STEPS[(i + step) % 3](send) for i, (_, send) in enumerate(halves)]
    (terms,) = call(join_kernel, [((8, 352, S), BF)], ([h[0] for h in halves] + got))
    terms = swap(terms, ("x", "zh", "y", "core"), wide_cubes())
    keep, send = call(second_sum_kernel, [((162, S), F32), ((162, S), BF)], (terms,))
    (copies,) = call(copies_kernel, [((8, 162, S), BF)], (keep, last_pair(send)))
    copies = swap(copies, DSP)
    gqt, got, gqs, gos = call(
        last_kernel, [((ROWS, 3 * HD), F32), ((ROWS, HD), F32)] * 2, (copies,)
    )
    return in_grad[None, None], gqs, gos, gqt, got


def solution(mesh):
    fine = Mesh(mesh.devices.reshape(2, 4, 4, 4, 2), ("zl", "x", "zh", "y", "core"))
    dp = ("zh", "y", "core")
    act = P(dp, ("zl", "x"), None, None)
    in_specs = (act, act, P(), P(), P(), P())
    out_specs = (act, P(dp, None), P(dp, None), P(dp, None), P(dp, None))
    return jax.shard_map(local, mesh=fine, in_specs=in_specs, out_specs=out_specs, check_vma=False)
```

```python
import functools

import jax
import jax.numpy as jnp
from jax import lax
from jax.experimental import pallas as pl
from jax.experimental.pallas import tpu as pltpu
from jax.sharding import Mesh, PartitionSpec as P

D = 1152
HEADS = 8
HDIM = 72
HD = 576
S = 128
POS = 16
ROWS = 36
HALF = 18
PIECE = 384
PIECE = 384
SCALE = HDIM ** (-0.5)
EPS = 1e-06
BF = jnp.bfloat16
F32 = jnp.float32
MIB = 1024 * 1024

NN = (((1,), (0,)), ((), ()))
NT = (((1,), (1,)), ((), ()))
TN = (((0,), (0,)), ((), ()))


def dot(a, b, dims=NN):
    return lax.dot_general(a, b, dims, preferred_element_type=F32)


def norm_rows(u):
    centred = u - jnp.mean(u, axis=-1, keepdims=True)
    inverse = lax.rsqrt(jnp.mean(centred * centred, axis=-1, keepdims=True) + EPS)
    return centred * inverse, inverse


def norm_grad(c, g, normed, inverse):
    mean_g = jnp.mean(g, axis=-1, keepdims=True)
    mean_x = jnp.mean(g * normed, axis=-1, keepdims=True)
    return c + inverse * (g - mean_g - normed * mean_x)


def rounded(x):
    return x.astype(BF).astype(F32)


def call(kernel, outs, args, scratch=(), flops=0, limit=24, hbm=(), far=False):
    vmem = pl.BlockSpec(memory_space=pltpu.VMEM)
    away = pl.BlockSpec(memory_space=pltpu.HBM)
    moved = 2 * sum(x.size * x.dtype.itemsize for x in args)
    return pl.pallas_call(
        kernel,
        out_shape=[jax.ShapeDtypeStruct(s, t) for s, t in outs],
        in_specs=[away if i in hbm else vmem for i in range(len(args))],
        out_specs=[away if far else vmem] * len(outs),
        scratch_shapes=[pltpu.VMEM(s, t) for s, t in scratch]
        + ([pltpu.SemaphoreType.DMA((11,))] if hbm else []),
        compiler_params=pltpu.CompilerParams(vmem_limit_bytes=limit * MIB),
        cost_estimate=pl.CostEstimate(flops=flops, bytes_accessed=moved, transcendentals=0),
    )(*args)


def head(ref, part, h):
    r = part * HD + h * HDIM
    return ref[r : r + HDIM].astype(BF)


def probabilities(pt, h, mask):
    s = dot(head(pt, 1, h), head(pt, 0, h), TN) * SCALE
    if mask is not None:
        s = jnp.where(mask, s, -1e30)
    e = jnp.exp(s - jnp.max(s, axis=0, keepdims=True))
    return e / jnp.sum(e, axis=0, keepdims=True)


def attend(pt, at, probs, mask):
    for h in range(HEADS):
        p = probabilities(pt, h, mask)
        probs[h] = p
        at[h * HDIM : (h + 1) * HDIM] = dot(head(pt, 2, h), p.astype(BF))


def attend_grad(pt, ga, p, h, pg):
    q, k, v, g = head(pt, 0, h), head(pt, 1, h), head(pt, 2, h), head(ga, 0, h)
    gp = dot(v, g, TN)
    gs = (p * (gp - jnp.sum(p * gp, axis=0, keepdims=True)) * SCALE).astype(BF)
    r = h * HDIM
    pg[r : r + HDIM] = dot(k, gs)
    pg[HD + r : HD + r + HDIM] = dot(q, gs, NT)
    pg[2 * HD + r : 2 * HD + r + HDIM] = dot(g, p.astype(BF), NT)


def space_forward_kernel(
    u_hbm, c_hbm, wq_hbm, wo_hbm,
    out_hbm, probs_hbm, pts_hbm, mine_hbm, theirs_hbm,
    pt, at, u_ref, wq, wo, t, perm, so, probs, pts, mine, theirs, sems,
):
    pairs = [(u_hbm, u_ref)]
    for i in range(3):
        rows = pl.ds(i * HD, HD)
        pairs.append((wq_hbm.at[rows], wq.at[rows]))
    pairs += [(wo_hbm, wo), (c_hbm, so.at[:, pl.ds(POS, POS)])]
    pairs += [(so, out_hbm), (probs, probs_hbm), (pts, pts_hbm)]
    pairs += [(mine, mine_hbm), (theirs, theirs_hbm)]
    copies = [pltpu.make_async_copy(x, y, sems.at[i]) for i, (x, y) in enumerate(pairs)]
    for i in range(4):
        copies[i].start()
    copies[0].wait()
    u = u_ref[...].astype(F32)
    normed, _ = norm_rows(u)
    hidden = normed.astype(BF)
    lay_rows(mine, theirs, 0, hidden.astype(F32), t, perm)
    for i in range(3):
        copies[1 + i].wait()
        if i == 0:
            copies[4].start()
            copies[5].start()
        pt[i * HD : (i + 1) * HD] = rounded(dot(wq[i * HD : (i + 1) * HD], hidden, NT))
    pts[...] = pt[...].astype(BF)
    copies[8].start()
    attend(pt, at, probs, None)
    copies[7].start()
    a = at[...].astype(BF)
    mine[576:1152] = a
    theirs[576:1152] = a
    copies[9].start()
    copies[10].start()
    copies[4].wait()
    sums = (u + dot(a, wo[...], TN)).astype(BF)
    for i in range(8):
        so[i, 0:POS] = sums[i * POS : (i + 1) * POS]
    copies[5].wait()
    copies[6].start()
    for i in (7, 8, 9, 10, 6):
        copies[i].wait()


def time_kernel(x_ref, wq, wo, me, te, mid, mine, theirs, pt, at, ga, pg, probs, u_ref, c_ref, t, perm):
    for i in range(8):
        u_ref[i * POS : (i + 1) * POS] = x_ref[i, 0:POS]
        c_ref[i * POS : (i + 1) * POS] = x_ref[i, POS : 2 * POS]
    c = c_ref[...]
    normed, inverse = norm_rows(u_ref[...].astype(F32))
    pt[...] = rounded(dot(wq[...], normed.astype(BF), NT))
    ga[...] = rounded(dot(wo[...], c, NT))
    row = lax.broadcasted_iota(jnp.int32, (S, S), 0)
    col = lax.broadcasted_iota(jnp.int32, (S, S), 1)
    attend(pt, at, probs, (row % POS) == (col % POS))
    for h in range(HEADS):
        attend_grad(pt, ga, probs[h], h, pg)
    g = pg[...].astype(BF)
    grad = dot(g, wq[...], TN)
    mid[...] = norm_grad(c.astype(F32), grad, normed, inverse).astype(BF)
    lay_rows(mine, theirs, 0, rounded(normed), t, perm)
    lay_rows(mine, theirs, 576, c.astype(F32), t, perm)
    a = at[...].astype(BF)
    for out in (mine, theirs):
        out[1152:2880] = g
        out[2880:3456] = a
    mine[3456:4608] = me[...]
    theirs[3456:4608] = te[...]


def space_attention_grad_kernel(c_ref, probs, pts, wo, mine, theirs, pt, ga, pg, t, perm):
    c = c_ref[...]
    ga[...] = rounded(dot(wo[...], c, NT))
    pt[...] = pts[...].astype(F32)
    for h in range(HEADS):
        attend_grad(pt, ga, probs[h], h, pg)
    g = pg[...].astype(BF)
    lay_rows(mine, theirs, 0, c.astype(F32), t, perm)
    for out in (mine, theirs):
        out[576:2304] = g


def in_grad_kernel(c_ref, u_ref, g_ref, wq, in_grad):
    grad = dot(g_ref[576:2304], wq[...], TN)
    normed, inverse = norm_rows(u_ref[...].astype(F32))
    in_grad[...] = norm_grad(c_ref[...].astype(F32), grad, normed, inverse).astype(BF)


def spread(x, t, perm):
    t[...] = x.T
    for own in range(2):

        @pl.when(lax.axis_index("zl") == own)
        def _():
            for core in range(2):
                for y in range(4):
                    for half in range(2):
                        for z in range(4):
                            src = ROWS * (z * 8 + y * 2 + core) + HALF * (half ^ own)
                            dst = 576 * core + 144 * y + 72 * half + HALF * z
                            perm[dst : dst + HALF] = t[src : src + HALF]


def lay_rows(mine, theirs, base, x, t, perm):
    spread(x, t, perm)
    core = lax.axis_index("core")
    for out, half in ((mine, core), (theirs, 1 - core)):
        rows = perm[pl.ds(pl.multiple_of(half * 576, 576), 576)]
        out[base : base + 576] = rows.astype(BF)


def quarter(axis, h, p):
    me, core = lax.axis_index(axis), lax.axis_index("core")
    a = (me // 2 + (h * core + p * (1 - core))) % 2
    b = ((me + 1) // 2 + (h * (1 - core) + p * core)) % 2
    return 2 * a + (a + b) % 2


def bits(i):
    core = lax.axis_index("core")
    a, b = i // 2, ((i + 1) // 2) % 2
    return a * core + b * (1 - core), a * (1 - core) + b * core


PAIRS = ([[0, 1], [3, 2]], [[0, 3], [1, 2]])
BITS = [(h, p) for h in range(2) for p in range(2)]


STREAMS = {"xt": (0, 0), "ct": (0, 576), "xs": (0, 3456), "cs": (1, 0)}
SEGMENTS = (
    (("xt", 0, 1152, 432, 0, 384),),
    (("xt", 0, 1152, 432, 384, 48), ("ct", 0, 2880, 144, 0, 144), ("xs", 1, 576, 432, 0, 192)),
    (("xs", 1, 576, 432, 192, 240), ("cs", 0, 4032, 144, 0, 144)),
)


def product_kernel(piece, *refs):
    *factors, keep, send, left = refs
    pairs = [factors[i : i + 2] for i in range(0, len(factors), 2)]
    for k, (stream, *_) in enumerate(SEGMENTS[piece]):
        which, first = STREAMS[stream]
        for i, (hy, py) in enumerate(BITS):
            rows = pl.ds(pl.multiple_of(quarter("y", hy, py) * 144 + first, 144), 144)
            for j, ref in enumerate(pairs[which]):
                left[k, i * 144 : (i + 1) * 144, j * S : (j + 1) * S] = ref[rows]
    for hx, px in BITS:
        q = quarter("x", hx, px)
        parts = []
        for k, (_, which, first, n, start, count) in enumerate(SEGMENTS[piece]):
            rows = pl.ds(pl.multiple_of(first + start + q * n, 16), count)
            right = jnp.concatenate([ref[rows] for ref in pairs[which]], axis=1)
            parts.append(dot(left[k], right, NT))
        both = jnp.concatenate(parts, axis=1)
        for i, (hy, py) in enumerate(BITS):
            for hz in range(2):
                r = 144 * i + 72 * hz
                one, two, three = ((hx, hy, hz), (hy, hz, hx), (hz, hx, hy))[piece]
                out = send if one else keep
                out[two, three, px * 2 + py] = both[r : r + 72].astype(out.dtype)


def halve_kernel(k_ref, g_ref, keep, send):
    for i, out in enumerate((keep, send)):
        out[...] = (k_ref[i].astype(F32) + g_ref[i].astype(F32)).astype(out.dtype)


def join_kernel(*refs):
    keep, got, out = refs[:3], refs[3:6], refs[6]
    own_x, own_y = bits(lax.axis_index("x"))[1], bits(lax.axis_index("y"))[1]
    for px in range(2):
        for py in range(2):
            place = ((own_x + px) % 2) * 2 + (own_y + py) % 2
            i = px * 2 + py
            accs = [k[i] + g[i].astype(F32) for k, g in zip(keep, got)]
            for z in range(4):
                h, p = bits(z)
                rows = slice(HALF * z, HALF * (z + 1))
                tiles = [acc[rows, S * j : S * (j + 1)] for acc in accs for j in range(3)]
                tiles.append(jnp.zeros((14, S), F32))
                to = pl.ds(pl.multiple_of(p * 176, 176), 176)
                out[place * 2 + h, to] = jnp.concatenate(tiles, axis=0).astype(BF)


def second_sum_kernel(x_ref, keep, send):
    own = bits(lax.axis_index("zh"))[1]
    for i, out in enumerate((keep, send)):
        rows = pl.ds(pl.multiple_of((own + i) % 2 * 176, 176), 176)
        acc = x_ref[0, rows].astype(F32)
        for j in range(1, 8):
            acc = acc + x_ref[j, rows].astype(F32)
        out[...] = acc[0:162].astype(out.dtype)


def copies_kernel(k_ref, g_ref, out):
    acc = (k_ref[...] + g_ref[...].astype(F32)).astype(BF)
    for i in range(8):
        out[i] = acc


def last_kernel(x_ref, qt, ot, qs, os):
    for half in range(2):
        parts = []
        for x in range(4):
            p = x_ref[half * 4 + x].astype(F32)
            parts.append(jnp.concatenate([p[HALF * i : HALF * (i + 1)] for i in range(9)], axis=1))
        rows = pl.ds(HALF * half, HALF)
        for base, qkv, proj in ((0, qt, ot), (HD, qs, os)):
            qkv[rows] = jnp.concatenate([p[:, base : base + 432] for p in parts], axis=1)
            proj[rows] = jnp.concatenate([p[:, base + 432 : base + HD] for p in parts], axis=1)


def swap(x, axes, groups=None):
    return lax.all_to_all(
        x, axes, split_axis=0, concat_axis=0, axis_index_groups=groups, tiled=True
    )


DSP = ("zl", "x")


def ring(x, axis):
    pairs = [(i * 2 + c, j * 2 + c) for c in range(2) for p in PAIRS[c] for i, j in (p, p[::-1])]
    return lax.ppermute(x, (axis, "core"), pairs)


def pair_z(x):
    pairs = []
    for z in range(8):
        for c in range(2):
            up = (z % 2 == 0) == (c == 0)
            to = (z + (1 if up else 7)) % 8
            pairs.append((((z % 2) * 4 + z // 2) * 2 + c, ((to % 2) * 4 + to // 2) * 2 + c))
    return lax.ppermute(x, ("zl", "zh", "core"), pairs)


STEPS = (lambda x: ring(x, "x"), lambda x: ring(x, "y"), pair_z)


def wide_cubes():
    return [
        [((x * 4 + z) * 4 + y) * 2 + core for x in gx for y in gy for z in gz]
        for core in range(2)
        for gx in PAIRS[1 - core]
        for gy in PAIRS[1 - core]
        for gz in PAIRS[core]
    ]


def last_pair(x):
    pairs = []
    for core in range(2):
        for i, j in PAIRS[1 - core]:
            pairs += [(i * 2 + core, j * 2 + core), (j * 2 + core, i * 2 + core)]
    return lax.ppermute(x, ("zh", "core"), pairs)


def to_other_core(x):
    return lax.ppermute(x, "core", [(0, 1), (1, 0)])


def local(latents, out_grad, wqs, wos, wqt, wot):
    u = latents[0, 0]
    wqs, wos, wqt, wot = wqs.T, wos.T, wqt.T, wot.T
    wide, thin, square = ((3 * HD, S), F32), ((HD, S), F32), ((HEADS, S, S), F32)
    full, flipped, factors = ((S, D), BF), ((D, S), F32), [((4608, S), BF)] * 2
    dense = 2 * S * D * 4 * HD
    early = [((1152, S), BF)] * 2
    late = [((2304, S), BF)] * 2
    sent, probs, pts, mine_e, theirs_e = call(
        space_forward_kernel,
        [((8, 2 * POS, D), BF), square, ((3 * HD, S), BF)] + early,
        (u, out_grad.reshape(8, POS, D), wqs, wos),
        [wide, thin, full, ((3 * HD, D), BF), ((HD, D), BF), flipped, flipped]
        + [((8, 2 * POS, D), BF), square, ((3 * HD, S), BF)]
        + early,
        flops=dense,
        limit=56,
        hbm=(0, 1, 2, 3),
        far=True,
    )
    mid, mine_e, theirs_e = call(
        time_kernel,
        [full] + factors,
        (swap(sent, DSP), wqt, wot, mine_e, theirs_e),
        [wide, thin, thin, wide, square, full, full, flipped, flipped],
        flops=2 * dense,
    )
    mid = swap(mid.reshape(8, POS, D), DSP).reshape(S, D)
    mid, theirs_e = lax.optimization_barrier((mid, theirs_e))
    theirs_e = to_other_core(theirs_e)
    mine_l, theirs_l = call(
        space_attention_grad_kernel,
        late,
        (mid, probs, pts, wos),
        [wide, thin, wide, flipped, flipped],
        flops=dense // 4,
    )
    theirs_l = to_other_core(theirs_l)
    (in_grad,) = call(in_grad_kernel, [full], (mid, u, mine_l, wqs), flops=dense)

    def product(piece, *pairs):
        return call(
            functools.partial(product_kernel, piece),
            [((2, 2, 4, 72, PIECE), BF)] * 2,
            pairs,
            [((len(SEGMENTS[piece]), 576, 2 * S), BF)],
            flops=2 * HD * 256 * 4 * PIECE,
        )

    early = (mine_e, theirs_e)
    keep, send = product(0, *early)
    keep, theirs_l = lax.optimization_barrier((keep, theirs_l))
    pairs = (*early, mine_l, theirs_l)
    halves = [(keep, send), product(1, *pairs), product(2, *pairs)]
    got = [STEPS[i](send) for i, (_, send) in enumerate(halves)]
    in_grad, got[2] = lax.optimization_barrier((in_grad, got[2]))
    for step in (1, 2):
        shape = ((2, 4, 72, PIECE), (4, 72, PIECE))[step - 1]
        halves = [
            call(halve_kernel, [(shape, F32), (shape, BF)], (h[0], g)) for h, g in zip(halves, got)
        ]
        got = [STEPS[(i + step) % 3](send) for i, (_, send) in enumerate(halves)]
    (terms,) = call(join_kernel, [((8, 352, S), BF)], ([h[0] for h in halves] + got))
    terms = swap(terms, ("x", "zh", "y", "core"), wide_cubes())
    keep, send = call(second_sum_kernel, [((162, S), F32), ((162, S), BF)], (terms,))
    (copies,) = call(copies_kernel, [((8, 162, S), BF)], (keep, last_pair(send)))
    copies = swap(copies, DSP)
    gqt, got, gqs, gos = call(
        last_kernel, [((ROWS, 3 * HD), F32), ((ROWS, HD), F32)] * 2, (copies,)
    )
    return in_grad[None, None], gqs, gos, gqt, got


def solution(mesh):
    fine = Mesh(mesh.devices.reshape(2, 4, 4, 4, 2), ("zl", "x", "zh", "y", "core"))
    dp = ("zh", "y", "core")
    act = P(dp, ("zl", "x"), None, None)
    in_specs = (act, act, P(), P(), P(), P())
    out_specs = (act, P(dp, None), P(dp, None), P(dp, None), P(dp, None))
    return jax.shard_map(local, mesh=fine, in_specs=in_specs, out_specs=out_specs, check_vma=False)
```

```python
import functools

import jax
import jax.numpy as jnp
from jax import lax
from jax.experimental import pallas as pl
from jax.experimental.pallas import tpu as pltpu
from jax.sharding import Mesh, PartitionSpec as P

D = 1152
HEADS = 8
HDIM = 72
HD = 576
S = 128
POS = 16
ROWS = 36
HALF = 18
PIECE = 384
PIECE = 384
SCALE = HDIM ** (-0.5)
EPS = 1e-06
BF = jnp.bfloat16
F32 = jnp.float32
MIB = 1024 * 1024

NN = (((1,), (0,)), ((), ()))
NT = (((1,), (1,)), ((), ()))
TN = (((0,), (0,)), ((), ()))


def dot(a, b, dims=NN):
    return lax.dot_general(a, b, dims, preferred_element_type=F32)


def norm_rows(u):
    centred = u - jnp.mean(u, axis=-1, keepdims=True)
    inverse = lax.rsqrt(jnp.mean(centred * centred, axis=-1, keepdims=True) + EPS)
    return centred * inverse, inverse


def norm_grad(c, g, normed, inverse):
    mean_g = jnp.mean(g, axis=-1, keepdims=True)
    mean_x = jnp.mean(g * normed, axis=-1, keepdims=True)
    return c + inverse * (g - mean_g - normed * mean_x)


def rounded(x):
    return x.astype(BF).astype(F32)


def call(kernel, outs, args, scratch=(), flops=0, limit=24, hbm=(), far=False):
    vmem = pl.BlockSpec(memory_space=pltpu.VMEM)
    away = pl.BlockSpec(memory_space=pltpu.HBM)
    moved = 2 * sum(x.size * x.dtype.itemsize for x in args)
    return pl.pallas_call(
        kernel,
        out_shape=[jax.ShapeDtypeStruct(s, t) for s, t in outs],
        in_specs=[away if i in hbm else vmem for i in range(len(args))],
        out_specs=[away if far else vmem] * len(outs),
        scratch_shapes=[pltpu.VMEM(s, t) for s, t in scratch]
        + ([pltpu.SemaphoreType.DMA((11,))] if hbm else []),
        compiler_params=pltpu.CompilerParams(vmem_limit_bytes=limit * MIB),
        cost_estimate=pl.CostEstimate(flops=flops, bytes_accessed=moved, transcendentals=0),
    )(*args)


def head(ref, part, h):
    r = part * HD + h * HDIM
    return ref[r : r + HDIM].astype(BF)


def probabilities(pt, h, mask):
    s = dot(head(pt, 1, h), head(pt, 0, h), TN) * SCALE
    if mask is not None:
        s = jnp.where(mask, s, -1e30)
    e = jnp.exp(s - jnp.max(s, axis=0, keepdims=True))
    return e / jnp.sum(e, axis=0, keepdims=True)


def attend(pt, at, probs, mask):
    for h in range(HEADS):
        p = probabilities(pt, h, mask)
        probs[h] = p
        at[h * HDIM : (h + 1) * HDIM] = dot(head(pt, 2, h), p.astype(BF))


def attend_grad(pt, ga, p, h, pg):
    q, k, v, g = head(pt, 0, h), head(pt, 1, h), head(pt, 2, h), head(ga, 0, h)
    gp = dot(v, g, TN)
    gs = (p * (gp - jnp.sum(p * gp, axis=0, keepdims=True)) * SCALE).astype(BF)
    r = h * HDIM
    pg[r : r + HDIM] = dot(k, gs)
    pg[HD + r : HD + r + HDIM] = dot(q, gs, NT)
    pg[2 * HD + r : 2 * HD + r + HDIM] = dot(g, p.astype(BF), NT)


def space_forward_kernel(
    u_hbm, c_hbm, wq_hbm, wo_hbm,
    out_hbm, probs_hbm, pts_hbm, mine_hbm, theirs_hbm,
    pt, at, u_ref, wq, wo, t, perm, so, probs, pts, mine, theirs, sems,
):
    pairs = [(u_hbm, u_ref)]
    for i in range(3):
        rows = pl.ds(i * HD, HD)
        pairs.append((wq_hbm.at[rows], wq.at[rows]))
    pairs += [(wo_hbm, wo), (c_hbm, so.at[:, pl.ds(POS, POS)])]
    pairs += [(so, out_hbm), (probs, probs_hbm), (pts, pts_hbm)]
    pairs += [(mine, mine_hbm), (theirs, theirs_hbm)]
    copies = [pltpu.make_async_copy(x, y, sems.at[i]) for i, (x, y) in enumerate(pairs)]
    for i in range(4):
        copies[i].start()
    copies[0].wait()
    u = u_ref[...].astype(F32)
    normed, _ = norm_rows(u)
    hidden = normed.astype(BF)
    lay_rows(mine, theirs, 0, hidden.astype(F32), t, perm)
    for i in range(3):
        copies[1 + i].wait()
        if i == 0:
            copies[4].start()
            copies[5].start()
        pt[i * HD : (i + 1) * HD] = rounded(dot(wq[i * HD : (i + 1) * HD], hidden, NT))
    pts[...] = pt[...].astype(BF)
    copies[8].start()
    attend(pt, at, probs, None)
    copies[7].start()
    a = at[...].astype(BF)
    mine[576:1152] = a
    theirs[576:1152] = a
    copies[9].start()
    copies[10].start()
    copies[4].wait()
    sums = (u + dot(a, wo[...], TN)).astype(BF)
    for i in range(8):
        so[i, 0:POS] = sums[i * POS : (i + 1) * POS]
    copies[5].wait()
    copies[6].start()
    for i in (7, 8, 9, 10, 6):
        copies[i].wait()


def time_kernel(x_ref, wq, wo, me, te, mid, mine, theirs, pt, at, ga, pg, probs, u_ref, c_ref, t, perm):
    for i in range(8):
        u_ref[i * POS : (i + 1) * POS] = x_ref[i, 0:POS]
        c_ref[i * POS : (i + 1) * POS] = x_ref[i, POS : 2 * POS]
    c = c_ref[...]
    normed, inverse = norm_rows(u_ref[...].astype(F32))
    pt[...] = rounded(dot(wq[...], normed.astype(BF), NT))
    ga[...] = rounded(dot(wo[...], c, NT))
    row = lax.broadcasted_iota(jnp.int32, (S, S), 0)
    col = lax.broadcasted_iota(jnp.int32, (S, S), 1)
    attend(pt, at, probs, (row % POS) == (col % POS))
    for h in range(HEADS):
        attend_grad(pt, ga, probs[h], h, pg)
    g = pg[...].astype(BF)
    grad = dot(g, wq[...], TN)
    mid[...] = norm_grad(c.astype(F32), grad, normed, inverse).astype(BF)
    lay_rows(mine, theirs, 0, rounded(normed), t, perm)
    lay_rows(mine, theirs, 576, c.astype(F32), t, perm)
    a = at[...].astype(BF)
    for out in (mine, theirs):
        out[1152:2880] = g
        out[2880:3456] = a
    mine[3456:4608] = me[...]
    theirs[3456:4608] = te[...]


def space_attention_grad_kernel(c_ref, probs, pts, wo, mine, theirs, pt, ga, pg, t, perm):
    c = c_ref[...]
    ga[...] = rounded(dot(wo[...], c, NT))
    pt[...] = pts[...].astype(F32)
    for h in range(HEADS):
        attend_grad(pt, ga, probs[h], h, pg)
    g = pg[...].astype(BF)
    lay_rows(mine, theirs, 0, c.astype(F32), t, perm)
    for out in (mine, theirs):
        out[576:2304] = g


def in_grad_kernel(c_ref, u_ref, g_ref, wq, in_grad):
    grad = dot(g_ref[576:2304], wq[...], TN)
    normed, inverse = norm_rows(u_ref[...].astype(F32))
    in_grad[...] = norm_grad(c_ref[...].astype(F32), grad, normed, inverse).astype(BF)


def spread(x, t, perm):
    t[...] = x.T
    for own in range(2):

        @pl.when(lax.axis_index("zl") == own)
        def _():
            for core in range(2):
                for y in range(4):
                    for half in range(2):
                        for z in range(4):
                            src = ROWS * (z * 8 + y * 2 + core) + HALF * (half ^ own)
                            dst = 576 * core + 144 * y + 72 * half + HALF * z
                            perm[dst : dst + HALF] = t[src : src + HALF]


def lay_rows(mine, theirs, base, x, t, perm):
    spread(x, t, perm)
    core = lax.axis_index("core")
    for out, half in ((mine, core), (theirs, 1 - core)):
        rows = perm[pl.ds(pl.multiple_of(half * 576, 576), 576)]
        out[base : base + 576] = rows.astype(BF)


def quarter(axis, h, p):
    me, core = lax.axis_index(axis), lax.axis_index("core")
    a = (me // 2 + (h * core + p * (1 - core))) % 2
    b = ((me + 1) // 2 + (h * (1 - core) + p * core)) % 2
    return 2 * a + (a + b) % 2


def bits(i):
    core = lax.axis_index("core")
    a, b = i // 2, ((i + 1) // 2) % 2
    return a * core + b * (1 - core), a * (1 - core) + b * core


PAIRS = ([[0, 1], [3, 2]], [[0, 3], [1, 2]])
BITS = [(h, p) for h in range(2) for p in range(2)]


STREAMS = {"xt": (0, 0), "ct": (0, 576), "xs": (0, 3456), "cs": (1, 0)}
SEGMENTS = (
    (("xt", 0, 1152, 432, 0, 384),),
    (("xt", 0, 1152, 432, 384, 48), ("ct", 0, 2880, 144, 0, 144), ("xs", 1, 576, 432, 0, 192)),
    (("xs", 1, 576, 432, 192, 240), ("cs", 0, 4032, 144, 0, 144)),
)


def product_kernel(piece, *refs):
    *factors, keep, send, left = refs
    pairs = [factors[i : i + 2] for i in range(0, len(factors), 2)]
    for k, (stream, *_) in enumerate(SEGMENTS[piece]):
        which, first = STREAMS[stream]
        for i, (hy, py) in enumerate(BITS):
            rows = pl.ds(pl.multiple_of(quarter("y", hy, py) * 144 + first, 144), 144)
            for j, ref in enumerate(pairs[which]):
                left[k, i * 144 : (i + 1) * 144, j * S : (j + 1) * S] = ref[rows]
    for hx, px in BITS:
        q = quarter("x", hx, px)
        parts = []
        for k, (_, which, first, n, start, count) in enumerate(SEGMENTS[piece]):
            rows = pl.ds(pl.multiple_of(first + start + q * n, 16), count)
            right = jnp.concatenate([ref[rows] for ref in pairs[which]], axis=1)
            parts.append(dot(left[k], right, NT))
        both = jnp.concatenate(parts, axis=1)
        for i, (hy, py) in enumerate(BITS):
            for hz in range(2):
                r = 144 * i + 72 * hz
                one, two, three = ((hx, hy, hz), (hy, hz, hx), (hz, hx, hy))[piece]
                out = send if one else keep
                out[two, three, px * 2 + py] = both[r : r + 72].astype(out.dtype)


def halve_kernel(k_ref, g_ref, keep, send):
    for i, out in enumerate((keep, send)):
        out[...] = (k_ref[i].astype(F32) + g_ref[i].astype(F32)).astype(out.dtype)


def zh_bits(z, core):
    a, b = z // 2, ((z + 1) // 2) % 2
    return (b, a) if core else (a, b)


def join_kernel(*refs):
    keep, got, out = refs[:3], refs[3:6], refs[6]
    own_x, own_y = bits(lax.axis_index("x"))[1], bits(lax.axis_index("y"))[1]
    for px in range(2):
        for py in range(2):
            place = ((own_x + px) % 2) * 2 + (own_y + py) % 2
            i = px * 2 + py
            accs = [k[i].astype(F32) + g[i].astype(F32) for k, g in zip(keep, got)]
            for core in range(2):

                @pl.when(lax.axis_index("core") == core)
                def _():
                    for h in range(2):
                        tiles = []
                        for p in range(2):
                            (z,) = [z for z in range(4) if zh_bits(z, core) == (h, p)]
                            rows = slice(HALF * z, HALF * (z + 1))
                            tiles += [acc[rows, S * j : S * (j + 1)] for acc in accs for j in range(3)]
                        out[place * 2 + h] = jnp.concatenate(tiles, axis=0).astype(BF)


def second_sum_kernel(x_ref, keep, send):
    acc = x_ref[0].astype(F32)
    for j in range(1, 8):
        acc = acc + x_ref[j].astype(F32)
    first, second = acc[0:162], acc[162:324]
    zh, core = lax.axis_index("zh"), lax.axis_index("core")
    own = (zh // 2) * core + (((zh + 1) // 2) % 2) * (1 - core)
    keep[...] = jnp.where(own == 0, first, second)
    send[...] = jnp.where(own == 0, second, first).astype(BF)


def copies_kernel(k_ref, g_ref, out):
    acc = (k_ref[...] + g_ref[...].astype(F32)).astype(BF)
    for i in range(8):
        out[i] = acc


def last_kernel(x_ref, qt, ot, qs, os):
    for half in range(2):
        parts = []
        for x in range(4):
            p = x_ref[half * 4 + x].astype(F32)
            parts.append(jnp.concatenate([p[HALF * i : HALF * (i + 1)] for i in range(9)], axis=1))
        rows = pl.ds(HALF * half, HALF)
        for base, qkv, proj in ((0, qt, ot), (HD, qs, os)):
            qkv[rows] = jnp.concatenate([p[:, base : base + 432] for p in parts], axis=1)
            proj[rows] = jnp.concatenate([p[:, base + 432 : base + HD] for p in parts], axis=1)


def swap(x, axes, groups=None):
    return lax.all_to_all(
        x, axes, split_axis=0, concat_axis=0, axis_index_groups=groups, tiled=True
    )


DSP = ("zl", "x")


def ring(x, axis):
    pairs = [(i * 2 + c, j * 2 + c) for c in range(2) for p in PAIRS[c] for i, j in (p, p[::-1])]
    return lax.ppermute(x, (axis, "core"), pairs)


def pair_z(x):
    pairs = []
    for z in range(8):
        for c in range(2):
            up = (z % 2 == 0) == (c == 0)
            to = (z + (1 if up else 7)) % 8
            pairs.append((((z % 2) * 4 + z // 2) * 2 + c, ((to % 2) * 4 + to // 2) * 2 + c))
    return lax.ppermute(x, ("zl", "zh", "core"), pairs)


STEPS = (lambda x: ring(x, "x"), lambda x: ring(x, "y"), pair_z)


def wide_cubes():
    return [
        [((x * 4 + z) * 4 + y) * 2 + core for x in gx for y in gy for z in gz]
        for core in range(2)
        for gx in PAIRS[1 - core]
        for gy in PAIRS[1 - core]
        for gz in PAIRS[1 - core]
    ]


def last_pair(x):
    pairs = []
    for core in range(2):
        for i, j in PAIRS[core]:
            pairs += [(i * 2 + core, j * 2 + core), (j * 2 + core, i * 2 + core)]
    return lax.ppermute(x, ("zh", "core"), pairs)


def to_other_core(x):
    return lax.ppermute(x, "core", [(0, 1), (1, 0)])


def local(latents, out_grad, wqs, wos, wqt, wot):
    u = latents[0, 0]
    wqs, wos, wqt, wot = wqs.T, wos.T, wqt.T, wot.T
    wide, thin, square = ((3 * HD, S), F32), ((HD, S), F32), ((HEADS, S, S), F32)
    full, flipped, factors = ((S, D), BF), ((D, S), F32), [((4608, S), BF)] * 2
    dense = 2 * S * D * 4 * HD
    early = [((1152, S), BF)] * 2
    late = [((2304, S), BF)] * 2
    sent, probs, pts, mine_e, theirs_e = call(
        space_forward_kernel,
        [((8, 2 * POS, D), BF), square, ((3 * HD, S), BF)] + early,
        (u, out_grad.reshape(8, POS, D), wqs, wos),
        [wide, thin, full, ((3 * HD, D), BF), ((HD, D), BF), flipped, flipped]
        + [((8, 2 * POS, D), BF), square, ((3 * HD, S), BF)]
        + early,
        flops=dense,
        limit=56,
        hbm=(0, 1, 2, 3),
        far=True,
    )
    mid, mine_e, theirs_e = call(
        time_kernel,
        [full] + factors,
        (swap(sent, DSP), wqt, wot, mine_e, theirs_e),
        [wide, thin, thin, wide, square, full, full, flipped, flipped],
        flops=2 * dense,
    )
    mid = swap(mid.reshape(8, POS, D), DSP).reshape(S, D)
    mid, theirs_e = lax.optimization_barrier((mid, theirs_e))
    theirs_e = to_other_core(theirs_e)
    mine_l, theirs_l = call(
        space_attention_grad_kernel,
        late,
        (mid, probs, pts, wos),
        [wide, thin, wide, flipped, flipped],
        flops=dense // 4,
    )
    theirs_l = to_other_core(theirs_l)
    (in_grad,) = call(in_grad_kernel, [full], (mid, u, mine_l, wqs), flops=dense)

    def product(piece, *pairs):
        return call(
            functools.partial(product_kernel, piece),
            [((2, 2, 4, 72, PIECE), BF)] * 2,
            pairs,
            [((len(SEGMENTS[piece]), 576, 2 * S), BF)],
            flops=2 * HD * 256 * 4 * PIECE,
        )

    early = (mine_e, theirs_e)
    keep, send = product(0, *early)
    keep, theirs_l = lax.optimization_barrier((keep, theirs_l))
    pairs = (*early, mine_l, theirs_l)
    halves = [(keep, send), product(1, *pairs), product(2, *pairs)]
    got = [STEPS[i](send) for i, (_, send) in enumerate(halves)]
    in_grad, got[2] = lax.optimization_barrier((in_grad, got[2]))
    for step in (1, 2):
        shape = ((2, 4, 72, PIECE), (4, 72, PIECE))[step - 1]
        halves = [
            call(halve_kernel, [(shape, F32), (shape, BF)], (h[0], g)) for h, g in zip(halves, got)
        ]
        got = [STEPS[(i + step) % 3](send) for i, (_, send) in enumerate(halves)]
    (terms,) = call(join_kernel, [((8, 324, S), BF)], ([h[0] for h in halves] + got))
    terms = swap(terms, ("x", "zh", "y", "core"), wide_cubes())
    keep, send = call(second_sum_kernel, [((162, S), F32), ((162, S), BF)], (terms,))
    (copies,) = call(copies_kernel, [((8, 162, S), BF)], (keep, last_pair(send)))
    copies = swap(copies, DSP)
    gqt, got, gqs, gos = call(
        last_kernel, [((ROWS, 3 * HD), F32), ((ROWS, HD), F32)] * 2, (copies,)
    )
    return in_grad[None, None], gqs, gos, gqt, got


def solution(mesh):
    fine = Mesh(mesh.devices.reshape(2, 4, 4, 4, 2), ("zl", "x", "zh", "y", "core"))
    dp = ("zh", "y", "core")
    act = P(dp, ("zl", "x"), None, None)
    in_specs = (act, act, P(), P(), P(), P())
    out_specs = (act, P(dp, None), P(dp, None), P(dp, None), P(dp, None))
    return jax.shard_map(local, mesh=fine, in_specs=in_specs, out_specs=out_specs, check_vma=False)
```

```python
import functools

import jax
import jax.numpy as jnp
from jax import lax
from jax.experimental import pallas as pl
from jax.experimental.pallas import tpu as pltpu
from jax.sharding import Mesh, PartitionSpec as P

D = 1152
HEADS = 8
HDIM = 72
HD = 576
S = 128
POS = 16
ROWS = 36
HALF = 18
PIECE = 384
PIECE = 384
SCALE = HDIM ** (-0.5)
EPS = 1e-06
BF = jnp.bfloat16
F32 = jnp.float32
MIB = 1024 * 1024

NN = (((1,), (0,)), ((), ()))
NT = (((1,), (1,)), ((), ()))
TN = (((0,), (0,)), ((), ()))


def dot(a, b, dims=NN):
    return lax.dot_general(a, b, dims, preferred_element_type=F32)


def norm_rows(u):
    centred = u - jnp.mean(u, axis=-1, keepdims=True)
    inverse = lax.rsqrt(jnp.mean(centred * centred, axis=-1, keepdims=True) + EPS)
    return centred * inverse, inverse


def norm_grad(c, g, normed, inverse):
    mean_g = jnp.mean(g, axis=-1, keepdims=True)
    mean_x = jnp.mean(g * normed, axis=-1, keepdims=True)
    return c + inverse * (g - mean_g - normed * mean_x)


def rounded(x):
    return x.astype(BF).astype(F32)


def call(kernel, outs, args, scratch=(), flops=0, limit=24, hbm=(), far=False):
    vmem = pl.BlockSpec(memory_space=pltpu.VMEM)
    away = pl.BlockSpec(memory_space=pltpu.HBM)
    moved = 2 * sum(x.size * x.dtype.itemsize for x in args)
    return pl.pallas_call(
        kernel,
        out_shape=[jax.ShapeDtypeStruct(s, t) for s, t in outs],
        in_specs=[away if i in hbm else vmem for i in range(len(args))],
        out_specs=[away if far else vmem] * len(outs),
        scratch_shapes=[pltpu.VMEM(s, t) for s, t in scratch]
        + ([pltpu.SemaphoreType.DMA((11,))] if hbm else []),
        compiler_params=pltpu.CompilerParams(vmem_limit_bytes=limit * MIB),
        cost_estimate=pl.CostEstimate(flops=flops, bytes_accessed=moved, transcendentals=0),
    )(*args)


def head(ref, part, h):
    r = part * HD + h * HDIM
    return ref[r : r + HDIM].astype(BF)


def probabilities(pt, h, mask):
    s = dot(head(pt, 1, h), head(pt, 0, h), TN) * SCALE
    if mask is not None:
        s = jnp.where(mask, s, -1e30)
    e = jnp.exp(s - jnp.max(s, axis=0, keepdims=True))
    return e / jnp.sum(e, axis=0, keepdims=True)


def attend(pt, at, probs, mask):
    for h in range(HEADS):
        p = probabilities(pt, h, mask)
        probs[h] = p
        at[h * HDIM : (h + 1) * HDIM] = dot(head(pt, 2, h), p.astype(BF))


def attend_grad(pt, ga, p, h, pg):
    q, k, v, g = head(pt, 0, h), head(pt, 1, h), head(pt, 2, h), head(ga, 0, h)
    gp = dot(v, g, TN)
    gs = (p * (gp - jnp.sum(p * gp, axis=0, keepdims=True)) * SCALE).astype(BF)
    r = h * HDIM
    pg[r : r + HDIM] = dot(k, gs)
    pg[HD + r : HD + r + HDIM] = dot(q, gs, NT)
    pg[2 * HD + r : 2 * HD + r + HDIM] = dot(g, p.astype(BF), NT)


def space_forward_kernel(
    u_hbm, c_hbm, wq_hbm, wo_hbm,
    out_hbm, probs_hbm, pts_hbm, mine_hbm, theirs_hbm,
    pt, at, u_ref, wq, wo, t, perm, so, probs, pts, mine, theirs, sems,
):
    pairs = [(u_hbm, u_ref)]
    for i in range(3):
        rows = pl.ds(i * HD, HD)
        pairs.append((wq_hbm.at[rows], wq.at[rows]))
    pairs += [(wo_hbm, wo), (c_hbm, so.at[:, pl.ds(POS, POS)])]
    pairs += [(so, out_hbm), (probs, probs_hbm), (pts, pts_hbm)]
    pairs += [(mine, mine_hbm), (theirs, theirs_hbm)]
    copies = [pltpu.make_async_copy(x, y, sems.at[i]) for i, (x, y) in enumerate(pairs)]
    for i in range(4):
        copies[i].start()
    copies[0].wait()
    u = u_ref[...].astype(F32)
    normed, _ = norm_rows(u)
    hidden = normed.astype(BF)
    lay_rows(mine, theirs, 0, hidden.astype(F32), t, perm)
    for i in range(3):
        copies[1 + i].wait()
        if i == 0:
            copies[4].start()
            copies[5].start()
        pt[i * HD : (i + 1) * HD] = rounded(dot(wq[i * HD : (i + 1) * HD], hidden, NT))
    pts[...] = pt[...].astype(BF)
    copies[8].start()
    attend(pt, at, probs, None)
    copies[7].start()
    a = at[...].astype(BF)
    mine[576:1152] = a
    theirs[576:1152] = a
    copies[9].start()
    copies[10].start()
    copies[4].wait()
    sums = (u + dot(a, wo[...], TN)).astype(BF)
    for i in range(8):
        so[i, 0:POS] = sums[i * POS : (i + 1) * POS]
    copies[5].wait()
    copies[6].start()
    for i in (7, 8, 9, 10, 6):
        copies[i].wait()


def time_kernel(x_ref, wq, wo, me, te, mid, mine, theirs, pt, at, ga, pg, probs, u_ref, c_ref, t, perm):
    for i in range(8):
        u_ref[i * POS : (i + 1) * POS] = x_ref[i, 0:POS]
        c_ref[i * POS : (i + 1) * POS] = x_ref[i, POS : 2 * POS]
    c = c_ref[...]
    normed, inverse = norm_rows(u_ref[...].astype(F32))
    pt[...] = rounded(dot(wq[...], normed.astype(BF), NT))
    ga[...] = rounded(dot(wo[...], c, NT))
    row = lax.broadcasted_iota(jnp.int32, (S, S), 0)
    col = lax.broadcasted_iota(jnp.int32, (S, S), 1)
    attend(pt, at, probs, (row % POS) == (col % POS))
    for h in range(HEADS):
        attend_grad(pt, ga, probs[h], h, pg)
    g = pg[...].astype(BF)
    grad = dot(g, wq[...], TN)
    mid[...] = norm_grad(c.astype(F32), grad, normed, inverse).astype(BF)
    lay_rows(mine, theirs, 0, rounded(normed), t, perm)
    lay_rows(mine, theirs, 576, c.astype(F32), t, perm)
    a = at[...].astype(BF)
    for out in (mine, theirs):
        out[1152:2880] = g
        out[2880:3456] = a
    mine[3456:4608] = me[...]
    theirs[3456:4608] = te[...]


def space_attention_grad_kernel(c_ref, probs, pts, wo, mine, theirs, pt, ga, pg, t, perm):
    c = c_ref[...]
    ga[...] = rounded(dot(wo[...], c, NT))
    pt[...] = pts[...].astype(F32)
    for h in range(HEADS):
        attend_grad(pt, ga, probs[h], h, pg)
    g = pg[...].astype(BF)
    lay_rows(mine, theirs, 0, c.astype(F32), t, perm)
    for out in (mine, theirs):
        out[576:2304] = g


def in_grad_kernel(c_ref, u_ref, g_ref, wq, in_grad):
    grad = dot(g_ref[576:2304], wq[...], TN)
    normed, inverse = norm_rows(u_ref[...].astype(F32))
    in_grad[...] = norm_grad(c_ref[...].astype(F32), grad, normed, inverse).astype(BF)


def spread(x, t, perm):
    t[...] = x.T
    for own in range(2):

        @pl.when(lax.axis_index("zl") == own)
        def _():
            for core in range(2):
                for y in range(4):
                    for half in range(2):
                        for z in range(4):
                            src = ROWS * (z * 8 + y * 2 + core) + HALF * (half ^ own)
                            dst = 576 * core + 144 * y + 72 * half + HALF * z
                            perm[dst : dst + HALF] = t[src : src + HALF]


def lay_rows(mine, theirs, base, x, t, perm):
    spread(x, t, perm)
    core = lax.axis_index("core")
    for out, half in ((mine, core), (theirs, 1 - core)):
        rows = perm[pl.ds(pl.multiple_of(half * 576, 576), 576)]
        out[base : base + 576] = rows.astype(BF)


def first(axis):
    core = lax.axis_index("core")
    return 1 - core if axis == "y" else core


def quarter(axis, h, p):
    me, core = lax.axis_index(axis), first(axis)
    a = (me // 2 + (h * core + p * (1 - core))) % 2
    b = ((me + 1) // 2 + (h * (1 - core) + p * core)) % 2
    return 2 * a + (a + b) % 2


def bits(axis, i):
    core = first(axis)
    a, b = i // 2, ((i + 1) // 2) % 2
    return a * core + b * (1 - core), a * (1 - core) + b * core


PAIRS = ([[0, 1], [3, 2]], [[0, 3], [1, 2]])
BITS = [(h, p) for h in range(2) for p in range(2)]


STREAMS = {"xt": (0, 0), "ct": (0, 576), "xs": (0, 3456), "cs": (1, 0)}
SEGMENTS = (
    (("xt", 0, 1152, 432, 0, 384),),
    (("xt", 0, 1152, 432, 384, 48), ("ct", 0, 2880, 144, 0, 144), ("xs", 1, 576, 432, 0, 192)),
    (("xs", 1, 576, 432, 192, 240), ("cs", 0, 4032, 144, 0, 144)),
)


def product_kernel(piece, *refs):
    *factors, keep, send, left = refs
    pairs = [factors[i : i + 2] for i in range(0, len(factors), 2)]
    for k, (stream, *_) in enumerate(SEGMENTS[piece]):
        which, first = STREAMS[stream]
        for i, (hy, py) in enumerate(BITS):
            rows = pl.ds(pl.multiple_of(quarter("y", hy, py) * 144 + first, 144), 144)
            for j, ref in enumerate(pairs[which]):
                left[k, i * 144 : (i + 1) * 144, j * S : (j + 1) * S] = ref[rows]
    for hx, px in BITS:
        q = quarter("x", hx, px)
        parts = []
        for k, (_, which, first, n, start, count) in enumerate(SEGMENTS[piece]):
            rows = pl.ds(pl.multiple_of(first + start + q * n, 16), count)
            right = jnp.concatenate([ref[rows] for ref in pairs[which]], axis=1)
            parts.append(dot(left[k], right, NT))
        both = jnp.concatenate(parts, axis=1)
        for i, (hy, py) in enumerate(BITS):
            for hz in range(2):
                r = 144 * i + 72 * hz
                one, two, three = ((hx, hy, hz), (hy, hz, hx), (hz, hx, hy))[piece]
                out = send if one else keep
                out[two, three, px * 2 + py] = both[r : r + 72].astype(out.dtype)


def halve_kernel(k_ref, g_ref, keep, send):
    for i, out in enumerate((keep, send)):
        out[...] = (k_ref[i].astype(F32) + g_ref[i].astype(F32)).astype(out.dtype)


def join_kernel(*refs):
    keep, got, out = refs[:3], refs[3:6], refs[6]
    own_x, own_y = (bits(axis, lax.axis_index(axis))[1] for axis in "xy")
    for px in range(2):
        for py in range(2):
            place = ((own_x + px) % 2) * 2 + (own_y + py) % 2
            i = px * 2 + py
            accs = [k[i] + g[i].astype(F32) for k, g in zip(keep, got)]
            for z in range(4):
                h, p = bits("zh", z)
                rows = slice(HALF * z, HALF * (z + 1))
                tiles = [acc[rows, S * j : S * (j + 1)] for acc in accs for j in range(3)]
                tiles.append(jnp.zeros((14, S), F32))
                to = pl.ds(pl.multiple_of(p * 176, 176), 176)
                out[place * 2 + h, to] = jnp.concatenate(tiles, axis=0).astype(BF)


def second_sum_kernel(x_ref, keep, send):
    own = bits("zh", lax.axis_index("zh"))[1]
    for i, out in enumerate((keep, send)):
        rows = pl.ds(pl.multiple_of((own + i) % 2 * 176, 176), 176)
        acc = x_ref[0, rows].astype(F32)
        for j in range(1, 8):
            acc = acc + x_ref[j, rows].astype(F32)
        out[...] = acc[0:162].astype(out.dtype)


def copies_kernel(k_ref, g_ref, out):
    acc = (k_ref[...] + g_ref[...].astype(F32)).astype(BF)
    for i in range(8):
        out[i] = acc


def last_kernel(x_ref, qt, ot, qs, os):
    for half in range(2):
        parts = []
        for x in range(4):
            p = x_ref[half * 4 + x].astype(F32)
            parts.append(jnp.concatenate([p[HALF * i : HALF * (i + 1)] for i in range(9)], axis=1))
        rows = pl.ds(HALF * half, HALF)
        for base, qkv, proj in ((0, qt, ot), (HD, qs, os)):
            qkv[rows] = jnp.concatenate([p[:, base : base + 432] for p in parts], axis=1)
            proj[rows] = jnp.concatenate([p[:, base + 432 : base + HD] for p in parts], axis=1)


def swap(x, axes, groups=None):
    return lax.all_to_all(
        x, axes, split_axis=0, concat_axis=0, axis_index_groups=groups, tiled=True
    )


DSP = ("zl", "x")


def ring(x, axis):
    pairs = []
    for c in range(2):
        for i, j in PAIRS[1 - c if axis == "y" else c]:
            pairs += [(i * 2 + c, j * 2 + c), (j * 2 + c, i * 2 + c)]
    return lax.ppermute(x, (axis, "core"), pairs)


def pair_z(x):
    pairs = []
    for z in range(8):
        for c in range(2):
            up = (z % 2 == 0) == (c == 0)
            to = (z + (1 if up else 7)) % 8
            pairs.append((((z % 2) * 4 + z // 2) * 2 + c, ((to % 2) * 4 + to // 2) * 2 + c))
    return lax.ppermute(x, ("zl", "zh", "core"), pairs)


STEPS = (lambda x: ring(x, "x"), lambda x: ring(x, "y"), pair_z)


def wide_cubes():
    return [
        [((x * 4 + z) * 4 + y) * 2 + core for x in gx for y in gy for z in gz]
        for core in range(2)
        for gx in PAIRS[1 - core]
        for gy in PAIRS[core]
        for gz in PAIRS[core]
    ]


def last_pair(x):
    pairs = []
    for core in range(2):
        for i, j in PAIRS[1 - core]:
            pairs += [(i * 2 + core, j * 2 + core), (j * 2 + core, i * 2 + core)]
    return lax.ppermute(x, ("zh", "core"), pairs)


def to_other_core(x):
    return lax.ppermute(x, "core", [(0, 1), (1, 0)])


def local(latents, out_grad, wqs, wos, wqt, wot):
    u = latents[0, 0]
    wqs, wos, wqt, wot = wqs.T, wos.T, wqt.T, wot.T
    wide, thin, square = ((3 * HD, S), F32), ((HD, S), F32), ((HEADS, S, S), F32)
    full, flipped, factors = ((S, D), BF), ((D, S), F32), [((4608, S), BF)] * 2
    dense = 2 * S * D * 4 * HD
    early = [((1152, S), BF)] * 2
    late = [((2304, S), BF)] * 2
    sent, probs, pts, mine_e, theirs_e = call(
        space_forward_kernel,
        [((8, 2 * POS, D), BF), square, ((3 * HD, S), BF)] + early,
        (u, out_grad.reshape(8, POS, D), wqs, wos),
        [wide, thin, full, ((3 * HD, D), BF), ((HD, D), BF), flipped, flipped]
        + [((8, 2 * POS, D), BF), square, ((3 * HD, S), BF)]
        + early,
        flops=dense,
        limit=56,
        hbm=(0, 1, 2, 3),
        far=True,
    )
    mid, mine_e, theirs_e = call(
        time_kernel,
        [full] + factors,
        (swap(sent, DSP), wqt, wot, mine_e, theirs_e),
        [wide, thin, thin, wide, square, full, full, flipped, flipped],
        flops=2 * dense,
    )
    mid = swap(mid.reshape(8, POS, D), DSP).reshape(S, D)
    mid, theirs_e = lax.optimization_barrier((mid, theirs_e))
    theirs_e = to_other_core(theirs_e)
    mine_l, theirs_l = call(
        space_attention_grad_kernel,
        late,
        (mid, probs, pts, wos),
        [wide, thin, wide, flipped, flipped],
        flops=dense // 4,
    )
    theirs_l = to_other_core(theirs_l)
    (in_grad,) = call(in_grad_kernel, [full], (mid, u, mine_l, wqs), flops=dense)

    def product(piece, *pairs):
        return call(
            functools.partial(product_kernel, piece),
            [((2, 2, 4, 72, PIECE), BF)] * 2,
            pairs,
            [((len(SEGMENTS[piece]), 576, 2 * S), BF)],
            flops=2 * HD * 256 * 4 * PIECE,
        )

    early = (mine_e, theirs_e)
    keep, send = product(0, *early)
    keep, theirs_l = lax.optimization_barrier((keep, theirs_l))
    pairs = (*early, mine_l, theirs_l)
    halves = [(keep, send), product(1, *pairs), product(2, *pairs)]
    got = [STEPS[i](send) for i, (_, send) in enumerate(halves)]
    in_grad, got[2] = lax.optimization_barrier((in_grad, got[2]))
    for step in (1, 2):
        shape = ((2, 4, 72, PIECE), (4, 72, PIECE))[step - 1]
        halves = [
            call(halve_kernel, [(shape, F32), (shape, BF)], (h[0], g)) for h, g in zip(halves, got)
        ]
        got = [STEPS[(i + step) % 3](send) for i, (_, send) in enumerate(halves)]
    (terms,) = call(join_kernel, [((8, 352, S), BF)], ([h[0] for h in halves] + got))
    terms = swap(terms, ("x", "zh", "y", "core"), wide_cubes())
    keep, send = call(second_sum_kernel, [((162, S), F32), ((162, S), BF)], (terms,))
    (copies,) = call(copies_kernel, [((8, 162, S), BF)], (keep, last_pair(send)))
    copies = swap(copies, DSP)
    gqt, got, gqs, gos = call(
        last_kernel, [((ROWS, 3 * HD), F32), ((ROWS, HD), F32)] * 2, (copies,)
    )
    return in_grad[None, None], gqs, gos, gqt, got


def solution(mesh):
    fine = Mesh(mesh.devices.reshape(2, 4, 4, 4, 2), ("zl", "x", "zh", "y", "core"))
    dp = ("zh", "y", "core")
    act = P(dp, ("zl", "x"), None, None)
    in_specs = (act, act, P(), P(), P(), P())
    out_specs = (act, P(dp, None), P(dp, None), P(dp, None), P(dp, None))
    return jax.shard_map(local, mesh=fine, in_specs=in_specs, out_specs=out_specs, check_vma=False)
```

```python
import functools

import jax
import jax.numpy as jnp
from jax import lax
from jax.experimental import pallas as pl
from jax.experimental.pallas import tpu as pltpu
from jax.sharding import Mesh, PartitionSpec as P

D = 1152
HEADS = 8
HDIM = 72
HD = 576
S = 128
POS = 16
ROWS = 36
HALF = 18
PIECE = 384
PIECE = 384
SCALE = HDIM ** (-0.5)
EPS = 1e-06
BF = jnp.bfloat16
F32 = jnp.float32
MIB = 1024 * 1024

NN = (((1,), (0,)), ((), ()))
NT = (((1,), (1,)), ((), ()))
TN = (((0,), (0,)), ((), ()))


def dot(a, b, dims=NN):
    return lax.dot_general(a, b, dims, preferred_element_type=F32)


def norm_rows(u):
    centred = u - jnp.mean(u, axis=-1, keepdims=True)
    inverse = lax.rsqrt(jnp.mean(centred * centred, axis=-1, keepdims=True) + EPS)
    return centred * inverse, inverse


def norm_grad(c, g, normed, inverse):
    mean_g = jnp.mean(g, axis=-1, keepdims=True)
    mean_x = jnp.mean(g * normed, axis=-1, keepdims=True)
    return c + inverse * (g - mean_g - normed * mean_x)


def rounded(x):
    return x.astype(BF).astype(F32)


def call(kernel, outs, args, scratch=(), flops=0, limit=24, hbm=(), far=False):
    vmem = pl.BlockSpec(memory_space=pltpu.VMEM)
    away = pl.BlockSpec(memory_space=pltpu.HBM)
    moved = 2 * sum(x.size * x.dtype.itemsize for x in args)
    return pl.pallas_call(
        kernel,
        out_shape=[jax.ShapeDtypeStruct(s, t) for s, t in outs],
        in_specs=[away if i in hbm else vmem for i in range(len(args))],
        out_specs=[away if far else vmem] * len(outs),
        scratch_shapes=[pltpu.VMEM(s, t) for s, t in scratch]
        + ([pltpu.SemaphoreType.DMA((11,))] if hbm else []),
        compiler_params=pltpu.CompilerParams(vmem_limit_bytes=limit * MIB),
        cost_estimate=pl.CostEstimate(flops=flops, bytes_accessed=moved, transcendentals=0),
    )(*args)


def head(ref, part, h):
    r = part * HD + h * HDIM
    return ref[r : r + HDIM].astype(BF)


def probabilities(pt, h, mask):
    s = dot(head(pt, 1, h), head(pt, 0, h), TN) * SCALE
    if mask is not None:
        s = jnp.where(mask, s, -1e30)
    e = jnp.exp(s - jnp.max(s, axis=0, keepdims=True))
    return e / jnp.sum(e, axis=0, keepdims=True)


def attend(pt, at, probs, mask):
    for h in range(HEADS):
        p = probabilities(pt, h, mask)
        probs[h] = p
        at[h * HDIM : (h + 1) * HDIM] = dot(head(pt, 2, h), p.astype(BF))


def attend_grad(pt, ga, p, h, pg):
    q, k, v, g = head(pt, 0, h), head(pt, 1, h), head(pt, 2, h), head(ga, 0, h)
    gp = dot(v, g, TN)
    gs = (p * (gp - jnp.sum(p * gp, axis=0, keepdims=True)) * SCALE).astype(BF)
    r = h * HDIM
    pg[r : r + HDIM] = dot(k, gs)
    pg[HD + r : HD + r + HDIM] = dot(q, gs, NT)
    pg[2 * HD + r : 2 * HD + r + HDIM] = dot(g, p.astype(BF), NT)


def space_forward_kernel(
    u_hbm, c_hbm, wq_hbm, wo_hbm,
    out_hbm, probs_hbm, pts_hbm, mine_hbm, theirs_hbm,
    pt, at, u_ref, wq, wo, t, perm, so, probs, pts, mine, theirs, sems,
):
    pairs = [(u_hbm, u_ref)]
    for i in range(3):
        rows = pl.ds(i * HD, HD)
        pairs.append((wq_hbm.at[rows], wq.at[rows]))
    pairs += [(wo_hbm, wo), (c_hbm, so.at[:, pl.ds(POS, POS)])]
    pairs += [(so, out_hbm), (probs, probs_hbm), (pts, pts_hbm)]
    pairs += [(mine, mine_hbm), (theirs, theirs_hbm)]
    copies = [pltpu.make_async_copy(x, y, sems.at[i]) for i, (x, y) in enumerate(pairs)]
    for i in range(4):
        copies[i].start()
    copies[0].wait()
    u = u_ref[...].astype(F32)
    normed, _ = norm_rows(u)
    hidden = normed.astype(BF)
    lay_rows(mine, theirs, 0, hidden.astype(F32), t, perm)
    for i in range(3):
        copies[1 + i].wait()
        if i == 0:
            copies[4].start()
            copies[5].start()
        pt[i * HD : (i + 1) * HD] = rounded(dot(wq[i * HD : (i + 1) * HD], hidden, NT))
    pts[...] = pt[...].astype(BF)
    copies[8].start()
    attend(pt, at, probs, None)
    copies[7].start()
    a = at[...].astype(BF)
    mine[576:1152] = a
    theirs[576:1152] = a
    copies[9].start()
    copies[10].start()
    copies[4].wait()
    sums = (u + dot(a, wo[...], TN)).astype(BF)
    for i in range(8):
        so[i, 0:POS] = sums[i * POS : (i + 1) * POS]
    copies[5].wait()
    copies[6].start()
    for i in (7, 8, 9, 10, 6):
        copies[i].wait()


def time_kernel(x_ref, wq, wo, me, te, mid, mine, theirs, pt, at, ga, pg, probs, u_ref, c_ref, t, perm):
    for i in range(8):
        u_ref[i * POS : (i + 1) * POS] = x_ref[i, 0:POS]
        c_ref[i * POS : (i + 1) * POS] = x_ref[i, POS : 2 * POS]
    c = c_ref[...]
    normed, inverse = norm_rows(u_ref[...].astype(F32))
    pt[...] = rounded(dot(wq[...], normed.astype(BF), NT))
    ga[...] = rounded(dot(wo[...], c, NT))
    row = lax.broadcasted_iota(jnp.int32, (S, S), 0)
    col = lax.broadcasted_iota(jnp.int32, (S, S), 1)
    attend(pt, at, probs, (row % POS) == (col % POS))
    for h in range(HEADS):
        attend_grad(pt, ga, probs[h], h, pg)
    g = pg[...].astype(BF)
    grad = dot(g, wq[...], TN)
    mid[...] = norm_grad(c.astype(F32), grad, normed, inverse).astype(BF)
    lay_rows(mine, theirs, 0, rounded(normed), t, perm)
    lay_rows(mine, theirs, 576, c.astype(F32), t, perm)
    a = at[...].astype(BF)
    for out in (mine, theirs):
        out[1152:2880] = g
        out[2880:3456] = a
    mine[3456:4608] = me[...]
    theirs[3456:4608] = te[...]


def space_attention_grad_kernel(c_ref, probs, pts, wo, mine, theirs, pt, ga, pg, t, perm):
    c = c_ref[...]
    ga[...] = rounded(dot(wo[...], c, NT))
    pt[...] = pts[...].astype(F32)
    for h in range(HEADS):
        attend_grad(pt, ga, probs[h], h, pg)
    g = pg[...].astype(BF)
    lay_rows(mine, theirs, 0, c.astype(F32), t, perm)
    for out in (mine, theirs):
        out[576:2304] = g


def in_grad_kernel(c_ref, u_ref, g_ref, wq, in_grad):
    grad = dot(g_ref[576:2304], wq[...], TN)
    normed, inverse = norm_rows(u_ref[...].astype(F32))
    in_grad[...] = norm_grad(c_ref[...].astype(F32), grad, normed, inverse).astype(BF)


def spread(x, t, perm):
    t[...] = x.T
    for own in range(2):

        @pl.when(lax.axis_index("zl") == own)
        def _():
            for core in range(2):
                for y in range(4):
                    for half in range(2):
                        for z in range(4):
                            src = ROWS * (z * 8 + y * 2 + core) + HALF * (half ^ own)
                            dst = 576 * core + 144 * y + 72 * half + HALF * z
                            perm[dst : dst + HALF] = t[src : src + HALF]


def lay_rows(mine, theirs, base, x, t, perm):
    spread(x, t, perm)
    core = lax.axis_index("core")
    for out, half in ((mine, core), (theirs, 1 - core)):
        rows = perm[pl.ds(pl.multiple_of(half * 576, 576), 576)]
        out[base : base + 576] = rows.astype(BF)


def quarter(axis, h, p):
    me, core = lax.axis_index(axis), lax.axis_index("core")
    a = (me // 2 + (h * core + p * (1 - core))) % 2
    b = ((me + 1) // 2 + (h * (1 - core) + p * core)) % 2
    return 2 * a + (a + b) % 2


def bits(i):
    core = lax.axis_index("core")
    a, b = i // 2, ((i + 1) // 2) % 2
    return a * core + b * (1 - core), a * (1 - core) + b * core


PAIRS = ([[0, 1], [3, 2]], [[0, 3], [1, 2]])
BITS = [(h, p) for h in range(2) for p in range(2)]
PLACES = ([(0, 0), (1, 0), (1, 1), (0, 1)], [(0, 0), (0, 1), (1, 1), (1, 0)])


STREAMS = {"xt": (0, 0), "ct": (0, 576), "xs": (0, 3456), "cs": (1, 0)}
SEGMENTS = (
    (("xt", 0, 1152, 432, 0, 384),),
    (("xt", 0, 1152, 432, 384, 48), ("ct", 0, 2880, 144, 0, 144), ("xs", 1, 576, 432, 0, 192)),
    (("xs", 1, 576, 432, 192, 240), ("cs", 0, 4032, 144, 0, 144)),
)


def product_kernel(piece, *refs):
    *factors, keep, send, left = refs
    pairs = [factors[i : i + 2] for i in range(0, len(factors), 2)]
    for k, (stream, *_) in enumerate(SEGMENTS[piece]):
        which, first = STREAMS[stream]
        for i, (hy, py) in enumerate(BITS):
            rows = pl.ds(pl.multiple_of(quarter("y", hy, py) * 144 + first, 144), 144)
            for j, ref in enumerate(pairs[which]):
                left[k, i * 144 : (i + 1) * 144, j * S : (j + 1) * S] = ref[rows]
    for hx, px in BITS:
        q = quarter("x", hx, px)
        parts = []
        for k, (_, which, first, n, start, count) in enumerate(SEGMENTS[piece]):
            rows = pl.ds(pl.multiple_of(first + start + q * n, 16), count)
            right = jnp.concatenate([ref[rows] for ref in pairs[which]], axis=1)
            parts.append(dot(left[k], right, NT))
        both = jnp.concatenate(parts, axis=1)
        for i, (hy, py) in enumerate(BITS):
            for hz in range(2):
                r = 144 * i + 72 * hz
                one, two, three = ((hx, hy, hz), (hy, hz, hx), (hz, hx, hy))[piece]
                out = send if one else keep
                out[two, three, px * 2 + py] = both[r : r + 72].astype(out.dtype)


def halve_kernel(k_ref, g_ref, keep, send):
    for i, out in enumerate((keep, send)):
        out[...] = (k_ref[i].astype(F32) + g_ref[i].astype(F32)).astype(out.dtype)


def join_kernel(*refs):
    keep, got, out = refs[:3], refs[3:6], refs[6]
    own_x, own_y = bits(lax.axis_index("x"))[1], bits(lax.axis_index("y"))[1]
    for px in range(2):
        for py in range(2):
            place = ((own_x + px) % 2) * 2 + (own_y + py) % 2
            i = px * 2 + py
            accs = [k[i].astype(F32) + g[i].astype(F32) for k, g in zip(keep, got)]
            for core in range(2):

                @pl.when(lax.axis_index("core") == core)
                def _():
                    for h in range(2):
                        tiles = []
                        for z in (PLACES[core].index((h, p)) for p in range(2)):
                            rows = slice(HALF * z, HALF * (z + 1))
                            tiles += [acc[rows, S * j : S * (j + 1)] for acc in accs for j in range(3)]
                        out[place * 2 + h] = jnp.concatenate(tiles, axis=0).astype(BF)


def second_sum_kernel(x_ref, keep, send):
    acc = x_ref[0].astype(F32)
    for j in range(1, 8):
        acc = acc + x_ref[j].astype(F32)
    first, second = acc[0:162], acc[162:324]
    own = bits(lax.axis_index("zh"))[1]
    keep[...] = jnp.where(own == 0, first, second)
    send[...] = jnp.where(own == 0, second, first).astype(BF)


def copies_kernel(k_ref, g_ref, out):
    acc = (k_ref[...] + g_ref[...].astype(F32)).astype(BF)
    for i in range(8):
        out[i] = acc


def last_kernel(x_ref, qt, ot, qs, os):
    for half in range(2):
        parts = []
        for x in range(4):
            p = x_ref[half * 4 + x].astype(F32)
            parts.append(jnp.concatenate([p[HALF * i : HALF * (i + 1)] for i in range(9)], axis=1))
        rows = pl.ds(HALF * half, HALF)
        for base, qkv, proj in ((0, qt, ot), (HD, qs, os)):
            qkv[rows] = jnp.concatenate([p[:, base : base + 432] for p in parts], axis=1)
            proj[rows] = jnp.concatenate([p[:, base + 432 : base + HD] for p in parts], axis=1)


def swap(x, axes, groups=None):
    return lax.all_to_all(
        x, axes, split_axis=0, concat_axis=0, axis_index_groups=groups, tiled=True
    )


DSP = ("zl", "x")


def ring(x, axis):
    pairs = [(i * 2 + c, j * 2 + c) for c in range(2) for p in PAIRS[c] for i, j in (p, p[::-1])]
    return lax.ppermute(x, (axis, "core"), pairs)


def pair_z(x):
    pairs = []
    for z in range(8):
        for c in range(2):
            up = (z % 2 == 0) == (c == 0)
            to = (z + (1 if up else 7)) % 8
            pairs.append((((z % 2) * 4 + z // 2) * 2 + c, ((to % 2) * 4 + to // 2) * 2 + c))
    return lax.ppermute(x, ("zl", "zh", "core"), pairs)


STEPS = (lambda x: ring(x, "x"), lambda x: ring(x, "y"), pair_z)


def wide_cubes():
    return [
        [((x * 4 + z) * 4 + y) * 2 + core for x in gx for y in gy for z in gz]
        for core in range(2)
        for gx in PAIRS[1 - core]
        for gy in PAIRS[1 - core]
        for gz in PAIRS[core]
    ]


def last_pair(x):
    pairs = []
    for core in range(2):
        for i, j in PAIRS[1 - core]:
            pairs += [(i * 2 + core, j * 2 + core), (j * 2 + core, i * 2 + core)]
    return lax.ppermute(x, ("zh", "core"), pairs)


def to_other_core(x):
    return lax.ppermute(x, "core", [(0, 1), (1, 0)])


def local(latents, out_grad, wqs, wos, wqt, wot):
    u = latents[0, 0]
    wqs, wos, wqt, wot = wqs.T, wos.T, wqt.T, wot.T
    wide, thin, square = ((3 * HD, S), F32), ((HD, S), F32), ((HEADS, S, S), F32)
    full, flipped, factors = ((S, D), BF), ((D, S), F32), [((4608, S), BF)] * 2
    dense = 2 * S * D * 4 * HD
    early = [((1152, S), BF)] * 2
    late = [((2304, S), BF)] * 2
    sent, probs, pts, mine_e, theirs_e = call(
        space_forward_kernel,
        [((8, 2 * POS, D), BF), square, ((3 * HD, S), BF)] + early,
        (u, out_grad.reshape(8, POS, D), wqs, wos),
        [wide, thin, full, ((3 * HD, D), BF), ((HD, D), BF), flipped, flipped]
        + [((8, 2 * POS, D), BF), square, ((3 * HD, S), BF)]
        + early,
        flops=dense,
        limit=56,
        hbm=(0, 1, 2, 3),
        far=True,
    )
    mid, mine_e, theirs_e = call(
        time_kernel,
        [full] + factors,
        (swap(sent, DSP), wqt, wot, mine_e, theirs_e),
        [wide, thin, thin, wide, square, full, full, flipped, flipped],
        flops=2 * dense,
    )
    mid = swap(mid.reshape(8, POS, D), DSP).reshape(S, D)
    mid, theirs_e = lax.optimization_barrier((mid, theirs_e))
    theirs_e = to_other_core(theirs_e)
    mine_l, theirs_l = call(
        space_attention_grad_kernel,
        late,
        (mid, probs, pts, wos),
        [wide, thin, wide, flipped, flipped],
        flops=dense // 4,
    )
    theirs_l = to_other_core(theirs_l)
    (in_grad,) = call(in_grad_kernel, [full], (mid, u, mine_l, wqs), flops=dense)

    def product(piece, *pairs):
        return call(
            functools.partial(product_kernel, piece),
            [((2, 2, 4, 72, PIECE), BF)] * 2,
            pairs,
            [((len(SEGMENTS[piece]), 576, 2 * S), BF)],
            flops=2 * HD * 256 * 4 * PIECE,
        )

    early = (mine_e, theirs_e)
    keep, send = product(0, *early)
    keep, theirs_l = lax.optimization_barrier((keep, theirs_l))
    pairs = (*early, mine_l, theirs_l)
    halves = [(keep, send), product(1, *pairs), product(2, *pairs)]
    got = [STEPS[i](send) for i, (_, send) in enumerate(halves)]
    in_grad, got[2] = lax.optimization_barrier((in_grad, got[2]))
    for step in (1, 2):
        shape = ((2, 4, 72, PIECE), (4, 72, PIECE))[step - 1]
        halves = [
            call(halve_kernel, [(shape, F32), (shape, BF)], (h[0], g)) for h, g in zip(halves, got)
        ]
        got = [STEPS[(i + step) % 3](send) for i, (_, send) in enumerate(halves)]
    (terms,) = call(join_kernel, [((8, 324, S), BF)], ([h[0] for h in halves] + got))
    terms = swap(terms, ("x", "zh", "y", "core"), wide_cubes())
    keep, send = call(second_sum_kernel, [((162, S), F32), ((162, S), BF)], (terms,))
    (copies,) = call(copies_kernel, [((8, 162, S), BF)], (keep, last_pair(send)))
    copies = swap(copies, DSP)
    gqt, got, gqs, gos = call(
        last_kernel, [((ROWS, 3 * HD), F32), ((ROWS, HD), F32)] * 2, (copies,)
    )
    return in_grad[None, None], gqs, gos, gqt, got


def solution(mesh):
    fine = Mesh(mesh.devices.reshape(2, 4, 4, 4, 2), ("zl", "x", "zh", "y", "core"))
    dp = ("zh", "y", "core")
    act = P(dp, ("zl", "x"), None, None)
    in_specs = (act, act, P(), P(), P(), P())
    out_specs = (act, P(dp, None), P(dp, None), P(dp, None), P(dp, None))
    return jax.shard_map(local, mesh=fine, in_specs=in_specs, out_specs=out_specs, check_vma=False)
```

```python
import functools

import jax
import jax.numpy as jnp
from jax import lax
from jax.experimental import pallas as pl
from jax.experimental.pallas import tpu as pltpu
from jax.sharding import Mesh, PartitionSpec as P

D = 1152
HEADS = 8
HDIM = 72
HD = 576
S = 128
POS = 16
ROWS = 36
HALF = 18
PIECE = 384
PIECE = 384
SCALE = HDIM ** (-0.5)
EPS = 1e-06
BF = jnp.bfloat16
F32 = jnp.float32
MIB = 1024 * 1024

NN = (((1,), (0,)), ((), ()))
NT = (((1,), (1,)), ((), ()))
TN = (((0,), (0,)), ((), ()))


def dot(a, b, dims=NN):
    return lax.dot_general(a, b, dims, preferred_element_type=F32)


def norm_rows(u):
    centred = u - jnp.mean(u, axis=-1, keepdims=True)
    inverse = lax.rsqrt(jnp.mean(centred * centred, axis=-1, keepdims=True) + EPS)
    return centred * inverse, inverse


def norm_grad(c, g, normed, inverse):
    mean_g = jnp.mean(g, axis=-1, keepdims=True)
    mean_x = jnp.mean(g * normed, axis=-1, keepdims=True)
    return c + inverse * (g - mean_g - normed * mean_x)


def rounded(x):
    return x.astype(BF).astype(F32)


def call(kernel, outs, args, scratch=(), flops=0, limit=24, hbm=(), far=False):
    vmem = pl.BlockSpec(memory_space=pltpu.VMEM)
    away = pl.BlockSpec(memory_space=pltpu.HBM)
    moved = 2 * sum(x.size * x.dtype.itemsize for x in args)
    return pl.pallas_call(
        kernel,
        out_shape=[jax.ShapeDtypeStruct(s, t) for s, t in outs],
        in_specs=[away if i in hbm else vmem for i in range(len(args))],
        out_specs=[away if far else vmem] * len(outs),
        scratch_shapes=[pltpu.VMEM(s, t) for s, t in scratch]
        + ([pltpu.SemaphoreType.DMA((11,))] if hbm else []),
        compiler_params=pltpu.CompilerParams(vmem_limit_bytes=limit * MIB),
        cost_estimate=pl.CostEstimate(flops=flops, bytes_accessed=moved, transcendentals=0),
    )(*args)


def head(ref, part, h):
    r = part * HD + h * HDIM
    return ref[r : r + HDIM].astype(BF)


def probabilities(pt, h, mask):
    s = dot(head(pt, 1, h), head(pt, 0, h), TN) * SCALE
    if mask is not None:
        s = jnp.where(mask, s, -1e30)
    e = jnp.exp(s - jnp.max(s, axis=0, keepdims=True))
    return e / jnp.sum(e, axis=0, keepdims=True)


def attend(pt, at, probs, mask):
    for h in range(HEADS):
        p = probabilities(pt, h, mask)
        probs[h] = p
        at[h * HDIM : (h + 1) * HDIM] = dot(head(pt, 2, h), p.astype(BF))


def attend_grad(pt, ga, p, h, pg):
    q, k, v, g = head(pt, 0, h), head(pt, 1, h), head(pt, 2, h), head(ga, 0, h)
    gp = dot(v, g, TN)
    gs = (p * (gp - jnp.sum(p * gp, axis=0, keepdims=True)) * SCALE).astype(BF)
    r = h * HDIM
    pg[r : r + HDIM] = dot(k, gs)
    pg[HD + r : HD + r + HDIM] = dot(q, gs, NT)
    pg[2 * HD + r : 2 * HD + r + HDIM] = dot(g, p.astype(BF), NT)


def space_forward_kernel(
    u_hbm, c_hbm, wq_hbm, wo_hbm,
    out_hbm, probs_hbm, pts_hbm, mine_hbm, theirs_hbm,
    pt, at, u_ref, wq, wo, t, perm, so, probs, pts, mine, theirs, sems,
):
    pairs = [(u_hbm, u_ref)]
    for i in range(3):
        rows = pl.ds(i * HD, HD)
        pairs.append((wq_hbm.at[rows], wq.at[rows]))
    pairs += [(wo_hbm, wo), (c_hbm, so.at[:, pl.ds(POS, POS)])]
    pairs += [(so, out_hbm), (probs, probs_hbm), (pts, pts_hbm)]
    pairs += [(mine, mine_hbm), (theirs, theirs_hbm)]
    copies = [pltpu.make_async_copy(x, y, sems.at[i]) for i, (x, y) in enumerate(pairs)]
    for i in range(4):
        copies[i].start()
    copies[0].wait()
    u = u_ref[...].astype(F32)
    normed, _ = norm_rows(u)
    hidden = normed.astype(BF)
    lay_rows(mine, theirs, 0, hidden.astype(F32), t, perm)
    for i in range(3):
        copies[1 + i].wait()
        if i == 0:
            copies[4].start()
            copies[5].start()
        pt[i * HD : (i + 1) * HD] = rounded(dot(wq[i * HD : (i + 1) * HD], hidden, NT))
    pts[...] = pt[...].astype(BF)
    copies[8].start()
    attend(pt, at, probs, None)
    copies[7].start()
    a = at[...].astype(BF)
    mine[576:1152] = a
    theirs[576:1152] = a
    copies[9].start()
    copies[10].start()
    copies[4].wait()
    sums = (u + dot(a, wo[...], TN)).astype(BF)
    for i in range(8):
        so[i, 0:POS] = sums[i * POS : (i + 1) * POS]
    copies[5].wait()
    copies[6].start()
    for i in (7, 8, 9, 10, 6):
        copies[i].wait()


def time_kernel(x_ref, wq, wo, te, mid, mine, theirs, pt, at, ga, pg, probs, u_ref, c_ref, t, perm):
    for i in range(8):
        u_ref[i * POS : (i + 1) * POS] = x_ref[i, 0:POS]
        c_ref[i * POS : (i + 1) * POS] = x_ref[i, POS : 2 * POS]
    c = c_ref[...]
    normed, inverse = norm_rows(u_ref[...].astype(F32))
    pt[...] = rounded(dot(wq[...], normed.astype(BF), NT))
    ga[...] = rounded(dot(wo[...], c, NT))
    row = lax.broadcasted_iota(jnp.int32, (S, S), 0)
    col = lax.broadcasted_iota(jnp.int32, (S, S), 1)
    attend(pt, at, probs, (row % POS) == (col % POS))
    for h in range(HEADS):
        attend_grad(pt, ga, probs[h], h, pg)
    g = pg[...].astype(BF)
    grad = dot(g, wq[...], TN)
    mid[...] = norm_grad(c.astype(F32), grad, normed, inverse).astype(BF)
    lay_rows(mine, theirs, 0, rounded(normed), t, perm)
    lay_rows(mine, theirs, 576, c.astype(F32), t, perm)
    a = at[...].astype(BF)
    for out in (mine, theirs):
        out[1152:2880] = g
        out[2880:3456] = a
    theirs[3456:4608] = te[...]


def space_attention_grad_kernel(c_ref, probs, pts, wo, mine, theirs, pt, ga, pg, t, perm):
    c = c_ref[...]
    ga[...] = rounded(dot(wo[...], c, NT))
    pt[...] = pts[...].astype(F32)
    for h in range(HEADS):
        attend_grad(pt, ga, probs[h], h, pg)
    g = pg[...].astype(BF)
    lay_rows(mine, theirs, 0, c.astype(F32), t, perm)
    for out in (mine, theirs):
        out[576:2304] = g


def in_grad_kernel(c_ref, u_ref, g_ref, wq, in_grad):
    grad = dot(g_ref[576:2304], wq[...], TN)
    normed, inverse = norm_rows(u_ref[...].astype(F32))
    in_grad[...] = norm_grad(c_ref[...].astype(F32), grad, normed, inverse).astype(BF)


def spread(x, t, perm):
    t[...] = x.T
    for own in range(2):

        @pl.when(lax.axis_index("zl") == own)
        def _():
            for core in range(2):
                for y in range(4):
                    for half in range(2):
                        for z in range(4):
                            src = ROWS * (z * 8 + y * 2 + core) + HALF * (half ^ own)
                            dst = 576 * core + 144 * y + 72 * half + HALF * z
                            perm[dst : dst + HALF] = t[src : src + HALF]


def lay_rows(mine, theirs, base, x, t, perm):
    spread(x, t, perm)
    core = lax.axis_index("core")
    for out, half in ((mine, core), (theirs, 1 - core)):
        rows = perm[pl.ds(pl.multiple_of(half * 576, 576), 576)]
        out[base : base + 576] = rows.astype(BF)


def quarter(axis, h, p):
    me, core = lax.axis_index(axis), lax.axis_index("core")
    a = (me // 2 + (h * core + p * (1 - core))) % 2
    b = ((me + 1) // 2 + (h * (1 - core) + p * core)) % 2
    return 2 * a + (a + b) % 2


def bits(i):
    core = lax.axis_index("core")
    a, b = i // 2, ((i + 1) // 2) % 2
    return a * core + b * (1 - core), a * (1 - core) + b * core


PAIRS = ([[0, 1], [3, 2]], [[0, 3], [1, 2]])
BITS = [(h, p) for h in range(2) for p in range(2)]
PLACES = ([(0, 0), (1, 0), (1, 1), (0, 1)], [(0, 0), (0, 1), (1, 1), (1, 0)])


STREAMS = {"xt": (0, 0), "ct": (0, 576), "xs": (1, 0), "cs": (2, 0)}
SEGMENTS = (
    (("xt", 0, 1152, 432, 0, 384),),
    (("xt", 0, 1152, 432, 384, 48), ("ct", 0, 2880, 144, 0, 144), ("xs", 2, 576, 432, 0, 192)),
    (("xs", 2, 576, 432, 192, 240), ("cs", 1, 576, 144, 0, 144)),
)


def product_kernel(piece, *refs):
    *factors, keep, send, left = refs
    theirs = factors[1]
    pairs = [(factors[0], theirs)]
    if len(factors) > 2:
        pairs += [(factors[2], theirs.at[3456:4608]), (factors[3], factors[4])]
    for k, (stream, *_) in enumerate(SEGMENTS[piece]):
        which, first = STREAMS[stream]
        for i, (hy, py) in enumerate(BITS):
            rows = pl.ds(pl.multiple_of(quarter("y", hy, py) * 144 + first, 144), 144)
            for j, ref in enumerate(pairs[which]):
                left[k, i * 144 : (i + 1) * 144, j * S : (j + 1) * S] = ref[rows]
    for hx, px in BITS:
        q = quarter("x", hx, px)
        parts = []
        for k, (_, which, first, n, start, count) in enumerate(SEGMENTS[piece]):
            rows = pl.ds(pl.multiple_of(first + start + q * n, 16), count)
            right = jnp.concatenate([ref[rows] for ref in pairs[which]], axis=1)
            parts.append(dot(left[k], right, NT))
        both = jnp.concatenate(parts, axis=1)
        for i, (hy, py) in enumerate(BITS):
            for hz in range(2):
                r = 144 * i + 72 * hz
                one, two, three = ((hx, hy, hz), (hy, hz, hx), (hz, hx, hy))[piece]
                out = send if one else keep
                out[two, three, px * 2 + py] = both[r : r + 72].astype(out.dtype)


def halve_kernel(k_ref, g_ref, keep, send):
    for i, out in enumerate((keep, send)):
        out[...] = (k_ref[i].astype(F32) + g_ref[i].astype(F32)).astype(out.dtype)


def join_kernel(*refs):
    keep, got, out = refs[:3], refs[3:6], refs[6]
    own_x, own_y = bits(lax.axis_index("x"))[1], bits(lax.axis_index("y"))[1]
    for px in range(2):
        for py in range(2):
            place = ((own_x + px) % 2) * 2 + (own_y + py) % 2
            i = px * 2 + py
            accs = [k[i].astype(F32) + g[i].astype(F32) for k, g in zip(keep, got)]
            for core in range(2):

                @pl.when(lax.axis_index("core") == core)
                def _():
                    for h in range(2):
                        tiles = []
                        for z in (PLACES[core].index((h, p)) for p in range(2)):
                            rows = slice(HALF * z, HALF * (z + 1))
                            tiles += [acc[rows, S * j : S * (j + 1)] for acc in accs for j in range(3)]
                        out[place * 2 + h] = jnp.concatenate(tiles, axis=0).astype(BF)


def second_sum_kernel(x_ref, keep, send):
    acc = x_ref[0].astype(F32)
    for j in range(1, 8):
        acc = acc + x_ref[j].astype(F32)
    first, second = acc[0:162], acc[162:324]
    own = bits(lax.axis_index("zh"))[1]
    keep[...] = jnp.where(own == 0, first, second)
    send[...] = jnp.where(own == 0, second, first).astype(BF)


def copies_kernel(k_ref, g_ref, out):
    acc = (k_ref[...] + g_ref[...].astype(F32)).astype(BF)
    for i in range(8):
        out[i] = acc


def last_kernel(x_ref, qt, ot, qs, os):
    for half in range(2):
        parts = []
        for x in range(4):
            p = x_ref[half * 4 + x].astype(F32)
            parts.append(jnp.concatenate([p[HALF * i : HALF * (i + 1)] for i in range(9)], axis=1))
        rows = pl.ds(HALF * half, HALF)
        for base, qkv, proj in ((0, qt, ot), (HD, qs, os)):
            qkv[rows] = jnp.concatenate([p[:, base : base + 432] for p in parts], axis=1)
            proj[rows] = jnp.concatenate([p[:, base + 432 : base + HD] for p in parts], axis=1)


def swap(x, axes, groups=None):
    return lax.all_to_all(
        x, axes, split_axis=0, concat_axis=0, axis_index_groups=groups, tiled=True
    )


DSP = ("zl", "x")


def ring(x, axis):
    pairs = [(i * 2 + c, j * 2 + c) for c in range(2) for p in PAIRS[c] for i, j in (p, p[::-1])]
    return lax.ppermute(x, (axis, "core"), pairs)


def pair_z(x):
    pairs = []
    for z in range(8):
        for c in range(2):
            up = (z % 2 == 0) == (c == 0)
            to = (z + (1 if up else 7)) % 8
            pairs.append((((z % 2) * 4 + z // 2) * 2 + c, ((to % 2) * 4 + to // 2) * 2 + c))
    return lax.ppermute(x, ("zl", "zh", "core"), pairs)


STEPS = (lambda x: ring(x, "x"), lambda x: ring(x, "y"), pair_z)


def wide_cubes():
    return [
        [((x * 4 + z) * 4 + y) * 2 + core for x in gx for y in gy for z in gz]
        for core in range(2)
        for gx in PAIRS[1 - core]
        for gy in PAIRS[1 - core]
        for gz in PAIRS[core]
    ]


def last_pair(x):
    pairs = []
    for core in range(2):
        for i, j in PAIRS[1 - core]:
            pairs += [(i * 2 + core, j * 2 + core), (j * 2 + core, i * 2 + core)]
    return lax.ppermute(x, ("zh", "core"), pairs)


def to_other_core(x):
    return lax.ppermute(x, "core", [(0, 1), (1, 0)])


def local(latents, out_grad, wqs, wos, wqt, wot):
    u = latents[0, 0]
    wqs, wos, wqt, wot = wqs.T, wos.T, wqt.T, wot.T
    wide, thin, square = ((3 * HD, S), F32), ((HD, S), F32), ((HEADS, S, S), F32)
    full, flipped = ((S, D), BF), ((D, S), F32)
    dense = 2 * S * D * 4 * HD
    early = [((1152, S), BF)] * 2
    late = [((2304, S), BF)] * 2
    sent, probs, pts, mine_e, theirs_e = call(
        space_forward_kernel,
        [((8, 2 * POS, D), BF), square, ((3 * HD, S), BF)] + early,
        (u, out_grad.reshape(8, POS, D), wqs, wos),
        [wide, thin, full, ((3 * HD, D), BF), ((HD, D), BF), flipped, flipped]
        + [((8, 2 * POS, D), BF), square, ((3 * HD, S), BF)]
        + early,
        flops=dense,
        limit=56,
        hbm=(0, 1, 2, 3),
        far=True,
    )
    mid, mine_t, theirs_e = call(
        time_kernel,
        [full, ((3456, S), BF), ((4608, S), BF)],
        (swap(sent, DSP), wqt, wot, theirs_e),
        [wide, thin, thin, wide, square, full, full, flipped, flipped],
        flops=2 * dense,
    )
    mid = swap(mid.reshape(8, POS, D), DSP).reshape(S, D)
    mid, theirs_e = lax.optimization_barrier((mid, theirs_e))
    theirs_e = to_other_core(theirs_e)
    mine_l, theirs_l = call(
        space_attention_grad_kernel,
        late,
        (mid, probs, pts, wos),
        [wide, thin, wide, flipped, flipped],
        flops=dense // 4,
    )
    theirs_l = to_other_core(theirs_l)
    (in_grad,) = call(in_grad_kernel, [full], (mid, u, mine_l, wqs), flops=dense)

    def product(piece, *pairs):
        return call(
            functools.partial(product_kernel, piece),
            [((2, 2, 4, 72, PIECE), BF)] * 2,
            pairs,
            [((len(SEGMENTS[piece]), 576, 2 * S), BF)],
            flops=2 * HD * 256 * 4 * PIECE,
        )

    early = (mine_t, theirs_e)
    keep, send = product(0, *early)
    keep, theirs_l = lax.optimization_barrier((keep, theirs_l))
    pairs = (*early, mine_e, mine_l, theirs_l)
    halves = [(keep, send), product(1, *pairs), product(2, *pairs)]
    got = [STEPS[i](send) for i, (_, send) in enumerate(halves)]
    in_grad, got[2] = lax.optimization_barrier((in_grad, got[2]))
    for step in (1, 2):
        shape = ((2, 4, 72, PIECE), (4, 72, PIECE))[step - 1]
        halves = [
            call(halve_kernel, [(shape, F32), (shape, BF)], (h[0], g)) for h, g in zip(halves, got)
        ]
        got = [STEPS[(i + step) % 3](send) for i, (_, send) in enumerate(halves)]
    (terms,) = call(join_kernel, [((8, 324, S), BF)], ([h[0] for h in halves] + got))
    terms = swap(terms, ("x", "zh", "y", "core"), wide_cubes())
    keep, send = call(second_sum_kernel, [((162, S), F32), ((162, S), BF)], (terms,))
    (copies,) = call(copies_kernel, [((8, 162, S), BF)], (keep, last_pair(send)))
    copies = swap(copies, DSP)
    gqt, got, gqs, gos = call(
        last_kernel, [((ROWS, 3 * HD), F32), ((ROWS, HD), F32)] * 2, (copies,)
    )
    return in_grad[None, None], gqs, gos, gqt, got


def solution(mesh):
    fine = Mesh(mesh.devices.reshape(2, 4, 4, 4, 2), ("zl", "x", "zh", "y", "core"))
    dp = ("zh", "y", "core")
    act = P(dp, ("zl", "x"), None, None)
    in_specs = (act, act, P(), P(), P(), P())
    out_specs = (act, P(dp, None), P(dp, None), P(dp, None), P(dp, None))
    return jax.shard_map(local, mesh=fine, in_specs=in_specs, out_specs=out_specs, check_vma=False)
```

```python
import functools

import jax
import jax.numpy as jnp
from jax import lax
from jax.experimental import pallas as pl
from jax.experimental.pallas import tpu as pltpu
from jax.sharding import Mesh, PartitionSpec as P

D = 1152
HEADS = 8
HDIM = 72
HD = 576
S = 128
POS = 16
ROWS = 36
HALF = 18
PIECE = 384
PIECE = 384
SCALE = HDIM ** (-0.5)
EPS = 1e-06
BF = jnp.bfloat16
F32 = jnp.float32
MIB = 1024 * 1024

NN = (((1,), (0,)), ((), ()))
NT = (((1,), (1,)), ((), ()))
TN = (((0,), (0,)), ((), ()))


def dot(a, b, dims=NN):
    return lax.dot_general(a, b, dims, preferred_element_type=F32)


def norm_rows(u):
    centred = u - jnp.mean(u, axis=-1, keepdims=True)
    inverse = lax.rsqrt(jnp.mean(centred * centred, axis=-1, keepdims=True) + EPS)
    return centred * inverse, inverse


def norm_grad(c, g, normed, inverse):
    mean_g = jnp.mean(g, axis=-1, keepdims=True)
    mean_x = jnp.mean(g * normed, axis=-1, keepdims=True)
    return c + inverse * (g - mean_g - normed * mean_x)


def rounded(x):
    return x.astype(BF).astype(F32)


def call(kernel, outs, args, scratch=(), flops=0, limit=24, hbm=(), far=False):
    vmem = pl.BlockSpec(memory_space=pltpu.VMEM)
    away = pl.BlockSpec(memory_space=pltpu.HBM)
    moved = 2 * sum(x.size * x.dtype.itemsize for x in args)
    return pl.pallas_call(
        kernel,
        out_shape=[jax.ShapeDtypeStruct(s, t) for s, t in outs],
        in_specs=[away if i in hbm else vmem for i in range(len(args))],
        out_specs=[away if far else vmem] * len(outs),
        scratch_shapes=[pltpu.VMEM(s, t) for s, t in scratch]
        + ([pltpu.SemaphoreType.DMA((11,))] if hbm else []),
        compiler_params=pltpu.CompilerParams(vmem_limit_bytes=limit * MIB),
        cost_estimate=pl.CostEstimate(flops=flops, bytes_accessed=moved, transcendentals=0),
    )(*args)


def head(ref, part, h):
    r = part * HD + h * HDIM
    return ref[r : r + HDIM].astype(BF)


def probabilities(pt, h, mask):
    s = dot(head(pt, 1, h), head(pt, 0, h), TN) * SCALE
    if mask is not None:
        s = jnp.where(mask, s, -1e30)
    e = jnp.exp(s - jnp.max(s, axis=0, keepdims=True))
    return e / jnp.sum(e, axis=0, keepdims=True)


def attend(pt, at, probs, mask):
    for h in range(HEADS):
        p = probabilities(pt, h, mask)
        probs[h] = p
        at[h * HDIM : (h + 1) * HDIM] = dot(head(pt, 2, h), p.astype(BF))


def attend_grad(pt, ga, p, h, pg):
    q, k, v, g = head(pt, 0, h), head(pt, 1, h), head(pt, 2, h), head(ga, 0, h)
    gp = dot(v, g, TN)
    gs = (p * (gp - jnp.sum(p * gp, axis=0, keepdims=True)) * SCALE).astype(BF)
    r = h * HDIM
    pg[r : r + HDIM] = dot(k, gs)
    pg[HD + r : HD + r + HDIM] = dot(q, gs, NT)
    pg[2 * HD + r : 2 * HD + r + HDIM] = dot(g, p.astype(BF), NT)


def space_forward_kernel(
    u_hbm, c_hbm, wq_hbm, wo_hbm,
    out_hbm, probs_hbm, pts_hbm, mine_hbm, theirs_hbm,
    pt, at, u_ref, wq, wo, t, perm, so, probs, pts, mine, theirs, sems,
):
    pairs = [(u_hbm, u_ref)]
    for i in range(3):
        rows = pl.ds(i * HD, HD)
        pairs.append((wq_hbm.at[rows], wq.at[rows]))
    pairs += [(wo_hbm, wo), (c_hbm, so.at[:, pl.ds(POS, POS)])]
    pairs += [(so, out_hbm), (probs, probs_hbm), (pts, pts_hbm)]
    pairs += [(mine, mine_hbm), (theirs, theirs_hbm)]
    copies = [pltpu.make_async_copy(x, y, sems.at[i]) for i, (x, y) in enumerate(pairs)]
    for i in range(4):
        copies[i].start()
    copies[0].wait()
    u = u_ref[...].astype(F32)
    normed, _ = norm_rows(u)
    hidden = normed.astype(BF)
    lay_rows(mine, theirs, 0, hidden.astype(F32), t, perm)
    for i in range(3):
        copies[1 + i].wait()
        if i == 0:
            copies[4].start()
            copies[5].start()
        pt[i * HD : (i + 1) * HD] = rounded(dot(wq[i * HD : (i + 1) * HD], hidden, NT))
    pts[...] = pt[...].astype(BF)
    copies[8].start()
    attend(pt, at, probs, None)
    copies[7].start()
    a = at[...].astype(BF)
    mine[576:1152] = a
    theirs[576:1152] = a
    copies[9].start()
    copies[10].start()
    copies[4].wait()
    sums = (u + dot(a, wo[...], TN)).astype(BF)
    for i in range(8):
        so[i, 0:POS] = sums[i * POS : (i + 1) * POS]
    copies[5].wait()
    copies[6].start()
    for i in (7, 8, 9, 10, 6):
        copies[i].wait()


def time_kernel(x_ref, wq, wo, me, te, mid, mine, theirs, pt, at, ga, pg, probs, u_ref, c_ref, t, perm):
    for i in range(8):
        u_ref[i * POS : (i + 1) * POS] = x_ref[i, 0:POS]
        c_ref[i * POS : (i + 1) * POS] = x_ref[i, POS : 2 * POS]
    c = c_ref[...]
    normed, inverse = norm_rows(u_ref[...].astype(F32))
    pt[...] = rounded(dot(wq[...], normed.astype(BF), NT))
    ga[...] = rounded(dot(wo[...], c, NT))
    row = lax.broadcasted_iota(jnp.int32, (S, S), 0)
    col = lax.broadcasted_iota(jnp.int32, (S, S), 1)
    attend(pt, at, probs, (row % POS) == (col % POS))
    for h in range(HEADS):
        attend_grad(pt, ga, probs[h], h, pg)
    g = pg[...].astype(BF)
    grad = dot(g, wq[...], TN)
    mid[...] = norm_grad(c.astype(F32), grad, normed, inverse).astype(BF)
    lay_rows(mine, theirs, 0, rounded(normed), t, perm)
    lay_rows(mine, theirs, 576, c.astype(F32), t, perm)
    a = at[...].astype(BF)
    for out in (mine, theirs):
        out[1152:2880] = g
        out[2880:3456] = a
    mine[3456:4608] = me[...]
    theirs[3456:4608] = te[...]


def space_attention_grad_kernel(c_ref, probs, pts, wo, mine, theirs, pt, ga, pg, t, perm):
    c = c_ref[...]
    ga[...] = rounded(dot(wo[...], c, NT))
    pt[...] = pts[...].astype(F32)
    for h in range(HEADS):
        attend_grad(pt, ga, probs[h], h, pg)
    g = pg[...].astype(BF)
    lay_rows(mine, theirs, 0, c.astype(F32), t, perm)
    for out in (mine, theirs):
        out[576:2304] = g


def in_grad_kernel(c_ref, u_ref, g_ref, wq, in_grad):
    grad = dot(g_ref[576:2304], wq[...], TN)
    normed, inverse = norm_rows(u_ref[...].astype(F32))
    in_grad[...] = norm_grad(c_ref[...].astype(F32), grad, normed, inverse).astype(BF)


def spread(x, t, perm):
    t[...] = x.T
    for own in range(2):

        @pl.when(lax.axis_index("zl") == own)
        def _():
            for core in range(2):
                for y in range(4):
                    for half in range(2):
                        for z in range(4):
                            src = ROWS * (z * 8 + y * 2 + core) + HALF * (half ^ own)
                            dst = 576 * core + 144 * y + 72 * half + HALF * z
                            perm[dst : dst + HALF] = t[src : src + HALF]


def lay_rows(mine, theirs, base, x, t, perm):
    spread(x, t, perm)
    core = lax.axis_index("core")
    for out, half in ((mine, core), (theirs, 1 - core)):
        rows = perm[pl.ds(pl.multiple_of(half * 576, 576), 576)]
        out[base : base + 576] = rows.astype(BF)


def quarter(axis, h, p):
    me, core = lax.axis_index(axis), lax.axis_index("core")
    a = (me // 2 + (h * core + p * (1 - core))) % 2
    b = ((me + 1) // 2 + (h * (1 - core) + p * core)) % 2
    return 2 * a + (a + b) % 2


def bits(i):
    core = lax.axis_index("core")
    a, b = i // 2, ((i + 1) // 2) % 2
    return a * core + b * (1 - core), a * (1 - core) + b * core


PAIRS = ([[0, 1], [3, 2]], [[0, 3], [1, 2]])
BITS = [(h, p) for h in range(2) for p in range(2)]
PLACES = ([(0, 0), (1, 0), (1, 1), (0, 1)], [(0, 0), (0, 1), (1, 1), (1, 0)])


STREAMS = {"xt": (0, 0), "ct": (0, 576), "xs": (0, 3456), "cs": (1, 0)}
SEGMENTS = (
    (("xt", 0, 1152, 432, 0, 384),),
    (("xt", 0, 1152, 432, 384, 48), ("ct", 0, 2880, 144, 0, 144), ("xs", 1, 576, 432, 0, 192)),
    (("xs", 1, 576, 432, 192, 240), ("cs", 0, 4032, 144, 0, 144)),
)


def product_kernel(piece, *refs):
    *factors, keep, send, left = refs
    pairs = [factors[i : i + 2] for i in range(0, len(factors), 2)]
    for k, (stream, *_) in enumerate(SEGMENTS[piece]):
        which, first = STREAMS[stream]
        for i, (hy, py) in enumerate(BITS):
            rows = pl.ds(pl.multiple_of(quarter("y", hy, py) * 144 + first, 144), 144)
            for j, ref in enumerate(pairs[which]):
                left[k, i * 144 : (i + 1) * 144, j * S : (j + 1) * S] = ref[rows]
    for hx, px in BITS:
        q = quarter("x", hx, px)
        parts = []
        for k, (_, which, first, n, start, count) in enumerate(SEGMENTS[piece]):
            rows = pl.ds(pl.multiple_of(first + start + q * n, 16), count)
            right = jnp.concatenate([ref[rows] for ref in pairs[which]], axis=1)
            parts.append(dot(left[k], right, NT))
        both = jnp.concatenate(parts, axis=1)
        for i, (hy, py) in enumerate(BITS):
            for hz in range(2):
                r = 144 * i + 72 * hz
                one, two, three = ((hy, hz, hx), (hz, hx, hy), (hx, hy, hz))[piece]
                out = send if one else keep
                out[two, three, px * 2 + py] = both[r : r + 72].astype(out.dtype)


def halve_kernel(k_ref, g_ref, keep, send):
    for i, out in enumerate((keep, send)):
        out[...] = (k_ref[i].astype(F32) + g_ref[i].astype(F32)).astype(out.dtype)


def join_kernel(*refs):
    keep, got, out = refs[:3], refs[3:6], refs[6]
    own_x, own_y = bits(lax.axis_index("x"))[1], bits(lax.axis_index("y"))[1]
    for px in range(2):
        for py in range(2):
            place = ((own_x + px) % 2) * 2 + (own_y + py) % 2
            i = px * 2 + py
            accs = [k[i].astype(F32) + g[i].astype(F32) for k, g in zip(keep, got)]
            for core in range(2):

                @pl.when(lax.axis_index("core") == core)
                def _():
                    for h in range(2):
                        tiles = []
                        for z in (PLACES[core].index((h, p)) for p in range(2)):
                            rows = slice(HALF * z, HALF * (z + 1))
                            tiles += [acc[rows, S * j : S * (j + 1)] for acc in accs for j in range(3)]
                        out[place * 2 + h] = jnp.concatenate(tiles, axis=0).astype(BF)


def second_sum_kernel(x_ref, keep, send):
    acc = x_ref[0].astype(F32)
    for j in range(1, 8):
        acc = acc + x_ref[j].astype(F32)
    first, second = acc[0:162], acc[162:324]
    own = bits(lax.axis_index("zh"))[1]
    keep[...] = jnp.where(own == 0, first, second)
    send[...] = jnp.where(own == 0, second, first).astype(BF)


def copies_kernel(k_ref, g_ref, out):
    acc = (k_ref[...] + g_ref[...].astype(F32)).astype(BF)
    for i in range(8):
        out[i] = acc


def last_kernel(x_ref, qt, ot, qs, os):
    for half in range(2):
        parts = []
        for x in range(4):
            p = x_ref[half * 4 + x].astype(F32)
            parts.append(jnp.concatenate([p[HALF * i : HALF * (i + 1)] for i in range(9)], axis=1))
        rows = pl.ds(HALF * half, HALF)
        for base, qkv, proj in ((0, qt, ot), (HD, qs, os)):
            qkv[rows] = jnp.concatenate([p[:, base : base + 432] for p in parts], axis=1)
            proj[rows] = jnp.concatenate([p[:, base + 432 : base + HD] for p in parts], axis=1)


def swap(x, axes, groups=None):
    return lax.all_to_all(
        x, axes, split_axis=0, concat_axis=0, axis_index_groups=groups, tiled=True
    )


DSP = ("zl", "x")


def ring(x, axis):
    pairs = [(i * 2 + c, j * 2 + c) for c in range(2) for p in PAIRS[c] for i, j in (p, p[::-1])]
    return lax.ppermute(x, (axis, "core"), pairs)


def pair_z(x):
    pairs = []
    for z in range(8):
        for c in range(2):
            up = (z % 2 == 0) == (c == 0)
            to = (z + (1 if up else 7)) % 8
            pairs.append((((z % 2) * 4 + z // 2) * 2 + c, ((to % 2) * 4 + to // 2) * 2 + c))
    return lax.ppermute(x, ("zl", "zh", "core"), pairs)


STEPS = (lambda x: ring(x, "y"), pair_z, lambda x: ring(x, "x"))


def wide_cubes():
    return [
        [((x * 4 + z) * 4 + y) * 2 + core for x in gx for y in gy for z in gz]
        for core in range(2)
        for gx in PAIRS[1 - core]
        for gy in PAIRS[1 - core]
        for gz in PAIRS[core]
    ]


def last_pair(x):
    pairs = []
    for core in range(2):
        for i, j in PAIRS[1 - core]:
            pairs += [(i * 2 + core, j * 2 + core), (j * 2 + core, i * 2 + core)]
    return lax.ppermute(x, ("zh", "core"), pairs)


def to_other_core(x):
    return lax.ppermute(x, "core", [(0, 1), (1, 0)])


def local(latents, out_grad, wqs, wos, wqt, wot):
    u = latents[0, 0]
    wqs, wos, wqt, wot = wqs.T, wos.T, wqt.T, wot.T
    wide, thin, square = ((3 * HD, S), F32), ((HD, S), F32), ((HEADS, S, S), F32)
    full, flipped, factors = ((S, D), BF), ((D, S), F32), [((4608, S), BF)] * 2
    dense = 2 * S * D * 4 * HD
    early = [((1152, S), BF)] * 2
    late = [((2304, S), BF)] * 2
    sent, probs, pts, mine_e, theirs_e = call(
        space_forward_kernel,
        [((8, 2 * POS, D), BF), square, ((3 * HD, S), BF)] + early,
        (u, out_grad.reshape(8, POS, D), wqs, wos),
        [wide, thin, full, ((3 * HD, D), BF), ((HD, D), BF), flipped, flipped]
        + [((8, 2 * POS, D), BF), square, ((3 * HD, S), BF)]
        + early,
        flops=dense,
        limit=56,
        hbm=(0, 1, 2, 3),
        far=True,
    )
    mid, mine_e, theirs_e = call(
        time_kernel,
        [full] + factors,
        (swap(sent, DSP), wqt, wot, mine_e, theirs_e),
        [wide, thin, thin, wide, square, full, full, flipped, flipped],
        flops=2 * dense,
    )
    mid = swap(mid.reshape(8, POS, D), DSP).reshape(S, D)
    mid, theirs_e = lax.optimization_barrier((mid, theirs_e))
    theirs_e = to_other_core(theirs_e)
    mine_l, theirs_l = call(
        space_attention_grad_kernel,
        late,
        (mid, probs, pts, wos),
        [wide, thin, wide, flipped, flipped],
        flops=dense // 4,
    )
    theirs_l = to_other_core(theirs_l)
    (in_grad,) = call(in_grad_kernel, [full], (mid, u, mine_l, wqs), flops=dense)

    def product(piece, *pairs):
        return call(
            functools.partial(product_kernel, piece),
            [((2, 2, 4, 72, PIECE), BF)] * 2,
            pairs,
            [((len(SEGMENTS[piece]), 576, 2 * S), BF)],
            flops=2 * HD * 256 * 4 * PIECE,
        )

    early = (mine_e, theirs_e)
    keep, send = product(0, *early)
    keep, theirs_l = lax.optimization_barrier((keep, theirs_l))
    pairs = (*early, mine_l, theirs_l)
    halves = [(keep, send), product(1, *pairs), product(2, *pairs)]
    got = [STEPS[i](send) for i, (_, send) in enumerate(halves)]
    in_grad, got[2] = lax.optimization_barrier((in_grad, got[2]))
    for step in (1, 2):
        shape = ((2, 4, 72, PIECE), (4, 72, PIECE))[step - 1]
        halves = [
            call(halve_kernel, [(shape, F32), (shape, BF)], (h[0], g)) for h, g in zip(halves, got)
        ]
        got = [STEPS[(i + step) % 3](send) for i, (_, send) in enumerate(halves)]
    (terms,) = call(join_kernel, [((8, 324, S), BF)], ([h[0] for h in halves] + got))
    terms = swap(terms, ("x", "zh", "y", "core"), wide_cubes())
    keep, send = call(second_sum_kernel, [((162, S), F32), ((162, S), BF)], (terms,))
    (copies,) = call(copies_kernel, [((8, 162, S), BF)], (keep, last_pair(send)))
    copies = swap(copies, DSP)
    gqt, got, gqs, gos = call(
        last_kernel, [((ROWS, 3 * HD), F32), ((ROWS, HD), F32)] * 2, (copies,)
    )
    return in_grad[None, None], gqs, gos, gqt, got


def solution(mesh):
    fine = Mesh(mesh.devices.reshape(2, 4, 4, 4, 2), ("zl", "x", "zh", "y", "core"))
    dp = ("zh", "y", "core")
    act = P(dp, ("zl", "x"), None, None)
    in_specs = (act, act, P(), P(), P(), P())
    out_specs = (act, P(dp, None), P(dp, None), P(dp, None), P(dp, None))
    return jax.shard_map(local, mesh=fine, in_specs=in_specs, out_specs=out_specs, check_vma=False)
```
